128 devices in a mesh: lon: 16 (over x_lo, y, core), lat: 8 (over z, x_hi).
Axes of the slice: x: 4 (x_hi: 2, x_lo: 2; x = x_hi * 2 + x_lo), y: 4, z: 4, core: 2. Of those that a mesh axis runs over, the one named last changes fastest.
Arguments:
- field: bfloat16 [192, 48, 8, 192], P('lon', 'lat'), may hold values from -6 to 6
- w_qkv: bfloat16 [192, 576], replicated, may hold values from -0.4375 to 0.4375
- w_proj: bfloat16 [192, 192], replicated, may hold values from -0.4375 to 0.4375
- w_fc1: bfloat16 [192, 768], replicated, may hold values from -0.4375 to 0.4375
- w_fc2: bfloat16 [768, 192], replicated, may hold values from -0.21875 to 0.21875
- bias_table: float32 [8, 4, 6, 3312], P('lat'), may hold values from -4 to 342
- cotangent: bfloat16 [192, 48, 8, 192], P('lon', 'lat'), may hold values from -6 to 6
Outputs:
- out_field: bfloat16 [192, 48, 8, 192], P('lon', 'lat')
- grad_field: bfloat16 [192, 48, 8, 192], P('lon', 'lat')
- grad_qkv: float32 [192, 576], replicated
- grad_proj: float32 [192, 192], replicated
- grad_fc1: float32 [192, 768], replicated
- grad_fc2: float32 [768, 192], replicated
- grad_bias: float32 [8, 4, 6, 3312], P('lat')
The draws below stay inside these ranges and needn't reach their ends.
All inputs are finite; a program needn't handle non-finite values.
Results may differ from the reference program's by a relative error of at most 0.029.
Values may be sent and summed in bfloat16 or wider, within the bound.
A program may use at most 192 MiB of HBM per device.

```python
import jax
import jax.numpy as jnp
from jax import lax

C = 192
HEADS = 6
FFN_UNITS = 768
LEV = 8
WLON = 12
WLAT = 6
WLEV = 2
NLON = 192
NLAT = 48
LATWIN = 8
POS = 3312


def draw_bias_table(key, part):
    key = jax.random.fold_in(key, 7)
    shape = (LATWIN, LEV // WLEV, HEADS, WLEV * WLEV * WLAT * WLAT, 2 * WLON - 1)
    base_key = jax.random.fold_in(key, 0)
    base = jax.random.truncated_normal(base_key, -4.0, 4.0, shape, jnp.float32)
    return base.reshape(LATWIN, LEV // WLEV, HEADS, POS)


def shard_levels(own_key, shape, cuts, low, top_value):
    factor_of, own = 1.0, jax.random.fold_in(own_key, 6)
    for axis_at, shards_of in cuts:
        draws = jnp.exp(jax.random.uniform(jax.random.fold_in(own, axis_at), (shards_of,), jnp.float32, low / len(cuts), top_value / len(cuts)))
        factor_of = factor_of * jnp.repeat(draws, shape[axis_at] // shards_of).reshape([-1 if axis == axis_at else 1 for axis in range(len(shape))])
    return factor_of


def normal_values(rng, dims, width, most, pieces=(), kind=jnp.bfloat16):
    level = shard_levels(rng, dims, pieces, -0.22, 0.18) if pieces else 1.0
    values = jax.random.normal(rng, dims, jnp.float32) * width * level
    return jnp.minimum(jnp.maximum(values, -most), most).astype(kind)


def setup_inputs(seed: int = 0) -> dict:
    splits = jax.random.split(jax.random.key(seed), 8)
    field = normal_values(splits[0], (NLON, NLAT, LEV, C), 1.0, 6.0, ((0, 16), (1, 8)))
    w_qkv = normal_values(splits[1], (C, 3 * C), C ** -0.5, 0.4375)
    w_proj = normal_values(splits[2], (C, C), C ** -0.5, 0.4375)
    w_fc1 = normal_values(splits[3], (C, FFN_UNITS), C ** -0.5, 0.4375)
    w_fc2 = normal_values(splits[4], (FFN_UNITS, C), FFN_UNITS ** -0.5, 0.21875)
    bias_table = draw_bias_table(jax.random.fold_in(splits[7], 71), 0)
    cotangent = normal_values(splits[6], (NLON, NLAT, LEV, C), 1.0, 6.0, ((0, 16), (1, 8)))
    return {"field": field, "w_qkv": w_qkv, "w_proj": w_proj, "w_fc1": w_fc1, "w_fc2": w_fc2, "bias_table": bias_table, "cotangent": cotangent}


EPSILON = 1e-05
MASKED = -1000000000.0

def layer_norm(tiles):
    widened = tiles.astype(jnp.float32)
    centered = widened - lax.optimization_barrier(jnp.mean(widened, axis=-1, keepdims=True))
    spread = lax.optimization_barrier(jnp.mean(centered * centered, axis=-1, keepdims=True))
    return (centered * lax.rsqrt(spread + EPSILON)).astype(jnp.bfloat16)

def to_windows(tiles):
    lon_len, lat_len, levels, features = tiles.shape
    shaped = tiles.reshape(lon_len // WLON, WLON, lat_len // WLAT, WLAT, levels // WLEV, WLEV, features)
    shaped = shaped.transpose(2, 4, 0, 5, 3, 1, 6)
    return shaped.reshape(lat_len // WLAT, levels // WLEV, lon_len // WLON, WLEV * WLAT * WLON, features)

def from_windows(blocks, lon_len, lat_len):
    lat_win, lev_win, lon_win, window_len, features = blocks.shape
    shaped = blocks.reshape(lat_win, lev_win, lon_win, WLEV, WLAT, WLON, features)
    shaped = shaped.transpose(2, 5, 0, 4, 1, 3, 6)
    return shaped.reshape(lon_len, lat_len, lev_win * WLEV, features)

def expand_bias(table):
    lat_win, lev_win, head_count, positions = table.shape
    shaped = table.reshape(lat_win, lev_win, head_count, WLEV, WLEV, WLAT, WLAT, 2 * WLON - 1)
    stacked = jnp.stack([shaped[..., offset:offset + WLON][..., ::-1] for offset in range(WLON)], axis=-2)
    stacked = stacked.transpose(0, 1, 2, 3, 5, 7, 4, 6, 8)
    window_len = WLEV * WLAT * WLON
    return stacked.reshape(lat_win, lev_win, head_count, window_len, window_len)

def window_groups(last_lat, lev_win):
    token_ids = jnp.arange(WLEV * WLAT * WLON)
    level_place = token_ids // (WLAT * WLON)
    lat_place = token_ids // WLON % WLAT
    lat_group = jnp.where(last_lat[:, None] & (lat_place[None, :] >= WLAT // 2), 2, 0)
    lev_last = jnp.arange(lev_win) == lev_win - 1
    lev_group = jnp.where(lev_last[:, None] & (level_place[None, :] >= WLEV // 2), 1, 0)
    group = lat_group[:, None, :] + lev_group[None, :, :]
    return group[:, :, :, None] == group[:, :, None, :]

def forward_block(tokens, probes, weights, bias, allowed):
    w_qkv, w_proj, w_fc1, w_fc2 = weights
    probe_qkv, probe_scores, probe_proj, probe_fc1, probe_fc2 = probes
    lon_len, lat_len, levels, features = tokens.shape
    head_count = bias.shape[2]
    head_dim = features // head_count
    row_count = lon_len * lat_len * levels
    normed = layer_norm(tokens).reshape(row_count, features)
    qkv = (jnp.dot(normed, w_qkv, preferred_element_type=jnp.float32) + probe_qkv).astype(jnp.bfloat16)
    windows = to_windows(qkv.reshape(lon_len, lat_len, levels, 3 * features))
    lead_shape = windows.shape[:4]
    queries = windows[..., :features].reshape(lead_shape + (head_count, head_dim)).astype(jnp.float32)
    key_part = windows[..., features:2 * features].reshape(lead_shape + (head_count, head_dim)).astype(jnp.float32)
    value_part = windows[..., 2 * features:].reshape(lead_shape + (head_count, head_dim)).astype(jnp.float32)
    scores = jnp.einsum('avonhd,avomhd->avohnm', queries, key_part) * (1.0 / jnp.sqrt(jnp.float32(head_dim)))
    scores = scores + bias[:, :, None] + probe_scores
    scores = jnp.where(allowed[:, :, None, None], scores, MASKED)
    highest = lax.optimization_barrier(jnp.max(scores, axis=-1, keepdims=True))
    exponent = jnp.exp(scores - highest)
    soft_weights = (exponent / lax.optimization_barrier(jnp.sum(exponent, axis=-1, keepdims=True))).astype(jnp.bfloat16)
    blended = jnp.einsum('avohnm,avomhd->avonhd', soft_weights.astype(jnp.float32), value_part).astype(jnp.bfloat16)
    blended = from_windows(blended.reshape(lead_shape + (features,)), lon_len, lat_len).reshape(row_count, features)
    projected = jnp.dot(blended, w_proj, preferred_element_type=jnp.float32) + probe_proj
    middle = (tokens.reshape(row_count, features).astype(jnp.float32) + projected).astype(jnp.bfloat16)
    normed_two = layer_norm(middle)
    first_product = jnp.dot(normed_two, w_fc1, preferred_element_type=jnp.float32) + probe_fc1
    hidden = jax.nn.gelu(first_product, approximate=False).astype(jnp.bfloat16)
    second_product = jnp.dot(hidden, w_fc2, preferred_element_type=jnp.float32) + probe_fc2
    result = (middle.astype(jnp.float32) + second_product).astype(jnp.bfloat16)
    return (result.reshape(tokens.shape), (normed, blended, normed_two, hidden))

def contract(left_rows, right_rows):
    return jnp.einsum('tc,tk->ck', left_rows.astype(jnp.float32), right_rows.astype(jnp.bfloat16).astype(jnp.float32))

def local_pass(tokens, upstream, weights, bias_table, last_lat, first_col):
    lon_len, lat_len, levels, features = tokens.shape
    row_count = lon_len * lat_len * levels
    bias, expand_back = jax.vjp(expand_bias, bias_table)
    lat_win, lev_win, head_count, window_len = bias.shape[:4]
    allowed = window_groups(last_lat, lev_win)
    hidden_units = weights[2].shape[1]
    probes = (jnp.zeros((row_count, 3 * features), jnp.float32), jnp.zeros((lat_win, lev_win, lon_len // WLON, head_count, window_len, window_len), jnp.float32), jnp.zeros((row_count, features), jnp.float32), jnp.zeros((row_count, hidden_units), jnp.float32), jnp.zeros((row_count, features), jnp.float32))

    def apply(lattice, extra):
        return forward_block(lattice, extra, weights, bias, allowed)
    result, pullback, saved = jax.vjp(apply, tokens, probes, has_aux=True)
    grad_tokens, grad_probes = pullback(upstream)
    normed, blended, normed_two, hidden = saved
    start = first_col * lat_len * levels
    grads = (contract(normed[start:], grad_probes[0][start:]), contract(blended[start:], grad_probes[2][start:]), contract(normed_two[start:], grad_probes[3][start:]), contract(hidden[start:], grad_probes[4][start:]))
    score_grad = lax.optimization_barrier(jnp.sum(grad_probes[1][:, :, first_col // WLON:], axis=2))
    grad_bias, = expand_back(score_grad)
    return (result, grad_tokens, grads, grad_bias)

def reference(field, w_qkv, w_proj, w_fc1, w_fc2, bias_table, cotangent):
    shifts = (WLON // 2, WLAT // 2, WLEV // 2)
    rolled_field = jnp.roll(field, (-shifts[0], -shifts[1], -shifts[2]), axis=(0, 1, 2))
    rolled_cot = jnp.roll(cotangent, (-shifts[0], -shifts[1], -shifts[2]), axis=(0, 1, 2))
    features = field.shape[-1]

    def to_bands(tiles):
        return tiles.reshape(NLON, LATWIN, WLAT, LEV, features).transpose(1, 0, 2, 3, 4)

    def from_bands(bands):
        return bands.transpose(1, 0, 2, 3, 4).reshape(NLON, NLAT, LEV, features)
    band_last = jnp.arange(LATWIN) == LATWIN - 1
    weights = (w_qkv, w_proj, w_fc1, w_fc2)

    def one_band(inputs):
        band_field, band_cot, band_table, is_last = inputs
        return local_pass(band_field, band_cot, weights, band_table[None], is_last.reshape(1), 0)
    result, grad_tokens, grads, grad_bias = lax.map(one_band, (to_bands(rolled_field), to_bands(rolled_cot), bias_table, band_last))
    out_field = jnp.roll(from_bands(result), shifts, axis=(0, 1, 2))
    grad_field = jnp.roll(from_bands(grad_tokens), shifts, axis=(0, 1, 2))
    return (out_field, grad_field, lax.optimization_barrier(jnp.sum(grads[0], axis=0)), lax.optimization_barrier(jnp.sum(grads[1], axis=0)), lax.optimization_barrier(jnp.sum(grads[2], axis=0)), lax.optimization_barrier(jnp.sum(grads[3], axis=0)), grad_bias[:, 0])
```

```python
import functools
import math

import jax
import jax.numpy as jnp
import numpy as np
from jax import lax
from jax.experimental import pallas as pl
from jax.experimental.pallas import tpu as pltpu
from jax.sharding import PartitionSpec as P

C = 192
HEADS = 6
HIDDEN = 768
LEV = 8
WLON = 12
WLAT = 6
WLEV = 2
LWIN = LEV // WLEV
WH = LWIN * HEADS
WIN = WLEV * WLAT * WLON
TOK = LWIN * WIN
QUAD = TOK // 4
SITE = WLEV * WLAT
SHIFTS = 2 * WLON - 1
STRIP = SHIFTS * SITE
POS = WLEV * WLEV * WLAT * WLAT * SHIFTS
RUN = WLAT * SHIFTS
LANES = 384
STACK = HEADS * WIN
EPSILON = 1e-05
MASKED = -1000000000.0
LOG2E = math.log2(math.e)
SCALE = 1.0 / math.sqrt(C // HEADS)
RING = 4
E_TILES = 72
L_TILES = 36
B_TILES = 27
B_ROOM = 32
PACKED = 224
TILE = (16, 128)
BF16 = jnp.bfloat16
F32 = jnp.float32
MESH = pl.DeviceIdType.MESH
VMEM_LIMIT = 30 * 1024 * 1024


def token_places():
    w, o, lev, a = np.meshgrid(
        np.arange(LWIN), np.arange(WLON), np.arange(WLEV), np.arange(WLAT), indexing="ij"
    )
    quarter = (o // 6) * 2 + a // 3
    level = (2 * w + lev + 1) % LEV
    return (quarter * QUAD + ((o % 6) * 3 + a % 3) * LEV + level).reshape(TOK).astype(np.int32)


def lane_places():
    lev, a, d = np.meshgrid(np.arange(WLEV), np.arange(WLAT), np.arange(SHIFTS), indexing="ij")
    return ((SHIFTS - 1 - d) * SITE + lev * WLAT + a).reshape(STRIP).astype(np.int32)


def row_places():
    wh, _, site = np.meshgrid(np.arange(WH), np.arange(2), np.arange(SITE), indexing="ij")
    return (site * WH + wh).reshape(WH * 2 * SITE).astype(np.int32)


def row_codes():
    _, w, p, lev, a = np.meshgrid(
        np.arange(HEADS), np.arange(LWIN), np.arange(2), np.arange(WLEV), np.arange(WLAT), indexing="ij"
    )
    code = lev + 2 * (a >= WLAT // 2) + 4 * (w == LWIN - 1) + 8 * (p == 0)
    return code.reshape(WH * 2 * SITE).astype(np.int32)


def lane_codes():
    site = np.arange(LANES) % SITE
    return (site // WLAT + 2 * (site % WLAT >= WLAT // 2)).astype(np.int32)


def columns_of(*arrays):
    made = np.zeros((TOK, 8), np.int32)
    for i, array in enumerate(arrays):
        made[: len(array), i] = array
    return made


def dot(a, b):
    return jnp.dot(a, b, preferred_element_type=F32)


def dot_nt(a, b):
    return lax.dot_general(a, b, (((1,), (1,)), ((), ())), preferred_element_type=F32)


def dot_tn(a, b):
    return lax.dot_general(a, b, (((0,), (0,)), ((), ())), preferred_element_type=F32)


def one_hot(places, rows, cols):
    along = 1 if places.shape[1] == 1 else 0
    index = lax.broadcasted_iota(jnp.int32, (rows, cols), along)
    return jnp.where(index == places, 1.0, 0.0).astype(BF16)


def pieces(value, count):
    found = []
    for _ in range(count):
        part = value.astype(BF16)
        found.append(part)
        value = value - part.astype(F32)
    return found


def quarter(ref, index):
    part = ref[pl.ds((index // 2) * 6, 6), pl.ds((index % 2) * 3, 3)]
    return part.astype(F32).reshape(QUAD, C)


def pack(value):
    half = QUAD // 2
    rest = jnp.concatenate([value[:half, 128:], value[half:, 128:]], axis=1)
    blank = jnp.zeros((PACKED - QUAD - half, 128), F32)
    return jnp.concatenate([value[:, :128], rest, blank], axis=0).astype(BF16)


def unpack(value):
    half = QUAD // 2
    wide = value.astype(F32)
    rest = wide[QUAD : QUAD + half]
    right = jnp.concatenate([rest[:, :64], rest[:, 64:]], axis=0)
    return jnp.concatenate([wide[:QUAD], right], axis=1)


def place_of(lon, lat):
    x = lax.rem(lat, 2) * 2 + lax.div(lon, 8)
    return (x, lax.rem(lax.div(lon, 2), RING), lax.div(lat, 2)), lax.rem(lon, 2)


def device_at(chip, core):
    x, y, z = chip
    return ((lax.rem(x, 2) * RING + y) * 2 + core, z * 2 + lax.div(x, 2))


def moved(chip, axis, step):
    return tuple(lax.rem(c + step, RING) if i == axis else c for i, c in enumerate(chip))


def remote(src, dst, send, recv, device):
    return pltpu.make_async_remote_copy(
        src_ref=src, dst_ref=dst, send_sem=send, recv_sem=recv, device_id=device, device_id_type=MESH
    )


class Here:
    def __init__(self, n_lon, n_lat):
        self.lon, self.lat = lax.axis_index("lon"), lax.axis_index("lat")
        self.chip, self.core = place_of(self.lon, self.lat)
        self.sibling = (self.lon + 1 - 2 * self.core, self.lat)
        self.slot = [[lax.rem(c + k, RING) for k in range(RING)] for c in self.chip]
        self.along = [
            [device_at(moved(self.chip, axis, k), self.core) for k in range(RING)] for axis in range(3)
        ]
        self.eighth = lax.div(self.lon, 2)
        self.eighths = [lax.rem(self.eighth + k, 8) for k in range(8)]
        self.rows = [(chip * 2 + self.core, self.lat) for chip in self.eighths]
        self.across = {}
        for step in (-1, 1):
            to_lon = lax.rem(self.lon + n_lon + step, n_lon)
            to_lat = lax.rem(self.lat + n_lat + step, n_lat)
            self.across[step] = ((to_lon, to_lat), (to_lon, self.lat), (self.lon, to_lat))

    def greet(self):
        others = [*self.across[-1], *self.across[1], *self.rows[1:], self.sibling]
        for axis in range(3):
            others += self.along[axis][1:]
        barrier = pltpu.get_barrier_semaphore()
        for device in others:
            pl.semaphore_signal(barrier, inc=1, device_id=device, device_id_type=MESH)
        return lambda: pl.semaphore_wait(barrier, len(others))


def halo(here, source, target, send, recv, step):
    copies = []
    for index in range(3):
        src = index if step < 0 else 3 - index
        device = here.across[step][index]
        copies.append(remote(source.at[src], target.at[3 - src], send.at[index], recv.at[index], device))
    return copies


def begin(copies):
    for copy in copies:
        copy.start()


def end(copies):
    for copy in copies:
        copy.wait()


def wait_bytes(like, sem):
    pltpu.make_async_copy(like, like, sem).wait()


class WeightSum:
    def __init__(self, here, out, refs):
        self.here, self.out = here, out
        self.src, self.other, self.a1, self.r1, self.x2, self.x3, self.send, self.recv = refs

    @staticmethod
    def scratch(tiles):
        n1 = tiles // 12
        room = lambda *dims: pltpu.VMEM((*dims, *TILE), BF16)
        dma = pltpu.SemaphoreType.DMA
        return [
            room(2, tiles), room(tiles),
            room(3, RING, n1), room(3, RING - 1, n1), room(3, RING, n1), room(3, RING, n1),
            dma((6,)), dma((6,)),
        ]

    def put(self, half, block, first=0):
        narrow = block.astype(BF16)
        for c in range(block.shape[1] // 128):
            for r in range(C // 16):
                self.src[half, first + c * 12 + r] = narrow[
                    r * 16 : (r + 1) * 16, c * 128 : (c + 1) * 128
                ]

    def copies(self, at, axis_of, source, target):
        made = []
        for t in range(3):
            axis = (t + axis_of) % 3
            slot = self.here.slot[axis]
            for k in range(1, RING):
                made.append(
                    remote(
                        source(t, slot[k], slot[0]), target(t, k - 1, slot[0]),
                        self.send.at[at], self.recv.at[at], self.here.along[axis][k],
                    )
                )
        return made

    def phase(self, at):
        core = self.here.core
        if at == 0:
            return [remote(self.src.at[1 - core], self.other, self.send.at[0], self.recv.at[0], self.here.sibling)]
        if at == 1:
            return self.copies(1, 0, lambda t, to, me: self.a1.at[t, to], lambda t, k, me: self.r1.at[t, k])
        if at == 2:
            return self.copies(2, 1, lambda t, to, me: self.x2.at[t, me], lambda t, k, me: self.x2.at[t, me])
        if at == 3:
            return self.copies(3, 2, lambda t, to, me: self.x3.at[t, me], lambda t, k, me: self.x3.at[t, me])
        if at == 4:
            out = self.out.at[core]
            return self.copies(4, 0, lambda t, to, me: out.at[t, me], lambda t, k, me: out.at[t, me])
        return [remote(self.out.at[core], self.out.at[core], self.send.at[5], self.recv.at[5], self.here.sibling)]

    def start(self):
        begin(self.phase(0))

    def step(self, at):
        like = self.other if at in (0, 5) else self.r1
        wait_bytes(like, self.recv.at[at])
        wait_bytes(like, self.send.at[at])
        core = self.here.core
        if at == 0:
            total = self.src[core].astype(F32) + self.other[...].astype(F32)
            self.a1[...] = total.astype(BF16).reshape(self.a1.shape)
        for t in range(3):
            one, two, three = (self.here.slot[(t + i) % 3][0] for i in range(3))
            if at == 1:
                total = self.a1[t, one].astype(F32)
                for k in range(RING - 1):
                    total = total + self.r1[t, k].astype(F32)
                self.x2[t, two] = total.astype(BF16)
            if at in (2, 3):
                came = self.x2 if at == 2 else self.x3
                total = came[t, 0].astype(F32)
                for k in range(1, RING):
                    total = total + came[t, k].astype(F32)
                if at == 2:
                    self.x3[t, three] = total.astype(BF16)
                else:
                    self.out[core, t, one] = total.astype(BF16)
        if at < 5:
            begin(self.phase(at + 1))


class BiasSum:
    def __init__(self, here, out, refs):
        self.here, self.out = here, out
        self.src, self.other, self.a1, self.r1, self.send, self.recv = refs

    @staticmethod
    def scratch():
        room = lambda *dims: pltpu.VMEM((*dims, *TILE), BF16)
        dma = pltpu.SemaphoreType.DMA
        return [room(2, B_ROOM), room(B_ROOM), room(8, 4), room(7, 4), dma((4,)), dma((4,))]

    def put(self, block):
        narrow = block.astype(BF16)
        for c in range(3):
            for r in range(18):
                t = c * 18 + r
                self.src[t // B_TILES, t % B_TILES] = narrow[
                    r * 16 : (r + 1) * 16, c * 128 : (c + 1) * 128
                ]
        self.src[0, B_TILES:] = jnp.zeros((B_ROOM - B_TILES, *TILE), BF16)
        self.src[1, B_TILES:] = jnp.zeros((B_ROOM - B_TILES, *TILE), BF16)

    def phase(self, at):
        here, core = self.here, self.here.core
        sems = self.send.at[at], self.recv.at[at]
        if at == 0:
            return [remote(self.src.at[1 - core], self.other, *sems, here.sibling)]
        if at == 3:
            return [remote(self.out.at[core], self.out.at[core], *sems, here.sibling)]
        made = []
        for k in range(1, 8):
            source = self.a1.at[here.eighths[k]] if at == 1 else self.out.at[core, here.eighth]
            target = self.r1.at[k - 1] if at == 1 else self.out.at[core, here.eighth]
            made.append(remote(source, target, *sems, here.rows[k]))
        return made

    def start(self):
        begin(self.phase(0))

    def step(self, at):
        like = (self.other, self.r1, self.r1, self.other)[at]
        wait_bytes(like, self.recv.at[at])
        wait_bytes(like, self.send.at[at])
        core, chip = self.here.core, self.here.eighth
        if at == 0:
            total = self.src[core].astype(F32) + self.other[...].astype(F32)
            self.a1[...] = total.astype(BF16).reshape(8, 4, *TILE)
        if at == 1:
            total = self.a1[chip].astype(F32)
            for k in range(7):
                total = total + self.r1[k].astype(F32)
            self.out[core, chip] = total.astype(BF16)
        if at < 3:
            begin(self.phase(at + 1))


def layer_norm(x):
    centered = x - jnp.mean(x, axis=-1, keepdims=True)
    spread = jnp.mean(centered * centered, axis=-1, keepdims=True)
    rate = lax.rsqrt(spread + EPSILON)
    return centered * rate, rate


def layer_norm_back(cot, unit, rate):
    first = jnp.mean(cot, axis=-1, keepdims=True)
    second = jnp.mean(cot * unit, axis=-1, keepdims=True)
    return rate * (cot - first - unit * second)


def head_mask(head):
    lane = lax.broadcasted_iota(jnp.int32, (1, C), 1)
    return (lane >= head * 32) & (lane < head * 32 + 32)


def stacked(value):
    wide = value.astype(F32)
    parts = [jnp.where(head_mask(h), wide, 0.0).astype(BF16) for h in range(HEADS)]
    return jnp.concatenate(parts, axis=0)


def unstacked(value):
    total = jnp.where(head_mask(0), value[0:WIN], 0.0)
    for h in range(1, HEADS):
        total = total + jnp.where(head_mask(h), value[h * WIN : (h + 1) * WIN], 0.0)
    return total


def expand_bias(last_lat, table, columns, index_rows, lanes, tall_table, gathered, strips, scores):
    for head in range(HEADS):
        tall_table[head * LWIN : (head + 1) * LWIN, :] = table[head]
    for site in range(SITE):
        lev, a = site // WLAT, site % WLAT
        for other in range(WLEV):
            start = ((lev * WLEV + other) * WLAT + a) * RUN
            gathered[site * WH : (site + 1) * WH, other * RUN : (other + 1) * RUN] = tall_table[
                :, start : start + RUN
            ]
    moved = sum(dot(part, lanes[...]) for part in pieces(gathered[...], 3))
    rows = one_hot(columns[:, 1:2], WH * 2 * SITE, SITE * WH)
    moved = sum(dot(rows, part) for part in pieces(moved, 3))
    code = columns[:, 2:3]
    moved = jnp.where((code & 8) != 0, pltpu.roll(moved, LANES - SITE, 1), moved) * LOG2E
    seen = jnp.where((code & 4) != 0, 1, 0) + jnp.where(last_lat, 2, 0)
    apart = (code ^ index_rows[2:3, 0:LANES]) & seen
    strips[...] = jnp.where(apart != 0, MASKED, moved)

    def one(wh, carry):
        strip = strips[pl.ds(pl.multiple_of(wh * 2 * SITE, 8), 2 * SITE), :]
        start = lax.rem(wh, LWIN) * STACK + lax.div(wh, LWIN) * WIN
        for pair in range(WLON // 2):
            offset = (WLON - 2 - 2 * pair) * SITE
            scores[pl.ds(pl.multiple_of(start + pair * 24, 8), 24), :] = strip[
                :, offset : offset + WIN
            ]
        return carry

    lax.fori_loop(0, WH, one, 0)


def collapse_bias(first, last, scores, strips):
    def one(wh, carry):
        start = lax.rem(wh, LWIN) * STACK + lax.div(wh, LWIN) * WIN
        total = jnp.zeros((2 * SITE, LANES), F32)
        for pair in range(WLON // 2):
            offset = (WLON - 2 - 2 * pair) * SITE
            part = scores[pl.ds(pl.multiple_of(start + pair * 24, 8), 24), :]
            part = jnp.concatenate([part, jnp.zeros((2 * SITE, LANES - WIN), F32)], axis=1)
            total = total + (pltpu.roll(part, offset, 1) if offset else part)
        strips[pl.ds(pl.multiple_of(wh * 2 * SITE, 8), 2 * SITE), :] = total
        return carry

    lax.fori_loop(first, last, one, 0)


def join_strips(strips, columns, index_rows):
    total = strips[...]
    total = jnp.where((columns[:, 2:3] & 8) != 0, pltpu.roll(total, SITE, 1), total)
    rows = one_hot(index_rows[1:2, :], SITE * WH, WH * 2 * SITE)
    return sum(dot(rows, part) for part in pieces(total, 2))


def block_kernel(n_lon, n_lat, *refs):
    loaded = refs[:9]
    out_field, grad_field, qkv, proj, fc1, fc2, bias = refs[9:16]
    field, cot, w_qkv, w_proj, w_fc1, w_fc2, table, columns, index_rows, load_sem = refs[16:26]
    (
        out, e_out, l_out, b_out, sent, came, back, halo_send, halo_recv,
        xw, uw, scores, normed, query, key, value, unit, rate, blended, normed_two, hidden,
        cot_first, cot_mid, cot_q, cot_k, cot_v, ow, gw, tall_table, gathered, strips, w3,
        places_in, places_out, lanes,
    ) = refs[26:61]
    here = Here(n_lon, n_lat)
    early = WeightSum(here, e_out, refs[61:69])
    late = WeightSum(here, l_out, refs[69:77])
    strip_sum = BiasSum(here, b_out, refs[77:83])

    loads = [
        pltpu.make_async_copy(src, dst, load_sem.at[i]) for i, (src, dst) in enumerate(zip(loaded, refs[16:25]))
    ]
    begin(loads)
    greeted = here.greet()
    loads[0].wait()
    for index in range(3):
        sent[0, index] = pack(quarter(field, index))
    greeted()
    inward = [
        halo(here, sent.at[i], came.at[i], halo_send.at[i], halo_recv.at[i], -1) for i in range(2)
    ]
    outward = [
        halo(here, back.at[i], out.at[i], halo_send.at[2 + i], halo_recv.at[2 + i], 1) for i in range(2)
    ]
    begin(inward[0])
    end(loads[6:9])
    lanes[...] = one_hot(columns[0:STRIP, 3:4], STRIP, LANES)
    last_lat = here.lat == n_lat - 1
    expand_bias(last_lat, table, columns, index_rows, lanes, tall_table, gathered, strips, scores)
    places_in[...] = one_hot(columns[:, 0:1], TOK, TOK)
    places_out[...] = one_hot(index_rows[0:1, :], TOK, TOK)
    loads[1].wait()
    for index in range(3):
        sent[1, index] = pack(quarter(cot, index))
    loads[2].wait()
    for third in range(3):
        w3[third] = w_qkv[:, third * C : (third + 1) * C]

    def gather(kind, ref):
        parts = [quarter(ref, 3)] + [unpack(came[kind, i]) for i in range(1, 4)]
        whole = jnp.concatenate(parts, axis=0).astype(BF16)
        return dot(places_in[...], whole).astype(BF16)

    def scatter(kind, ref):
        whole = dot(places_out[...], ref[...])
        out[kind, 3] = pack(whole[:QUAD])
        for i in range(1, 4):
            back[kind, i] = pack(whole[i * QUAD : (i + 1) * QUAD])
        begin(outward[kind])

    def places(w):
        return pl.ds(w * WIN, WIN), pl.ds(w * STACK, STACK)

    def attend(w):
        rows, tall = places(w)
        unit_x, rate_x = layer_norm(xw[rows, :].astype(F32))
        unit[rows, :] = unit_x
        rate[rows, :] = rate_x
        norm = unit_x.astype(BF16)
        normed[rows, :] = norm
        q = dot(norm, w3[0]).astype(BF16)
        k = dot(norm, w3[1]).astype(BF16)
        v = dot(norm, w3[2]).astype(BF16)
        query[rows, :] = q
        key[rows, :] = k
        value[rows, :] = v
        s = dot_nt(stacked(q), k) * (SCALE * LOG2E) + scores[tall, :]
        e = jnp.exp2(s - jnp.max(s, axis=-1, keepdims=True))
        p = e * (1.0 / jnp.sum(e, axis=-1, keepdims=True))
        scores[tall, :] = p
        blended[rows, :] = unstacked(dot(p.astype(BF16), v)).astype(BF16)

    def feed(w):
        rows = pl.ds(w * 2 * WIN, 2 * WIN)
        middle = xw[rows, :].astype(F32) + dot(blended[rows, :], w_proj[...])
        middle = middle.astype(BF16).astype(F32)
        unit_m, rate_m = layer_norm(middle)
        norm_m = unit_m.astype(BF16)
        normed_two[rows, :] = norm_m
        first = dot(norm_m, w_fc1[...])
        phi = 0.5 + 0.5 * lax.erf(first * math.sqrt(0.5))
        hid = (first * phi).astype(BF16)
        hidden[rows, :] = hid
        bell = jnp.exp2(first * first * (-0.5 * LOG2E)) * (1.0 / math.sqrt(2.0 * math.pi))
        slope = phi + first * bell
        ow[rows, :] = (middle + dot_nt(hid, w_fc2[...])).astype(BF16)
        up = uw[rows, :]
        c_first = (dot(up, w_fc2[...]).astype(BF16).astype(F32) * slope).astype(BF16)
        cot_first[rows, :] = c_first
        c_norm = dot_nt(c_first, w_fc1[...]).astype(BF16).astype(F32)
        c_mid = layer_norm_back(c_norm, unit_m, rate_m).astype(BF16).astype(F32)
        cot_mid[rows, :] = (up.astype(F32) + c_mid).astype(BF16)

    def backward(w):
        rows, tall = places(w)
        up = cot_mid[rows, :]
        c_blend = stacked(dot_nt(up, w_proj[...]).astype(BF16))
        p = scores[tall, :]
        c_p = dot_nt(c_blend, value[rows, :])
        c_s = p * (c_p - jnp.sum(p * c_p, axis=-1, keepdims=True))
        scores[tall, :] = c_s
        c_v = dot_tn(p.astype(BF16), c_blend).astype(BF16)
        narrow = c_s.astype(BF16)
        c_q = (unstacked(dot(narrow, key[rows, :])) * SCALE).astype(BF16)
        c_k = (dot_tn(narrow, stacked(query[rows, :])) * SCALE).astype(BF16)
        cot_q[rows, :] = c_q
        cot_k[rows, :] = c_k
        cot_v[rows, :] = c_v

    def inputs_back(w):
        rows = pl.ds(w * 2 * WIN, 2 * WIN)
        c_norm = dot_nt(cot_q[rows, :], w3[0]) + dot_nt(cot_k[rows, :], w3[1])
        c_norm = (c_norm + dot_nt(cot_v[rows, :], w3[2])).astype(BF16).astype(F32)
        c_x = layer_norm_back(c_norm, unit[rows, :], rate[rows, :]).astype(BF16)
        gw[rows, :] = (cot_mid[rows, :].astype(F32) + c_x.astype(F32)).astype(BF16)

    end(inward[0])
    begin(inward[1])
    xw[...] = gather(0, field)
    for w in range(LWIN):
        attend(w)
    end(loads[3:6])
    end(inward[1])
    uw[...] = gather(1, cot)
    feed(0)
    feed(1)
    early.put(0, dot_tn(normed_two[...], cot_first[...]))
    early.put(1, dot_tn(uw[...], hidden[...]))
    early.start()
    scatter(0, ow)
    backward(0)
    backward(1)
    early.step(0)
    backward(2)
    backward(3)
    early.step(1)
    norm = normed[...]
    late.put(0, jnp.concatenate([dot_tn(norm, cot_q[...]), dot_tn(norm, cot_k[...])], axis=1))
    c_proj = dot_tn(blended[...], cot_mid[...])
    late.put(1, jnp.concatenate([dot_tn(norm, cot_v[...]), c_proj], axis=1))
    late.start()
    collapse_bias(0, WH, scores, strips)
    strip_sum.put(join_strips(strips, columns, index_rows))
    strip_sum.start()
    late.step(0)
    early.step(2)
    strip_sum.step(0)
    late.step(1)
    early.step(3)
    inputs_back(0)
    inputs_back(1)
    scatter(1, gw)
    late.step(2)
    early.step(4)
    late.step(3)
    strip_sum.step(1)
    end(outward[0])
    for index in range(4):
        whole_quarter(out_field, index, out[0, index])
    early.step(5)
    fc1[...] = joined(tiles_of(e_out, 0), 6)
    fc2[...] = joined(tiles_of(e_out, 1), 6)
    late.step(4)
    strip_sum.step(2)
    end(outward[1])
    for index in range(4):
        whole_quarter(grad_field, index, out[1, index])
    late.step(5)
    qkv[:, 0:384] = joined(tiles_of(l_out, 0), 3)
    right = joined(tiles_of(l_out, 1), 3)
    qkv[:, 384:576] = right[:, 0:C]
    proj[...] = right[:, C:]
    strip_sum.step(3)
    finish_bias(b_out, lanes, tall_table, bias)


def whole_quarter(target, index, packed):
    part = unpack(packed).reshape(6, 3, LEV, C).astype(BF16)
    target[pl.ds((index // 2) * 6, 6), pl.ds((index % 2) * 3, 3)] = part


def joined(tiles, columns):
    rows = len(tiles) // columns
    cols = [jnp.concatenate(tiles[c * rows : (c + 1) * rows], axis=0) for c in range(columns)]
    return jnp.concatenate(cols, axis=1).astype(F32)


def tiles_of(ref, half):
    n1 = ref.shape[3]
    return [ref[half, i // (4 * n1), i // n1 % 4, i % n1] for i in range(12 * n1)]


def finish_bias(b_in, lanes, tall_table, bias):
    tiles = [b_in[t // B_TILES, t % B_TILES // 4, t % B_TILES % 4] for t in range(2 * B_TILES)]
    runs = dot_nt(joined(tiles, 3).astype(BF16), lanes[...])
    for site in range(SITE):
        lev, a = site // WLAT, site % WLAT
        for other in range(WLEV):
            start = ((lev * WLEV + other) * WLAT + a) * RUN
            tall_table[:, start : start + RUN] = runs[
                site * WH : (site + 1) * WH, other * RUN : (other + 1) * RUN
            ]
    for head in range(HEADS):
        bias[head] = tall_table[head * LWIN : (head + 1) * LWIN, :]


def finish_kernel(*refs):
    count = len(refs) // 2
    copies = [pltpu.make_async_copy(refs[i], refs[count + i], refs[-1].at[i]) for i in range(count)]
    begin(copies)
    end(copies)


def per_device(n_lon, n_lat, field, w_qkv, w_proj, w_fc1, w_fc2, bias_table, cotangent):
    vmem, hbm = pl.BlockSpec(memory_space=pltpu.VMEM), pl.BlockSpec(memory_space=pltpu.HBM)
    shape = jax.ShapeDtypeStruct
    dma = pltpu.SemaphoreType.DMA
    rows = row_places()
    columns = columns_of(token_places(), rows, row_codes(), lane_places())
    index_rows = columns_of(token_places(), rows, lane_codes()).T.copy()
    inputs = (
        field, cotangent, w_qkv, w_proj, w_fc1, w_fc2.T, bias_table[0].transpose(1, 0, 2), columns, index_rows
    )
    inputs = [pltpu.with_memory_space_constraint(jnp.asarray(a), pltpu.HBM) for a in inputs]
    tile = shape((WLON, WLAT, LEV, C), BF16)
    outputs = (
        tile,
        tile,
        shape((C, 3 * C), F32),
        shape((C, C), F32),
        shape((C, HIDDEN), F32),
        shape((C, HIDDEN), F32),
        shape((HEADS, LWIN, POS), F32),
    )
    wide = lambda dtype, n=1: [pltpu.VMEM((TOK, C), dtype)] * n
    results = pl.pallas_call(
        functools.partial(block_kernel, n_lon, n_lat),
        out_shape=outputs,
        in_specs=[hbm] * len(inputs),
        out_specs=[vmem] * len(outputs),
        scratch_shapes=[
            *[pltpu.VMEM(a.shape, a.dtype) for a in inputs],
            dma((len(inputs),)),
            pltpu.VMEM((2, 4, PACKED, 128), BF16),
            pltpu.VMEM((2, 3, RING, E_TILES // 12, *TILE), BF16),
            pltpu.VMEM((2, 3, RING, L_TILES // 12, *TILE), BF16),
            pltpu.VMEM((2, 8, B_ROOM // 8, *TILE), BF16),
            pltpu.VMEM((2, 3, PACKED, 128), BF16),
            pltpu.VMEM((2, 4, PACKED, 128), BF16),
            pltpu.VMEM((2, 4, PACKED, 128), BF16),
            dma((4, 3)),
            dma((4, 3)),
            *wide(BF16, 2),
            pltpu.VMEM((LWIN * STACK, WIN), F32),
            *wide(BF16, 4),
            *wide(F32),
            pltpu.VMEM((TOK, 1), F32),
            *wide(BF16, 2),
            pltpu.VMEM((TOK, HIDDEN), BF16),
            pltpu.VMEM((TOK, HIDDEN), BF16),
            *wide(BF16, 6),
            pltpu.VMEM((WH, POS), F32),
            pltpu.VMEM((SITE * WH, STRIP), F32),
            pltpu.VMEM((WH * 2 * SITE, LANES), F32),
            pltpu.VMEM((3, C, C), BF16),
            pltpu.VMEM((TOK, TOK), BF16),
            pltpu.VMEM((TOK, TOK), BF16),
            pltpu.VMEM((STRIP, LANES), BF16),
            *WeightSum.scratch(E_TILES),
            *WeightSum.scratch(L_TILES),
            *BiasSum.scratch(),
        ],
        compiler_params=pltpu.CompilerParams(
            vmem_limit_bytes=VMEM_LIMIT, collective_id=0, has_side_effects=True
        ),
        name="block",
    )(*inputs)
    *results, fc2, bias = pl.pallas_call(
        finish_kernel,
        out_shape=outputs,
        in_specs=[vmem] * len(outputs),
        out_specs=[hbm] * len(outputs),
        scratch_shapes=[dma((len(outputs),))],
        compiler_params=pltpu.CompilerParams(vmem_limit_bytes=VMEM_LIMIT),
        name="finish",
    )(*results)
    return (*results, fc2.T, bias.transpose(1, 0, 2)[None])


def solution(mesh):
    whole, tiles, banded = P(), P("lon", "lat", None, None), P("lat", None, None, None)
    return jax.shard_map(
        functools.partial(per_device, mesh.shape["lon"], mesh.shape["lat"]),
        mesh=mesh,
        in_specs=(tiles, whole, whole, whole, whole, banded, tiles),
        out_specs=(tiles, tiles, whole, whole, whole, whole, banded),
        check_vma=False,
    )
```

```python
import functools
import math

import jax
import jax.numpy as jnp
import numpy as np
from jax import lax
from jax.experimental import pallas as pl
from jax.experimental.pallas import tpu as pltpu
from jax.sharding import PartitionSpec as P

C = 192
HEADS = 6
HIDDEN = 768
LEV = 8
WLON = 12
WLAT = 6
WLEV = 2
LWIN = LEV // WLEV
WH = LWIN * HEADS
WIN = WLEV * WLAT * WLON
TOK = LWIN * WIN
QUAD = TOK // 4
SITE = WLEV * WLAT
SHIFTS = 2 * WLON - 1
STRIP = SHIFTS * SITE
POS = WLEV * WLEV * WLAT * WLAT * SHIFTS
RUN = WLAT * SHIFTS
LANES = 384
STACK = HEADS * WIN
EPSILON = 1e-05
MASKED = -1000000000.0
LOG2E = math.log2(math.e)
SCALE = 1.0 / math.sqrt(C // HEADS)
RING = 4
E_TILES = 144
L_TILES = 72
B_TILES = 40
B_LEFT = STRIP - 256
B_ROWS = 48
PACKED = 224
TILE = (16, 128)
BF16 = jnp.bfloat16
F32 = jnp.float32
MESH = pl.DeviceIdType.MESH
VMEM_LIMIT = 30 * 1024 * 1024


def token_places():
    w, o, lev, a = np.meshgrid(
        np.arange(LWIN), np.arange(WLON), np.arange(WLEV), np.arange(WLAT), indexing="ij"
    )
    quarter = (o // 6) * 2 + a // 3
    level = (2 * w + lev + 1) % LEV
    return (quarter * QUAD + ((o % 6) * 3 + a % 3) * LEV + level).reshape(TOK).astype(np.int32)


def lane_places():
    lev, a, d = np.meshgrid(np.arange(WLEV), np.arange(WLAT), np.arange(SHIFTS), indexing="ij")
    return ((SHIFTS - 1 - d) * SITE + lev * WLAT + a).reshape(STRIP).astype(np.int32)


def row_places():
    wh, _, site = np.meshgrid(np.arange(WH), np.arange(2), np.arange(SITE), indexing="ij")
    return (site * WH + wh).reshape(WH * 2 * SITE).astype(np.int32)


def row_codes():
    _, w, p, lev, a = np.meshgrid(
        np.arange(HEADS), np.arange(LWIN), np.arange(2), np.arange(WLEV), np.arange(WLAT), indexing="ij"
    )
    code = lev + 2 * (a >= WLAT // 2) + 4 * (w == LWIN - 1) + 8 * (p == 0)
    return code.reshape(WH * 2 * SITE).astype(np.int32)


def lane_codes():
    site = np.arange(LANES) % SITE
    return (site // WLAT + 2 * (site % WLAT >= WLAT // 2)).astype(np.int32)


def columns_of(*arrays):
    made = np.zeros((TOK, 8), np.int32)
    for i, array in enumerate(arrays):
        made[: len(array), i] = array
    return made


def dot(a, b):
    return jnp.dot(a, b, preferred_element_type=F32)


def dot_nt(a, b):
    return lax.dot_general(a, b, (((1,), (1,)), ((), ())), preferred_element_type=F32)


def dot_tn(a, b):
    return lax.dot_general(a, b, (((0,), (0,)), ((), ())), preferred_element_type=F32)


def one_hot(places, rows, cols):
    along = 1 if places.shape[1] == 1 else 0
    index = lax.broadcasted_iota(jnp.int32, (rows, cols), along)
    return jnp.where(index == places, 1.0, 0.0).astype(BF16)


def pieces(value, count):
    found = []
    for _ in range(count):
        part = value.astype(BF16)
        found.append(part)
        value = value - part.astype(F32)
    return found


def quarter(ref, index):
    part = ref[pl.ds((index // 2) * 6, 6), pl.ds((index % 2) * 3, 3)]
    return part.astype(F32).reshape(QUAD, C)


def pack(value):
    half = QUAD // 2
    rest = jnp.concatenate([value[:half, 128:], value[half:, 128:]], axis=1)
    blank = jnp.zeros((PACKED - QUAD - half, 128), F32)
    return jnp.concatenate([value[:, :128], rest, blank], axis=0).astype(BF16)


def unpack(value):
    half = QUAD // 2
    wide = value.astype(F32)
    rest = wide[QUAD : QUAD + half]
    right = jnp.concatenate([rest[:, :64], rest[:, 64:]], axis=0)
    return jnp.concatenate([wide[:QUAD], right], axis=1)


def place_of(lon, lat):
    x = lax.rem(lat, 2) * 2 + lax.div(lon, 8)
    return (x, lax.rem(lax.div(lon, 2), RING), lax.div(lat, 2)), lax.rem(lon, 2)


def device_at(chip, core):
    x, y, z = chip
    return ((lax.rem(x, 2) * RING + y) * 2 + core, z * 2 + lax.div(x, 2))


def moved(chip, axis, step):
    return tuple(lax.rem(c + step, RING) if i == axis else c for i, c in enumerate(chip))


def remote(src, dst, send, recv, device):
    return pltpu.make_async_remote_copy(
        src_ref=src, dst_ref=dst, send_sem=send, recv_sem=recv, device_id=device, device_id_type=MESH
    )


class Here:
    def __init__(self, n_lon, n_lat):
        self.lon, self.lat = lax.axis_index("lon"), lax.axis_index("lat")
        self.chip, self.core = place_of(self.lon, self.lat)
        self.slot = [[lax.rem(c + k, RING) for k in range(RING)] for c in self.chip]
        chips = [[moved(self.chip, axis, k) for k in range(RING)] for axis in range(3)]
        self.along = [[device_at(chip, self.core) for chip in ring] for ring in chips]
        other = 1 - self.core
        self.eight = []
        for axis in range(3):
            found = []
            for k in range(RING):
                if k:
                    found.append((self.along[axis][k], self.slot[axis][k], self.core))
                found.append((device_at(chips[axis][k], other), self.slot[axis][k], other))
            self.eight.append(found)
        self.facing = (lax.rem(self.lon + 8, 16), self.lat)
        self.across = {}
        for step in (-1, 1):
            to_lon = lax.rem(self.lon + n_lon + step, n_lon)
            to_lat = lax.rem(self.lat + n_lat + step, n_lat)
            self.across[step] = ((to_lon, to_lat), (to_lon, self.lat), (self.lon, to_lat))

    def greet(self):
        others = [*self.across[-1], *self.across[1], self.facing]
        for axis in range(3):
            others += [device for device, _, _ in self.eight[axis]]
        barrier = pltpu.get_barrier_semaphore()
        for device in others:
            pl.semaphore_signal(barrier, inc=1, device_id=device, device_id_type=MESH)
        return lambda: pl.semaphore_wait(barrier, len(others))


def halo(here, source, target, send, recv, step):
    copies = []
    for index in range(3):
        src = index if step < 0 else 3 - index
        device = here.across[step][index]
        copies.append(remote(source.at[src], target.at[3 - src], send.at[index], recv.at[index], device))
    return copies


def begin(copies):
    for copy in copies:
        copy.start()


def end(copies):
    for copy in copies:
        copy.wait()


def wait_bytes(like, sem):
    pltpu.make_async_copy(like, like, sem).wait()


def room(*dims):
    return pltpu.VMEM((*dims, *TILE), BF16)


def tiles_in(block):
    narrow = block.astype(BF16)
    for c in range(block.shape[1] // 128):
        for r in range(block.shape[0] // 16):
            yield narrow[r * 16 : (r + 1) * 16, c * 128 : (c + 1) * 128]


def added(terms):
    total = terms[0].astype(F32)
    for term in terms[1:]:
        total = total + term.astype(F32)
    return total.astype(BF16)


class WeightSum:
    def __init__(self, here, out, refs):
        self.here, self.out = here, out
        self.src, self.r1, self.x2, self.x3, self.send, self.recv = refs

    @staticmethod
    def scratch(tiles):
        n1 = tiles // 24
        dma = pltpu.SemaphoreType.DMA
        return [room(3, RING, 2, n1), room(7, 3, n1), room(3, RING, n1), room(3, RING, n1), dma((4,)), dma((4,))]

    def put(self, block, first):
        n1 = self.src.shape[3]
        for at, tile in enumerate(tiles_in(block), first):
            self.src[at // (8 * n1), at // (2 * n1) % RING, at // n1 % 2, at % n1] = tile

    def phase(self, at):
        here, made = self.here, []
        sems = self.send.at[at], self.recv.at[at]
        for t in range(3):
            if at in (0, 3):
                mine = self.out.at[t, here.slot[t][0], here.core]
                for k, (device, slot, core) in enumerate(here.eight[t]):
                    if at == 0:
                        made.append(remote(self.src.at[t, slot, core], self.r1.at[k, t], *sems, device))
                    else:
                        made.append(remote(mine, mine, *sems, device))
            else:
                axis = (t + at) % 3
                mine = (self.x2 if at == 1 else self.x3).at[t, here.slot[axis][0]]
                made += [remote(mine, mine, *sems, here.along[axis][k]) for k in range(1, RING)]
        return made

    def start(self):
        begin(self.phase(0))

    def step(self, at):
        like = self.r1 if at in (0, 3) else self.r1.at[pl.ds(0, 3)]
        wait_bytes(like, self.recv.at[at])
        wait_bytes(like, self.send.at[at])
        core = self.here.core
        for t in range(3):
            one, two, three = (self.here.slot[(t + i) % 3][0] for i in range(3))
            if at == 0:
                self.x2[t, two] = added([self.src[t, one, core]] + [self.r1[k, t] for k in range(7)])
            if at == 1:
                self.x3[t, three] = added([self.x2[t, k] for k in range(RING)])
            if at == 2:
                self.out[t, one, core] = added([self.x3[t, k] for k in range(RING)])
        if at < 3:
            begin(self.phase(at + 1))


class BiasSum:
    def __init__(self, here, out, refs):
        self.here, self.out = here, out
        self.src, self.r1, self.x2, self.send, self.recv = refs

    @staticmethod
    def scratch():
        each = B_TILES // 8
        dma = pltpu.SemaphoreType.DMA
        return [room(RING, 2, each), room(7, each), room(2, each), dma((3,)), dma((3,))]

    def put(self, block):
        each = B_TILES // 8
        last = block[:, 256:]
        shared = last[0:B_ROWS]
        for g in range(1, 288 // B_ROWS):
            shared = shared + pltpu.roll(last[g * B_ROWS : (g + 1) * B_ROWS], g * B_LEFT, 1)
        tiles = [*tiles_in(block[:, :256]), *tiles_in(shared), jnp.zeros(TILE, BF16)]
        for at, tile in enumerate(tiles):
            self.src[at // (2 * each), at // each % 2, at % each] = tile

    def get(self):
        each = B_TILES // 8
        tiles = [self.out[at // (2 * each), at // each % 2, at % each] for at in range(B_TILES)]
        first = joined(tiles[:36], 2)
        shared = joined(tiles[36:39], 1)
        last = [shared]
        for g in range(1, 288 // B_ROWS):
            last.append(pltpu.roll(shared, 128 - g * B_LEFT, 1))
        return jnp.concatenate([first, jnp.concatenate(last, axis=0)], axis=1)

    def phase(self, at):
        here, made = self.here, []
        sems = self.send.at[at], self.recv.at[at]
        if at == 1:
            return [remote(self.x2.at[0], self.x2.at[1], *sems, here.facing)]
        mine = self.out.at[here.slot[1][0], here.core]
        for k, (device, slot, core) in enumerate(here.eight[1]):
            if at == 0:
                made.append(remote(self.src.at[slot, core], self.r1.at[k], *sems, device))
            else:
                made.append(remote(mine, mine, *sems, device))
        return made

    def start(self):
        begin(self.phase(0))

    def step(self, at):
        like = self.x2.at[1] if at == 1 else self.r1
        wait_bytes(like, self.recv.at[at])
        wait_bytes(like, self.send.at[at])
        slot, core = self.here.slot[1][0], self.here.core
        if at == 0:
            self.x2[0] = added([self.src[slot, core]] + [self.r1[k] for k in range(7)])
        if at == 1:
            self.out[slot, core] = added([self.x2[0], self.x2[1]])
        if at < 2:
            begin(self.phase(at + 1))


def layer_norm(x):
    centered = x - jnp.mean(x, axis=-1, keepdims=True)
    spread = jnp.mean(centered * centered, axis=-1, keepdims=True)
    rate = lax.rsqrt(spread + EPSILON)
    return centered * rate, rate


def layer_norm_back(cot, unit, rate):
    first = jnp.mean(cot, axis=-1, keepdims=True)
    second = jnp.mean(cot * unit, axis=-1, keepdims=True)
    return rate * (cot - first - unit * second)


def head_mask(head):
    lane = lax.broadcasted_iota(jnp.int32, (1, C), 1)
    return (lane >= head * 32) & (lane < head * 32 + 32)


def stacked(value):
    wide = value.astype(F32)
    parts = [jnp.where(head_mask(h), wide, 0.0).astype(BF16) for h in range(HEADS)]
    return jnp.concatenate(parts, axis=0)


def unstacked(value):
    total = jnp.where(head_mask(0), value[0:WIN], 0.0)
    for h in range(1, HEADS):
        total = total + jnp.where(head_mask(h), value[h * WIN : (h + 1) * WIN], 0.0)
    return total


def expand_bias(last_lat, table, columns, index_rows, lanes, tall_table, gathered, strips, scores):
    for head in range(HEADS):
        tall_table[head * LWIN : (head + 1) * LWIN, :] = table[head]
    for site in range(SITE):
        lev, a = site // WLAT, site % WLAT
        for other in range(WLEV):
            start = ((lev * WLEV + other) * WLAT + a) * RUN
            gathered[site * WH : (site + 1) * WH, other * RUN : (other + 1) * RUN] = tall_table[
                :, start : start + RUN
            ]
    moved = sum(dot(part, lanes[...]) for part in pieces(gathered[...], 3))
    rows = one_hot(columns[:, 1:2], WH * 2 * SITE, SITE * WH)
    moved = sum(dot(rows, part) for part in pieces(moved, 3))
    code = columns[:, 2:3]
    moved = jnp.where((code & 8) != 0, pltpu.roll(moved, LANES - SITE, 1), moved) * LOG2E
    seen = jnp.where((code & 4) != 0, 1, 0) + jnp.where(last_lat, 2, 0)
    apart = (code ^ index_rows[2:3, 0:LANES]) & seen
    strips[...] = jnp.where(apart != 0, MASKED, moved)

    def one(wh, carry):
        strip = strips[pl.ds(pl.multiple_of(wh * 2 * SITE, 8), 2 * SITE), :]
        start = lax.rem(wh, LWIN) * STACK + lax.div(wh, LWIN) * WIN
        for pair in range(WLON // 2):
            offset = (WLON - 2 - 2 * pair) * SITE
            scores[pl.ds(pl.multiple_of(start + pair * 24, 8), 24), :] = strip[
                :, offset : offset + WIN
            ]
        return carry

    lax.fori_loop(0, WH, one, 0)


def collapse_bias(first, last, scores, strips):
    def one(wh, carry):
        start = lax.rem(wh, LWIN) * STACK + lax.div(wh, LWIN) * WIN
        total = jnp.zeros((2 * SITE, LANES), F32)
        for pair in range(WLON // 2):
            offset = (WLON - 2 - 2 * pair) * SITE
            part = scores[pl.ds(pl.multiple_of(start + pair * 24, 8), 24), :]
            part = jnp.concatenate([part, jnp.zeros((2 * SITE, LANES - WIN), F32)], axis=1)
            total = total + (pltpu.roll(part, offset, 1) if offset else part)
        strips[pl.ds(pl.multiple_of(wh * 2 * SITE, 8), 2 * SITE), :] = total
        return carry

    lax.fori_loop(first, last, one, 0)


def join_strips(strips, columns, index_rows):
    total = strips[...]
    total = jnp.where((columns[:, 2:3] & 8) != 0, pltpu.roll(total, SITE, 1), total)
    rows = one_hot(index_rows[1:2, :], SITE * WH, WH * 2 * SITE)
    return sum(dot(rows, part) for part in pieces(total, 2))


def block_kernel(n_lon, n_lat, *refs):
    loaded = refs[:9]
    out_field, grad_field, qkv, proj, fc1, fc2, bias = refs[9:16]
    field, cot, w_qkv, w_proj, w_fc1, w_fc2, table, columns, index_rows, load_sem = refs[16:26]
    (
        out, e_out, l_out, b_out, sent, came, back, halo_send, halo_recv,
        xw, uw, scores, normed, query, key, value, unit, rate, blended, normed_two, hidden,
        cot_first, cot_mid, cot_q, cot_k, cot_v, ow, gw, tall_table, gathered, strips, w3,
        places_in, places_out, lanes,
    ) = refs[26:61]
    here = Here(n_lon, n_lat)
    early = WeightSum(here, e_out, refs[61:67])
    late = WeightSum(here, l_out, refs[67:73])
    strip_sum = BiasSum(here, b_out, refs[73:78])

    loads = [
        pltpu.make_async_copy(src, dst, load_sem.at[i]) for i, (src, dst) in enumerate(zip(loaded, refs[16:25]))
    ]
    begin(loads)
    greeted = here.greet()
    loads[0].wait()
    for index in range(3):
        sent[0, index] = pack(quarter(field, index))
    greeted()
    inward = [
        halo(here, sent.at[i], came.at[i], halo_send.at[i], halo_recv.at[i], -1) for i in range(2)
    ]
    outward = [
        halo(here, back.at[i], out.at[i], halo_send.at[2 + i], halo_recv.at[2 + i], 1) for i in range(2)
    ]
    begin(inward[0])
    end(loads[6:9])
    lanes[...] = one_hot(columns[0:STRIP, 3:4], STRIP, LANES)
    last_lat = here.lat == n_lat - 1
    expand_bias(last_lat, table, columns, index_rows, lanes, tall_table, gathered, strips, scores)
    places_in[...] = one_hot(columns[:, 0:1], TOK, TOK)
    places_out[...] = one_hot(index_rows[0:1, :], TOK, TOK)
    loads[1].wait()
    for index in range(3):
        sent[1, index] = pack(quarter(cot, index))
    loads[2].wait()
    for third in range(3):
        w3[third] = w_qkv[:, third * C : (third + 1) * C]

    def gather(kind, ref):
        parts = [quarter(ref, 3)] + [unpack(came[kind, i]) for i in range(1, 4)]
        whole = jnp.concatenate(parts, axis=0).astype(BF16)
        return dot(places_in[...], whole).astype(BF16)

    def scatter(kind, ref):
        whole = dot(places_out[...], ref[...])
        out[kind, 3] = pack(whole[:QUAD])
        for i in range(1, 4):
            back[kind, i] = pack(whole[i * QUAD : (i + 1) * QUAD])
        begin(outward[kind])

    def places(w):
        return pl.ds(w * WIN, WIN), pl.ds(w * STACK, STACK)

    def attend(w):
        rows, tall = places(w)
        unit_x, rate_x = layer_norm(xw[rows, :].astype(F32))
        unit[rows, :] = unit_x
        rate[rows, :] = rate_x
        norm = unit_x.astype(BF16)
        normed[rows, :] = norm
        q = dot(norm, w3[0]).astype(BF16)
        k = dot(norm, w3[1]).astype(BF16)
        v = dot(norm, w3[2]).astype(BF16)
        query[rows, :] = q
        key[rows, :] = k
        value[rows, :] = v
        s = dot_nt(stacked(q), k) * (SCALE * LOG2E) + scores[tall, :]
        e = jnp.exp2(s - jnp.max(s, axis=-1, keepdims=True))
        p = e * (1.0 / jnp.sum(e, axis=-1, keepdims=True))
        scores[tall, :] = p
        blended[rows, :] = unstacked(dot(p.astype(BF16), v)).astype(BF16)

    def feed(w):
        rows = pl.ds(w * 2 * WIN, 2 * WIN)
        middle = xw[rows, :].astype(F32) + dot(blended[rows, :], w_proj[...])
        middle = middle.astype(BF16).astype(F32)
        unit_m, rate_m = layer_norm(middle)
        norm_m = unit_m.astype(BF16)
        normed_two[rows, :] = norm_m
        first = dot(norm_m, w_fc1[...])
        phi = 0.5 + 0.5 * lax.erf(first * math.sqrt(0.5))
        hid = (first * phi).astype(BF16)
        hidden[rows, :] = hid
        bell = jnp.exp2(first * first * (-0.5 * LOG2E)) * (1.0 / math.sqrt(2.0 * math.pi))
        slope = phi + first * bell
        ow[rows, :] = (middle + dot_nt(hid, w_fc2[...])).astype(BF16)
        up = uw[rows, :]
        c_first = (dot(up, w_fc2[...]).astype(BF16).astype(F32) * slope).astype(BF16)
        cot_first[rows, :] = c_first
        c_norm = dot_nt(c_first, w_fc1[...]).astype(BF16).astype(F32)
        c_mid = layer_norm_back(c_norm, unit_m, rate_m).astype(BF16).astype(F32)
        cot_mid[rows, :] = (up.astype(F32) + c_mid).astype(BF16)

    def backward(w):
        rows, tall = places(w)
        up = cot_mid[rows, :]
        c_blend = stacked(dot_nt(up, w_proj[...]).astype(BF16))
        p = scores[tall, :]
        c_p = dot_nt(c_blend, value[rows, :])
        c_s = p * (c_p - jnp.sum(p * c_p, axis=-1, keepdims=True))
        scores[tall, :] = c_s
        c_v = dot_tn(p.astype(BF16), c_blend).astype(BF16)
        narrow = c_s.astype(BF16)
        c_q = (unstacked(dot(narrow, key[rows, :])) * SCALE).astype(BF16)
        c_k = (dot_tn(narrow, stacked(query[rows, :])) * SCALE).astype(BF16)
        cot_q[rows, :] = c_q
        cot_k[rows, :] = c_k
        cot_v[rows, :] = c_v

    def inputs_back(w):
        rows = pl.ds(w * 2 * WIN, 2 * WIN)
        c_norm = dot_nt(cot_q[rows, :], w3[0]) + dot_nt(cot_k[rows, :], w3[1])
        c_norm = (c_norm + dot_nt(cot_v[rows, :], w3[2])).astype(BF16).astype(F32)
        c_x = layer_norm_back(c_norm, unit[rows, :], rate[rows, :]).astype(BF16)
        gw[rows, :] = (cot_mid[rows, :].astype(F32) + c_x.astype(F32)).astype(BF16)

    end(inward[0])
    begin(inward[1])
    xw[...] = gather(0, field)
    for w in range(LWIN):
        attend(w)
    end(loads[3:6])
    end(inward[1])
    uw[...] = gather(1, cot)
    feed(0)
    feed(1)
    early.put(dot_tn(normed_two[...], cot_first[...]), 0)
    early.put(dot_tn(uw[...], hidden[...]), 72)
    early.start()
    scatter(0, ow)
    backward(0)
    backward(1)
    early.step(0)
    backward(2)
    backward(3)
    early.step(1)
    norm = normed[...]
    late.put(jnp.concatenate([dot_tn(norm, cot_q[...]), dot_tn(norm, cot_k[...])], axis=1), 0)
    c_proj = dot_tn(blended[...], cot_mid[...])
    late.put(jnp.concatenate([dot_tn(norm, cot_v[...]), c_proj], axis=1), 36)
    late.start()
    collapse_bias(0, WH, scores, strips)
    strip_sum.put(join_strips(strips, columns, index_rows))
    strip_sum.start()
    early.step(2)
    inputs_back(0)
    inputs_back(1)
    late.step(0)
    scatter(1, gw)
    strip_sum.step(0)
    early.step(3)
    late.step(1)
    fc1[...] = joined(tiles_of(e_out)[:72], 6)
    fc2[...] = joined(tiles_of(e_out)[72:], 6)
    strip_sum.step(1)
    end(outward[0])
    for index in range(4):
        whole_quarter(out_field, index, out[0, index])
    late.step(2)
    strip_sum.step(2)
    finish_bias(strip_sum.get(), lanes, tall_table, bias)
    end(outward[1])
    for index in range(4):
        whole_quarter(grad_field, index, out[1, index])
    late.step(3)
    qkv[:, 0:384] = joined(tiles_of(l_out)[:36], 3)
    right = joined(tiles_of(l_out)[36:], 3)
    qkv[:, 384:576] = right[:, 0:C]
    proj[...] = right[:, C:]


def whole_quarter(target, index, packed):
    part = unpack(packed).reshape(6, 3, LEV, C).astype(BF16)
    target[pl.ds((index // 2) * 6, 6), pl.ds((index % 2) * 3, 3)] = part


def joined(tiles, columns):
    rows = len(tiles) // columns
    cols = [jnp.concatenate(tiles[c * rows : (c + 1) * rows], axis=0) for c in range(columns)]
    return jnp.concatenate(cols, axis=1).astype(F32)


def tiles_of(ref):
    n1 = ref.shape[3]
    return [ref[i // (8 * n1), i // (2 * n1) % RING, i // n1 % 2, i % n1] for i in range(24 * n1)]


def finish_bias(strip, lanes, tall_table, bias):
    runs = dot_nt(strip.astype(BF16), lanes[...])
    for site in range(SITE):
        lev, a = site // WLAT, site % WLAT
        for other in range(WLEV):
            start = ((lev * WLEV + other) * WLAT + a) * RUN
            tall_table[:, start : start + RUN] = runs[
                site * WH : (site + 1) * WH, other * RUN : (other + 1) * RUN
            ]
    for head in range(HEADS):
        bias[head] = tall_table[head * LWIN : (head + 1) * LWIN, :]


def finish_kernel(*refs):
    count = len(refs) // 2
    copies = [pltpu.make_async_copy(refs[i], refs[count + i], refs[-1].at[i]) for i in range(count)]
    begin(copies)
    end(copies)


def per_device(n_lon, n_lat, field, w_qkv, w_proj, w_fc1, w_fc2, bias_table, cotangent):
    vmem, hbm = pl.BlockSpec(memory_space=pltpu.VMEM), pl.BlockSpec(memory_space=pltpu.HBM)
    shape = jax.ShapeDtypeStruct
    dma = pltpu.SemaphoreType.DMA
    rows = row_places()
    columns = columns_of(token_places(), rows, row_codes(), lane_places())
    index_rows = columns_of(token_places(), rows, lane_codes()).T.copy()
    inputs = (
        field, cotangent, w_qkv, w_proj, w_fc1, w_fc2.T, bias_table[0].transpose(1, 0, 2), columns, index_rows
    )
    inputs = [pltpu.with_memory_space_constraint(jnp.asarray(a), pltpu.HBM) for a in inputs]
    tile = shape((WLON, WLAT, LEV, C), BF16)
    outputs = (
        tile,
        tile,
        shape((C, 3 * C), F32),
        shape((C, C), F32),
        shape((C, HIDDEN), F32),
        shape((C, HIDDEN), F32),
        shape((HEADS, LWIN, POS), F32),
    )
    wide = lambda dtype, n=1: [pltpu.VMEM((TOK, C), dtype)] * n
    results = pl.pallas_call(
        functools.partial(block_kernel, n_lon, n_lat),
        out_shape=outputs,
        in_specs=[hbm] * len(inputs),
        out_specs=[vmem] * len(outputs),
        scratch_shapes=[
            *[pltpu.VMEM(a.shape, a.dtype) for a in inputs],
            dma((len(inputs),)),
            pltpu.VMEM((2, 4, PACKED, 128), BF16),
            room(3, RING, 2, E_TILES // 24),
            room(3, RING, 2, L_TILES // 24),
            room(RING, 2, B_TILES // 8),
            pltpu.VMEM((2, 3, PACKED, 128), BF16),
            pltpu.VMEM((2, 4, PACKED, 128), BF16),
            pltpu.VMEM((2, 4, PACKED, 128), BF16),
            dma((4, 3)),
            dma((4, 3)),
            *wide(BF16, 2),
            pltpu.VMEM((LWIN * STACK, WIN), F32),
            *wide(BF16, 4),
            *wide(F32),
            pltpu.VMEM((TOK, 1), F32),
            *wide(BF16, 2),
            pltpu.VMEM((TOK, HIDDEN), BF16),
            pltpu.VMEM((TOK, HIDDEN), BF16),
            *wide(BF16, 6),
            pltpu.VMEM((WH, POS), F32),
            pltpu.VMEM((SITE * WH, STRIP), F32),
            pltpu.VMEM((WH * 2 * SITE, LANES), F32),
            pltpu.VMEM((3, C, C), BF16),
            pltpu.VMEM((TOK, TOK), BF16),
            pltpu.VMEM((TOK, TOK), BF16),
            pltpu.VMEM((STRIP, LANES), BF16),
            *WeightSum.scratch(E_TILES),
            *WeightSum.scratch(L_TILES),
            *BiasSum.scratch(),
        ],
        compiler_params=pltpu.CompilerParams(
            vmem_limit_bytes=VMEM_LIMIT, collective_id=0, has_side_effects=True
        ),
        name="block",
    )(*inputs)
    *results, fc2, bias = pl.pallas_call(
        finish_kernel,
        out_shape=outputs,
        in_specs=[vmem] * len(outputs),
        out_specs=[hbm] * len(outputs),
        scratch_shapes=[dma((len(outputs),))],
        compiler_params=pltpu.CompilerParams(vmem_limit_bytes=VMEM_LIMIT),
        name="finish",
    )(*results)
    return (*results, fc2.T, bias.transpose(1, 0, 2)[None])


def solution(mesh):
    whole, tiles, banded = P(), P("lon", "lat", None, None), P("lat", None, None, None)
    return jax.shard_map(
        functools.partial(per_device, mesh.shape["lon"], mesh.shape["lat"]),
        mesh=mesh,
        in_specs=(tiles, whole, whole, whole, whole, banded, tiles),
        out_specs=(tiles, tiles, whole, whole, whole, whole, banded),
        check_vma=False,
    )
```

```python
import functools
import math

import jax
import jax.numpy as jnp
import numpy as np
from jax import lax
from jax.experimental import pallas as pl
from jax.experimental.pallas import tpu as pltpu
from jax.sharding import PartitionSpec as P

C = 192
HEADS = 6
HIDDEN = 768
LEV = 8
WLON = 12
WLAT = 6
WLEV = 2
LWIN = LEV // WLEV
WH = LWIN * HEADS
WIN = WLEV * WLAT * WLON
TOK = LWIN * WIN
QUAD = TOK // 4
SITE = WLEV * WLAT
SHIFTS = 2 * WLON - 1
STRIP = SHIFTS * SITE
POS = WLEV * WLEV * WLAT * WLAT * SHIFTS
RUN = WLAT * SHIFTS
LANES = 384
STACK = HEADS * WIN
EPSILON = 1e-05
MASKED = -1000000000.0
LOG2E = math.log2(math.e)
SCALE = 1.0 / math.sqrt(C // HEADS)
RING = 4
E_TILES = 144
L_TILES = 72
B_TILES = 40
B_LEFT = STRIP - 256
B_ROWS = 48
PACKED = 224
TILE = (16, 128)
BF16 = jnp.bfloat16
F32 = jnp.float32
MESH = pl.DeviceIdType.MESH
VMEM_LIMIT = 30 * 1024 * 1024


def token_places():
    w, o, lev, a = np.meshgrid(
        np.arange(LWIN), np.arange(WLON), np.arange(WLEV), np.arange(WLAT), indexing="ij"
    )
    quarter = (o // 6) * 2 + a // 3
    level = (2 * w + lev + 1) % LEV
    return (quarter * QUAD + ((o % 6) * 3 + a % 3) * LEV + level).reshape(TOK).astype(np.int32)


def lane_places():
    lev, a, d = np.meshgrid(np.arange(WLEV), np.arange(WLAT), np.arange(SHIFTS), indexing="ij")
    return ((SHIFTS - 1 - d) * SITE + lev * WLAT + a).reshape(STRIP).astype(np.int32)


def row_places():
    wh, _, site = np.meshgrid(np.arange(WH), np.arange(2), np.arange(SITE), indexing="ij")
    return (site * WH + wh).reshape(WH * 2 * SITE).astype(np.int32)


def row_codes():
    _, w, p, lev, a = np.meshgrid(
        np.arange(HEADS), np.arange(LWIN), np.arange(2), np.arange(WLEV), np.arange(WLAT), indexing="ij"
    )
    code = lev + 2 * (a >= WLAT // 2) + 4 * (w == LWIN - 1) + 8 * (p == 0)
    return code.reshape(WH * 2 * SITE).astype(np.int32)


def lane_codes():
    site = np.arange(LANES) % SITE
    return (site // WLAT + 2 * (site % WLAT >= WLAT // 2)).astype(np.int32)


def columns_of(*arrays):
    made = np.zeros((TOK, 8), np.int32)
    for i, array in enumerate(arrays):
        made[: len(array), i] = array
    return made


def dot(a, b):
    return jnp.dot(a, b, preferred_element_type=F32)


def dot_nt(a, b):
    return lax.dot_general(a, b, (((1,), (1,)), ((), ())), preferred_element_type=F32)


def dot_tn(a, b):
    return lax.dot_general(a, b, (((0,), (0,)), ((), ())), preferred_element_type=F32)


def one_hot(places, rows, cols):
    along = 1 if places.shape[1] == 1 else 0
    index = lax.broadcasted_iota(jnp.int32, (rows, cols), along)
    return jnp.where(index == places, 1.0, 0.0).astype(BF16)


def pieces(value, count):
    found = []
    for _ in range(count):
        part = value.astype(BF16)
        found.append(part)
        value = value - part.astype(F32)
    return found


def quarter(ref, index):
    part = ref[pl.ds((index // 2) * 6, 6), pl.ds((index % 2) * 3, 3)]
    return part.astype(F32).reshape(QUAD, C)


def pack(value):
    half = QUAD // 2
    rest = jnp.concatenate([value[:half, 128:], value[half:, 128:]], axis=1)
    blank = jnp.zeros((PACKED - QUAD - half, 128), F32)
    return jnp.concatenate([value[:, :128], rest, blank], axis=0).astype(BF16)


def unpack(value):
    half = QUAD // 2
    wide = value.astype(F32)
    rest = wide[QUAD : QUAD + half]
    right = jnp.concatenate([rest[:, :64], rest[:, 64:]], axis=0)
    return jnp.concatenate([wide[:QUAD], right], axis=1)


def place_of(lon, lat):
    x = lax.rem(lat, 2) * 2 + lax.div(lon, 8)
    return (x, lax.rem(lax.div(lon, 2), RING), lax.div(lat, 2)), lax.rem(lon, 2)


def device_at(chip, core):
    x, y, z = chip
    return ((lax.rem(x, 2) * RING + y) * 2 + core, z * 2 + lax.div(x, 2))


def moved(chip, axis, step):
    return tuple(lax.rem(c + step, RING) if i == axis else c for i, c in enumerate(chip))


def remote(src, dst, send, recv, device):
    return pltpu.make_async_remote_copy(
        src_ref=src, dst_ref=dst, send_sem=send, recv_sem=recv, device_id=device, device_id_type=MESH
    )


class Here:
    def __init__(self, n_lon, n_lat):
        self.lon, self.lat = lax.axis_index("lon"), lax.axis_index("lat")
        self.chip, self.core = place_of(self.lon, self.lat)
        self.sibling = (self.lon + 1 - 2 * self.core, self.lat)
        self.slot = [[lax.rem(c + k, RING) for k in range(RING)] for c in self.chip]
        chips = [[moved(self.chip, axis, k) for k in range(RING)] for axis in range(3)]
        self.along = [[device_at(chip, self.core) for chip in ring] for ring in chips]
        other = 1 - self.core
        self.eight = []
        for axis in range(3):
            found = []
            for k in range(RING):
                if k:
                    found.append((self.along[axis][k], self.slot[axis][k], self.core))
                found.append((device_at(chips[axis][k], other), self.slot[axis][k], other))
            self.eight.append(found)
        self.facing = (lax.rem(self.lon + 8, 16), self.lat)
        self.across = {}
        for step in (-1, 1):
            to_lon = lax.rem(self.lon + n_lon + step, n_lon)
            to_lat = lax.rem(self.lat + n_lat + step, n_lat)
            self.across[step] = ((to_lon, to_lat), (to_lon, self.lat), (self.lon, to_lat))

    def greet(self):
        others = [*self.across[-1], *self.across[1], self.facing]
        for axis in range(3):
            others += [device for device, _, _ in self.eight[axis]]
        barrier = pltpu.get_barrier_semaphore()
        for device in others:
            pl.semaphore_signal(barrier, inc=1, device_id=device, device_id_type=MESH)
        return lambda: pl.semaphore_wait(barrier, len(others))


def halo(here, source, target, send, recv, step):
    copies = []
    for index in range(3):
        src = index if step < 0 else 3 - index
        device = here.across[step][index]
        copies.append(remote(source.at[src], target.at[3 - src], send.at[index], recv.at[index], device))
    return copies


def begin(copies):
    for copy in copies:
        copy.start()


def end(copies):
    for copy in copies:
        copy.wait()


def wait_bytes(like, sem):
    pltpu.make_async_copy(like, like, sem).wait()


def room(*dims):
    return pltpu.VMEM((*dims, *TILE), BF16)


def tiles_in(block):
    narrow = block.astype(BF16)
    for c in range(block.shape[1] // 128):
        for r in range(block.shape[0] // 16):
            yield narrow[r * 16 : (r + 1) * 16, c * 128 : (c + 1) * 128]


def added(terms):
    total = terms[0].astype(F32)
    for term in terms[1:]:
        total = total + term.astype(F32)
    return total.astype(BF16)


class WeightSum:
    def __init__(self, here, out, refs):
        self.here, self.out = here, out
        self.src, self.r1, self.x2, self.x3, self.send, self.recv = refs

    @staticmethod
    def scratch(tiles):
        n1 = tiles // 24
        dma = pltpu.SemaphoreType.DMA
        return [room(3, RING, 2, n1), room(7, 3, n1), room(3, RING, n1), room(3, RING, n1), dma((4,)), dma((4,))]

    def put(self, block, first):
        n1 = self.src.shape[3]
        for at, tile in enumerate(tiles_in(block), first):
            self.src[at // (8 * n1), at // (2 * n1) % RING, at // n1 % 2, at % n1] = tile

    def phase(self, at):
        here, made = self.here, []
        sems = self.send.at[at], self.recv.at[at]
        for t in range(3):
            if at in (0, 3):
                mine = self.out.at[t, here.slot[t][0], here.core]
                for k, (device, slot, core) in enumerate(here.eight[t]):
                    if at == 0:
                        made.append(remote(self.src.at[t, slot, core], self.r1.at[k, t], *sems, device))
                    else:
                        made.append(remote(mine, mine, *sems, device))
            else:
                axis = (t + at) % 3
                mine = (self.x2 if at == 1 else self.x3).at[t, here.slot[axis][0]]
                made += [remote(mine, mine, *sems, here.along[axis][k]) for k in range(1, RING)]
        return made

    def start(self):
        begin(self.phase(0))

    def step(self, at):
        like = self.r1 if at in (0, 3) else self.r1.at[pl.ds(0, 3)]
        wait_bytes(like, self.recv.at[at])
        wait_bytes(like, self.send.at[at])
        core = self.here.core
        for t in range(3):
            one, two, three = (self.here.slot[(t + i) % 3][0] for i in range(3))
            if at == 0:
                self.x2[t, two] = added([self.src[t, one, core]] + [self.r1[k, t] for k in range(7)])
            if at == 1:
                self.x3[t, three] = added([self.x2[t, k] for k in range(RING)])
            if at == 2:
                self.out[t, one, core] = added([self.x3[t, k] for k in range(RING)])
        if at < 3:
            begin(self.phase(at + 1))


class PairSum:
    def __init__(self, here, out, refs):
        self.here, self.out = here, out
        self.src, self.other, self.a1, self.r1, self.x2, self.x3, self.send, self.recv = refs

    @staticmethod
    def scratch(tiles):
        n1 = tiles // 24
        dma = pltpu.SemaphoreType.DMA
        return [
            room(2, tiles // 2), room(tiles // 2),
            room(3, RING, n1), room(3, RING - 1, n1), room(3, RING, n1), room(3, RING, n1),
            dma((6,)), dma((6,)),
        ]

    def put(self, block, first):
        each = self.src.shape[1]
        for at, tile in enumerate(tiles_in(block), first):
            self.src[at // each, at % each] = tile

    def get(self):
        n1 = self.a1.shape[2]
        return [self.out[i // (12 * n1), i // (4 * n1) % 3, i // n1 % 4, i % n1] for i in range(24 * n1)]

    def copies(self, at, axis_of, source, target):
        made = []
        for t in range(3):
            axis = (t + axis_of) % 3
            slot = self.here.slot[axis]
            for k in range(1, RING):
                made.append(
                    remote(
                        source(t, slot[k], slot[0]), target(t, k - 1, slot[0]),
                        self.send.at[at], self.recv.at[at], self.here.along[axis][k],
                    )
                )
        return made

    def phase(self, at):
        core = self.here.core
        if at == 0:
            return [remote(self.src.at[1 - core], self.other, self.send.at[0], self.recv.at[0], self.here.sibling)]
        if at == 1:
            return self.copies(1, 0, lambda t, to, me: self.a1.at[t, to], lambda t, k, me: self.r1.at[t, k])
        if at == 2:
            return self.copies(2, 1, lambda t, to, me: self.x2.at[t, me], lambda t, k, me: self.x2.at[t, me])
        if at == 3:
            return self.copies(3, 2, lambda t, to, me: self.x3.at[t, me], lambda t, k, me: self.x3.at[t, me])
        if at == 4:
            out = self.out.at[core]
            return self.copies(4, 0, lambda t, to, me: out.at[t, me], lambda t, k, me: out.at[t, me])
        return [remote(self.out.at[core], self.out.at[core], self.send.at[5], self.recv.at[5], self.here.sibling)]

    def start(self):
        begin(self.phase(0))

    def step(self, at):
        like = self.other if at in (0, 5) else self.r1
        wait_bytes(like, self.recv.at[at])
        wait_bytes(like, self.send.at[at])
        core = self.here.core
        if at == 0:
            total = self.src[core].astype(F32) + self.other[...].astype(F32)
            self.a1[...] = total.astype(BF16).reshape(self.a1.shape)
        for t in range(3):
            one, two, three = (self.here.slot[(t + i) % 3][0] for i in range(3))
            if at == 1:
                total = self.a1[t, one].astype(F32)
                for k in range(RING - 1):
                    total = total + self.r1[t, k].astype(F32)
                self.x2[t, two] = total.astype(BF16)
            if at in (2, 3):
                came = self.x2 if at == 2 else self.x3
                total = came[t, 0].astype(F32)
                for k in range(1, RING):
                    total = total + came[t, k].astype(F32)
                if at == 2:
                    self.x3[t, three] = total.astype(BF16)
                else:
                    self.out[core, t, one] = total.astype(BF16)
        if at < 5:
            begin(self.phase(at + 1))


class BiasSum:
    def __init__(self, here, out, refs):
        self.here, self.out = here, out
        self.src, self.r1, self.x2, self.send, self.recv = refs

    @staticmethod
    def scratch():
        each = B_TILES // 8
        dma = pltpu.SemaphoreType.DMA
        return [room(RING, 2, each), room(7, each), room(2, each), dma((3,)), dma((3,))]

    def put(self, block):
        each = B_TILES // 8
        last = block[:, 256:]
        shared = last[0:B_ROWS]
        for g in range(1, 288 // B_ROWS):
            shared = shared + pltpu.roll(last[g * B_ROWS : (g + 1) * B_ROWS], g * B_LEFT, 1)
        tiles = [*tiles_in(block[:, :256]), *tiles_in(shared), jnp.zeros(TILE, BF16)]
        for at, tile in enumerate(tiles):
            self.src[at // (2 * each), at // each % 2, at % each] = tile

    def get(self):
        each = B_TILES // 8
        tiles = [self.out[at // (2 * each), at // each % 2, at % each] for at in range(B_TILES)]
        first = joined(tiles[:36], 2)
        shared = joined(tiles[36:39], 1)
        last = [shared]
        for g in range(1, 288 // B_ROWS):
            last.append(pltpu.roll(shared, 128 - g * B_LEFT, 1))
        return jnp.concatenate([first, jnp.concatenate(last, axis=0)], axis=1)

    def phase(self, at):
        here, made = self.here, []
        sems = self.send.at[at], self.recv.at[at]
        if at == 1:
            return [remote(self.x2.at[0], self.x2.at[1], *sems, here.facing)]
        mine = self.out.at[here.slot[1][0], here.core]
        for k, (device, slot, core) in enumerate(here.eight[1]):
            if at == 0:
                made.append(remote(self.src.at[slot, core], self.r1.at[k], *sems, device))
            else:
                made.append(remote(mine, mine, *sems, device))
        return made

    def start(self):
        begin(self.phase(0))

    def step(self, at):
        like = self.x2.at[1] if at == 1 else self.r1
        wait_bytes(like, self.recv.at[at])
        wait_bytes(like, self.send.at[at])
        slot, core = self.here.slot[1][0], self.here.core
        if at == 0:
            self.x2[0] = added([self.src[slot, core]] + [self.r1[k] for k in range(7)])
        if at == 1:
            self.out[slot, core] = added([self.x2[0], self.x2[1]])
        if at < 2:
            begin(self.phase(at + 1))


def layer_norm(x):
    centered = x - jnp.mean(x, axis=-1, keepdims=True)
    spread = jnp.mean(centered * centered, axis=-1, keepdims=True)
    rate = lax.rsqrt(spread + EPSILON)
    return centered * rate, rate


def layer_norm_back(cot, unit, rate):
    first = jnp.mean(cot, axis=-1, keepdims=True)
    second = jnp.mean(cot * unit, axis=-1, keepdims=True)
    return rate * (cot - first - unit * second)


def head_mask(head):
    lane = lax.broadcasted_iota(jnp.int32, (1, C), 1)
    return (lane >= head * 32) & (lane < head * 32 + 32)


def stacked(value):
    wide = value.astype(F32)
    parts = [jnp.where(head_mask(h), wide, 0.0).astype(BF16) for h in range(HEADS)]
    return jnp.concatenate(parts, axis=0)


def unstacked(value):
    total = jnp.where(head_mask(0), value[0:WIN], 0.0)
    for h in range(1, HEADS):
        total = total + jnp.where(head_mask(h), value[h * WIN : (h + 1) * WIN], 0.0)
    return total


def expand_bias(last_lat, table, columns, index_rows, lanes, tall_table, gathered, strips, scores):
    for head in range(HEADS):
        tall_table[head * LWIN : (head + 1) * LWIN, :] = table[head]
    for site in range(SITE):
        lev, a = site // WLAT, site % WLAT
        for other in range(WLEV):
            start = ((lev * WLEV + other) * WLAT + a) * RUN
            gathered[site * WH : (site + 1) * WH, other * RUN : (other + 1) * RUN] = tall_table[
                :, start : start + RUN
            ]
    moved = sum(dot(part, lanes[...]) for part in pieces(gathered[...], 3))
    rows = one_hot(columns[:, 1:2], WH * 2 * SITE, SITE * WH)
    moved = sum(dot(rows, part) for part in pieces(moved, 3))
    code = columns[:, 2:3]
    moved = jnp.where((code & 8) != 0, pltpu.roll(moved, LANES - SITE, 1), moved) * LOG2E
    seen = jnp.where((code & 4) != 0, 1, 0) + jnp.where(last_lat, 2, 0)
    apart = (code ^ index_rows[2:3, 0:LANES]) & seen
    strips[...] = jnp.where(apart != 0, MASKED, moved)

    def one(wh, carry):
        strip = strips[pl.ds(pl.multiple_of(wh * 2 * SITE, 8), 2 * SITE), :]
        start = lax.rem(wh, LWIN) * STACK + lax.div(wh, LWIN) * WIN
        for pair in range(WLON // 2):
            offset = (WLON - 2 - 2 * pair) * SITE
            scores[pl.ds(pl.multiple_of(start + pair * 24, 8), 24), :] = strip[
                :, offset : offset + WIN
            ]
        return carry

    lax.fori_loop(0, WH, one, 0)


def collapse_bias(first, last, scores, strips):
    def one(wh, carry):
        start = lax.rem(wh, LWIN) * STACK + lax.div(wh, LWIN) * WIN
        total = jnp.zeros((2 * SITE, LANES), F32)
        for pair in range(WLON // 2):
            offset = (WLON - 2 - 2 * pair) * SITE
            part = scores[pl.ds(pl.multiple_of(start + pair * 24, 8), 24), :]
            part = jnp.concatenate([part, jnp.zeros((2 * SITE, LANES - WIN), F32)], axis=1)
            total = total + (pltpu.roll(part, offset, 1) if offset else part)
        strips[pl.ds(pl.multiple_of(wh * 2 * SITE, 8), 2 * SITE), :] = total
        return carry

    lax.fori_loop(first, last, one, 0)


def join_strips(strips, columns, index_rows):
    total = strips[...]
    total = jnp.where((columns[:, 2:3] & 8) != 0, pltpu.roll(total, SITE, 1), total)
    rows = one_hot(index_rows[1:2, :], SITE * WH, WH * 2 * SITE)
    return sum(dot(rows, part) for part in pieces(total, 2))


def block_kernel(n_lon, n_lat, *refs):
    loaded = refs[:9]
    out_field, grad_field, qkv, proj, fc1, fc2, bias = refs[9:16]
    field, cot, w_qkv, w_proj, w_fc1, w_fc2, table, columns, index_rows, load_sem = refs[16:26]
    (
        out, e_out, l_out, b_out, sent, came, back, halo_send, halo_recv,
        xw, uw, scores, normed, query, key, value, unit, rate, blended, normed_two, hidden,
        cot_first, cot_mid, cot_q, cot_k, cot_v, ow, gw, tall_table, gathered, strips, w3,
        places_in, places_out, lanes,
    ) = refs[26:61]
    here = Here(n_lon, n_lat)
    early = PairSum(here, e_out, refs[61:69])
    late = WeightSum(here, l_out, refs[69:75])
    strip_sum = BiasSum(here, b_out, refs[75:80])

    loads = [
        pltpu.make_async_copy(src, dst, load_sem.at[i]) for i, (src, dst) in enumerate(zip(loaded, refs[16:25]))
    ]
    begin(loads)
    greeted = here.greet()
    loads[0].wait()
    for index in range(3):
        sent[0, index] = pack(quarter(field, index))
    greeted()
    inward = [
        halo(here, sent.at[i], came.at[i], halo_send.at[i], halo_recv.at[i], -1) for i in range(2)
    ]
    outward = [
        halo(here, back.at[i], out.at[i], halo_send.at[2 + i], halo_recv.at[2 + i], 1) for i in range(2)
    ]
    begin(inward[0])
    end(loads[6:9])
    lanes[...] = one_hot(columns[0:STRIP, 3:4], STRIP, LANES)
    last_lat = here.lat == n_lat - 1
    expand_bias(last_lat, table, columns, index_rows, lanes, tall_table, gathered, strips, scores)
    places_in[...] = one_hot(columns[:, 0:1], TOK, TOK)
    places_out[...] = one_hot(index_rows[0:1, :], TOK, TOK)
    loads[1].wait()
    for index in range(3):
        sent[1, index] = pack(quarter(cot, index))
    loads[2].wait()
    for third in range(3):
        w3[third] = w_qkv[:, third * C : (third + 1) * C]

    def gather(kind, ref):
        parts = [quarter(ref, 3)] + [unpack(came[kind, i]) for i in range(1, 4)]
        whole = jnp.concatenate(parts, axis=0).astype(BF16)
        return dot(places_in[...], whole).astype(BF16)

    def scatter(kind, ref):
        whole = dot(places_out[...], ref[...])
        out[kind, 3] = pack(whole[:QUAD])
        for i in range(1, 4):
            back[kind, i] = pack(whole[i * QUAD : (i + 1) * QUAD])
        begin(outward[kind])

    def places(w):
        return pl.ds(w * WIN, WIN), pl.ds(w * STACK, STACK)

    def attend(w):
        rows, tall = places(w)
        unit_x, rate_x = layer_norm(xw[rows, :].astype(F32))
        unit[rows, :] = unit_x
        rate[rows, :] = rate_x
        norm = unit_x.astype(BF16)
        normed[rows, :] = norm
        q = dot(norm, w3[0]).astype(BF16)
        k = dot(norm, w3[1]).astype(BF16)
        v = dot(norm, w3[2]).astype(BF16)
        query[rows, :] = q
        key[rows, :] = k
        value[rows, :] = v
        s = dot_nt(stacked(q), k) * (SCALE * LOG2E) + scores[tall, :]
        e = jnp.exp2(s - jnp.max(s, axis=-1, keepdims=True))
        p = e * (1.0 / jnp.sum(e, axis=-1, keepdims=True))
        scores[tall, :] = p
        blended[rows, :] = unstacked(dot(p.astype(BF16), v)).astype(BF16)

    def feed(w):
        rows = pl.ds(w * 2 * WIN, 2 * WIN)
        middle = xw[rows, :].astype(F32) + dot(blended[rows, :], w_proj[...])
        middle = middle.astype(BF16).astype(F32)
        unit_m, rate_m = layer_norm(middle)
        norm_m = unit_m.astype(BF16)
        normed_two[rows, :] = norm_m
        first = dot(norm_m, w_fc1[...])
        phi = 0.5 + 0.5 * lax.erf(first * math.sqrt(0.5))
        hid = (first * phi).astype(BF16)
        hidden[rows, :] = hid
        bell = jnp.exp2(first * first * (-0.5 * LOG2E)) * (1.0 / math.sqrt(2.0 * math.pi))
        slope = phi + first * bell
        ow[rows, :] = (middle + dot_nt(hid, w_fc2[...])).astype(BF16)
        up = uw[rows, :]
        c_first = (dot(up, w_fc2[...]).astype(BF16).astype(F32) * slope).astype(BF16)
        cot_first[rows, :] = c_first
        c_norm = dot_nt(c_first, w_fc1[...]).astype(BF16).astype(F32)
        c_mid = layer_norm_back(c_norm, unit_m, rate_m).astype(BF16).astype(F32)
        cot_mid[rows, :] = (up.astype(F32) + c_mid).astype(BF16)

    def backward(w):
        rows, tall = places(w)
        up = cot_mid[rows, :]
        c_blend = stacked(dot_nt(up, w_proj[...]).astype(BF16))
        p = scores[tall, :]
        c_p = dot_nt(c_blend, value[rows, :])
        c_s = p * (c_p - jnp.sum(p * c_p, axis=-1, keepdims=True))
        scores[tall, :] = c_s
        c_v = dot_tn(p.astype(BF16), c_blend).astype(BF16)
        narrow = c_s.astype(BF16)
        c_q = (unstacked(dot(narrow, key[rows, :])) * SCALE).astype(BF16)
        c_k = (dot_tn(narrow, stacked(query[rows, :])) * SCALE).astype(BF16)
        cot_q[rows, :] = c_q
        cot_k[rows, :] = c_k
        cot_v[rows, :] = c_v

    def inputs_back(w):
        rows = pl.ds(w * 2 * WIN, 2 * WIN)
        c_norm = dot_nt(cot_q[rows, :], w3[0]) + dot_nt(cot_k[rows, :], w3[1])
        c_norm = (c_norm + dot_nt(cot_v[rows, :], w3[2])).astype(BF16).astype(F32)
        c_x = layer_norm_back(c_norm, unit[rows, :], rate[rows, :]).astype(BF16)
        gw[rows, :] = (cot_mid[rows, :].astype(F32) + c_x.astype(F32)).astype(BF16)

    end(inward[0])
    begin(inward[1])
    xw[...] = gather(0, field)
    for w in range(LWIN):
        attend(w)
    end(loads[3:6])
    end(inward[1])
    uw[...] = gather(1, cot)
    feed(0)
    feed(1)
    early.put(dot_tn(normed_two[...], cot_first[...]), 0)
    early.put(dot_tn(uw[...], hidden[...]), 72)
    early.start()
    scatter(0, ow)
    backward(0)
    backward(1)
    early.step(0)
    backward(2)
    backward(3)
    early.step(1)
    norm = normed[...]
    late.put(jnp.concatenate([dot_tn(norm, cot_q[...]), dot_tn(norm, cot_k[...])], axis=1), 0)
    c_proj = dot_tn(blended[...], cot_mid[...])
    late.put(jnp.concatenate([dot_tn(norm, cot_v[...]), c_proj], axis=1), 36)
    late.start()
    collapse_bias(0, WH, scores, strips)
    strip_sum.put(join_strips(strips, columns, index_rows))
    strip_sum.start()
    early.step(2)
    inputs_back(0)
    inputs_back(1)
    late.step(0)
    scatter(1, gw)
    early.step(3)
    strip_sum.step(0)
    late.step(1)
    early.step(4)
    strip_sum.step(1)
    end(outward[0])
    for index in range(4):
        whole_quarter(out_field, index, out[0, index])
    late.step(2)
    early.step(5)
    fc1[...] = joined(early.get()[:72], 6)
    fc2[...] = joined(early.get()[72:], 6)
    strip_sum.step(2)
    finish_bias(strip_sum.get(), lanes, tall_table, bias)
    end(outward[1])
    for index in range(4):
        whole_quarter(grad_field, index, out[1, index])
    late.step(3)
    qkv[:, 0:384] = joined(tiles_of(l_out)[:36], 3)
    right = joined(tiles_of(l_out)[36:], 3)
    qkv[:, 384:576] = right[:, 0:C]
    proj[...] = right[:, C:]


def whole_quarter(target, index, packed):
    part = unpack(packed).reshape(6, 3, LEV, C).astype(BF16)
    target[pl.ds((index // 2) * 6, 6), pl.ds((index % 2) * 3, 3)] = part


def joined(tiles, columns):
    rows = len(tiles) // columns
    cols = [jnp.concatenate(tiles[c * rows : (c + 1) * rows], axis=0) for c in range(columns)]
    return jnp.concatenate(cols, axis=1).astype(F32)


def tiles_of(ref):
    n1 = ref.shape[3]
    return [ref[i // (8 * n1), i // (2 * n1) % RING, i // n1 % 2, i % n1] for i in range(24 * n1)]


def finish_bias(strip, lanes, tall_table, bias):
    runs = dot_nt(strip.astype(BF16), lanes[...])
    for site in range(SITE):
        lev, a = site // WLAT, site % WLAT
        for other in range(WLEV):
            start = ((lev * WLEV + other) * WLAT + a) * RUN
            tall_table[:, start : start + RUN] = runs[
                site * WH : (site + 1) * WH, other * RUN : (other + 1) * RUN
            ]
    for head in range(HEADS):
        bias[head] = tall_table[head * LWIN : (head + 1) * LWIN, :]


def finish_kernel(*refs):
    count = len(refs) // 2
    copies = [pltpu.make_async_copy(refs[i], refs[count + i], refs[-1].at[i]) for i in range(count)]
    begin(copies)
    end(copies)


def per_device(n_lon, n_lat, field, w_qkv, w_proj, w_fc1, w_fc2, bias_table, cotangent):
    vmem, hbm = pl.BlockSpec(memory_space=pltpu.VMEM), pl.BlockSpec(memory_space=pltpu.HBM)
    shape = jax.ShapeDtypeStruct
    dma = pltpu.SemaphoreType.DMA
    rows = row_places()
    columns = columns_of(token_places(), rows, row_codes(), lane_places())
    index_rows = columns_of(token_places(), rows, lane_codes()).T.copy()
    inputs = (
        field, cotangent, w_qkv, w_proj, w_fc1, w_fc2.T, bias_table[0].transpose(1, 0, 2), columns, index_rows
    )
    inputs = [pltpu.with_memory_space_constraint(jnp.asarray(a), pltpu.HBM) for a in inputs]
    tile = shape((WLON, WLAT, LEV, C), BF16)
    outputs = (
        tile,
        tile,
        shape((C, 3 * C), F32),
        shape((C, C), F32),
        shape((C, HIDDEN), F32),
        shape((C, HIDDEN), F32),
        shape((HEADS, LWIN, POS), F32),
    )
    wide = lambda dtype, n=1: [pltpu.VMEM((TOK, C), dtype)] * n
    results = pl.pallas_call(
        functools.partial(block_kernel, n_lon, n_lat),
        out_shape=outputs,
        in_specs=[hbm] * len(inputs),
        out_specs=[vmem] * len(outputs),
        scratch_shapes=[
            *[pltpu.VMEM(a.shape, a.dtype) for a in inputs],
            dma((len(inputs),)),
            pltpu.VMEM((2, 4, PACKED, 128), BF16),
            room(2, 3, RING, E_TILES // 24),
            room(3, RING, 2, L_TILES // 24),
            room(RING, 2, B_TILES // 8),
            pltpu.VMEM((2, 3, PACKED, 128), BF16),
            pltpu.VMEM((2, 4, PACKED, 128), BF16),
            pltpu.VMEM((2, 4, PACKED, 128), BF16),
            dma((4, 3)),
            dma((4, 3)),
            *wide(BF16, 2),
            pltpu.VMEM((LWIN * STACK, WIN), F32),
            *wide(BF16, 4),
            *wide(F32),
            pltpu.VMEM((TOK, 1), F32),
            *wide(BF16, 2),
            pltpu.VMEM((TOK, HIDDEN), BF16),
            pltpu.VMEM((TOK, HIDDEN), BF16),
            *wide(BF16, 6),
            pltpu.VMEM((WH, POS), F32),
            pltpu.VMEM((SITE * WH, STRIP), F32),
            pltpu.VMEM((WH * 2 * SITE, LANES), F32),
            pltpu.VMEM((3, C, C), BF16),
            pltpu.VMEM((TOK, TOK), BF16),
            pltpu.VMEM((TOK, TOK), BF16),
            pltpu.VMEM((STRIP, LANES), BF16),
            *PairSum.scratch(E_TILES),
            *WeightSum.scratch(L_TILES),
            *BiasSum.scratch(),
        ],
        compiler_params=pltpu.CompilerParams(
            vmem_limit_bytes=VMEM_LIMIT, collective_id=0, has_side_effects=True
        ),
        name="block",
    )(*inputs)
    *results, fc2, bias = pl.pallas_call(
        finish_kernel,
        out_shape=outputs,
        in_specs=[vmem] * len(outputs),
        out_specs=[hbm] * len(outputs),
        scratch_shapes=[dma((len(outputs),))],
        compiler_params=pltpu.CompilerParams(vmem_limit_bytes=VMEM_LIMIT),
        name="finish",
    )(*results)
    return (*results, fc2.T, bias.transpose(1, 0, 2)[None])


def solution(mesh):
    whole, tiles, banded = P(), P("lon", "lat", None, None), P("lat", None, None, None)
    return jax.shard_map(
        functools.partial(per_device, mesh.shape["lon"], mesh.shape["lat"]),
        mesh=mesh,
        in_specs=(tiles, whole, whole, whole, whole, banded, tiles),
        out_specs=(tiles, tiles, whole, whole, whole, whole, banded),
        check_vma=False,
    )
```

```python
import functools
import math

import jax
import jax.numpy as jnp
import numpy as np
from jax import lax
from jax.experimental import pallas as pl
from jax.experimental.pallas import tpu as pltpu
from jax.sharding import PartitionSpec as P

C = 192
HEADS = 6
HIDDEN = 768
LEV = 8
WLON = 12
WLAT = 6
WLEV = 2
LWIN = LEV // WLEV
WH = LWIN * HEADS
WIN = WLEV * WLAT * WLON
TOK = LWIN * WIN
QUAD = TOK // 4
SITE = WLEV * WLAT
SHIFTS = 2 * WLON - 1
STRIP = SHIFTS * SITE
POS = WLEV * WLEV * WLAT * WLAT * SHIFTS
RUN = WLAT * SHIFTS
LANES = 384
STACK = HEADS * WIN
EPSILON = 1e-05
MASKED = -1000000000.0
LOG2E = math.log2(math.e)
SCALE = 1.0 / math.sqrt(C // HEADS)
RING = 4
E_TILES = 144
L_TILES = 72
B_TILES = 40
B_LEFT = STRIP - 256
B_ROWS = 48
CHUNK = QUAD // 2
PAIR = 4 * CHUNK
PACKED = 112
TILE = (16, 128)
BF16 = jnp.bfloat16
F32 = jnp.float32
MESH = pl.DeviceIdType.MESH
VMEM_LIMIT = 30 * 1024 * 1024


def token_places():
    w, o, lev, a = np.meshgrid(
        np.arange(2), np.arange(WLON), np.arange(WLEV), np.arange(WLAT), indexing="ij"
    )
    site = (o % 6) * 3 + a % 3
    row = (site % 9) * 8 + (site // 9) * 4 + 2 * w + lev
    return (((o // 6) * 2 + a // 3) * CHUNK + row).reshape(PAIR).astype(np.int32)


def lane_places():
    lev, a, d = np.meshgrid(np.arange(WLEV), np.arange(WLAT), np.arange(SHIFTS), indexing="ij")
    return ((SHIFTS - 1 - d) * SITE + lev * WLAT + a).reshape(STRIP).astype(np.int32)


def row_places():
    wh, _, site = np.meshgrid(np.arange(WH), np.arange(2), np.arange(SITE), indexing="ij")
    return (site * WH + wh).reshape(WH * 2 * SITE).astype(np.int32)


def row_codes():
    _, w, p, lev, a = np.meshgrid(
        np.arange(HEADS), np.arange(LWIN), np.arange(2), np.arange(WLEV), np.arange(WLAT), indexing="ij"
    )
    code = lev + 2 * (a >= WLAT // 2) + 4 * (w == LWIN - 1) + 8 * (p == 0)
    return code.reshape(WH * 2 * SITE).astype(np.int32)


def lane_codes():
    site = np.arange(LANES) % SITE
    return (site // WLAT + 2 * (site % WLAT >= WLAT // 2)).astype(np.int32)


def columns_of(*arrays):
    made = np.zeros((TOK, 8), np.int32)
    for i, array in enumerate(arrays):
        made[: len(array), i] = array
    return made


def dot(a, b):
    return jnp.dot(a, b, preferred_element_type=F32)


def dot_nt(a, b):
    return lax.dot_general(a, b, (((1,), (1,)), ((), ())), preferred_element_type=F32)


def dot_tn(a, b):
    return lax.dot_general(a, b, (((0,), (0,)), ((), ())), preferred_element_type=F32)


def one_hot(places, rows, cols):
    along = 1 if places.shape[1] == 1 else 0
    index = lax.broadcasted_iota(jnp.int32, (rows, cols), along)
    return jnp.where(index == places, 1.0, 0.0).astype(BF16)


def pieces(value, count):
    found = []
    for _ in range(count):
        part = value.astype(BF16)
        found.append(part)
        value = value - part.astype(F32)
    return found


def split(ref, index):
    part = ref[pl.ds((index // 2) * 6, 6), pl.ds((index % 2) * 3, 3)]
    part = pltpu.roll(part.astype(F32).reshape(18, LEV, C), LEV - 1, 1)
    low, high = part[:9], part[9:]
    upper = lax.broadcasted_iota(jnp.int32, low.shape, 1) < LEV // 2
    first = jnp.where(upper, low, pltpu.roll(high, LEV // 2, 1))
    second = jnp.where(upper, pltpu.roll(low, LEV // 2, 1), high)
    return first.reshape(CHUNK, C), second.reshape(CHUNK, C)


def merge(ref, index, chunks):
    first, second = (chunk.reshape(9, LEV, C) for chunk in chunks)
    upper = lax.broadcasted_iota(jnp.int32, first.shape, 1) < LEV // 2
    low = jnp.where(upper, first, pltpu.roll(second, LEV // 2, 1))
    high = jnp.where(upper, pltpu.roll(first, LEV // 2, 1), second)
    part = pltpu.roll(jnp.concatenate([low, high], axis=0), 1, 1)
    ref[pl.ds((index // 2) * 6, 6), pl.ds((index % 2) * 3, 3)] = part.reshape(6, 3, LEV, C).astype(BF16)


def pack(value):
    rest = jnp.concatenate([value[:40, 128:], value[32:, 128:]], axis=1)
    return jnp.concatenate([value[:, :128], rest], axis=0).astype(BF16)


def unpack(value):
    wide = value.astype(F32)
    rest = wide[CHUNK:]
    right = jnp.concatenate([rest[:, :64], rest[8:, 64:]], axis=0)
    return jnp.concatenate([wide[:CHUNK], right], axis=1)


def place_of(lon, lat):
    x = lax.rem(lat, 2) * 2 + lax.div(lon, 8)
    return (x, lax.rem(lax.div(lon, 2), RING), lax.div(lat, 2)), lax.rem(lon, 2)


def device_at(chip, core):
    x, y, z = chip
    return ((lax.rem(x, 2) * RING + y) * 2 + core, z * 2 + lax.div(x, 2))


def moved(chip, axis, step):
    return tuple(lax.rem(c + step, RING) if i == axis else c for i, c in enumerate(chip))


def remote(src, dst, send, recv, device):
    return pltpu.make_async_remote_copy(
        src_ref=src, dst_ref=dst, send_sem=send, recv_sem=recv, device_id=device, device_id_type=MESH
    )


class Here:
    def __init__(self, n_lon, n_lat):
        self.lon, self.lat = lax.axis_index("lon"), lax.axis_index("lat")
        self.chip, self.core = place_of(self.lon, self.lat)
        self.sibling = (self.lon + 1 - 2 * self.core, self.lat)
        self.slot = [[lax.rem(c + k, RING) for k in range(RING)] for c in self.chip]
        chips = [[moved(self.chip, axis, k) for k in range(RING)] for axis in range(3)]
        self.along = [[device_at(chip, self.core) for chip in ring] for ring in chips]
        other = 1 - self.core
        self.eight = []
        for axis in range(3):
            found = []
            for k in range(RING):
                if k:
                    found.append((self.along[axis][k], self.slot[axis][k], self.core))
                found.append((device_at(chips[axis][k], other), self.slot[axis][k], other))
            self.eight.append(found)
        self.facing = (lax.rem(self.lon + 8, 16), self.lat)
        self.across = {}
        for step in (-1, 1):
            to_lon = lax.rem(self.lon + n_lon + step, n_lon)
            to_lat = lax.rem(self.lat + n_lat + step, n_lat)
            self.across[step] = ((to_lon, to_lat), (to_lon, self.lat), (self.lon, to_lat))

    def greet(self):
        others = [*self.across[-1], *self.across[1], self.sibling]
        for axis in range(3):
            others += [device for device, _, _ in self.eight[axis][1:]]
        barrier = pltpu.get_barrier_semaphore()
        for device in others:
            pl.semaphore_signal(barrier, inc=1, device_id=device, device_id_type=MESH)
        return lambda: pl.semaphore_wait(barrier, len(others))


def halo(here, source, target, send, recv, step):
    copies = []
    for index in range(3):
        src = index if step < 0 else 3 - index
        device = here.across[step][index]
        copies.append(remote(source.at[src], target.at[3 - src], send.at[index], recv.at[index], device))
    return copies


def begin(copies):
    for copy in copies:
        copy.start()


def end(copies):
    for copy in copies:
        copy.wait()


def wait_bytes(like, sem):
    pltpu.make_async_copy(like, like, sem).wait()


def room(*dims):
    return pltpu.VMEM((*dims, *TILE), BF16)


def tiles_in(block):
    narrow = block.astype(BF16)
    for c in range(block.shape[1] // 128):
        for r in range(block.shape[0] // 16):
            yield narrow[r * 16 : (r + 1) * 16, c * 128 : (c + 1) * 128]


def added(terms):
    total = terms[0].astype(F32)
    for term in terms[1:]:
        total = total + term.astype(F32)
    return total.astype(BF16)


class WeightSum:
    def __init__(self, here, out, refs):
        self.here, self.out = here, out
        self.src, self.r1, self.x2, self.x3, self.send, self.recv = refs

    @staticmethod
    def scratch(tiles):
        n1 = tiles // 24
        dma = pltpu.SemaphoreType.DMA
        return [room(3, RING, 2, n1), room(7, 3, n1), room(3, RING, n1), room(3, RING, n1), dma((4,)), dma((4,))]

    def put(self, block, first):
        n1 = self.src.shape[3]
        for at, tile in enumerate(tiles_in(block), first):
            self.src[at // (8 * n1), at // (2 * n1) % RING, at // n1 % 2, at % n1] = tile

    def phase(self, at):
        here, made = self.here, []
        sems = self.send.at[at], self.recv.at[at]
        for t in range(3):
            if at in (0, 3):
                mine = self.out.at[t, here.slot[t][0], here.core]
                for k, (device, slot, core) in enumerate(here.eight[t]):
                    if at == 0:
                        made.append(remote(self.src.at[t, slot, core], self.r1.at[k, t], *sems, device))
                    else:
                        made.append(remote(mine, mine, *sems, device))
            else:
                axis = (t + at) % 3
                mine = (self.x2 if at == 1 else self.x3).at[t, here.slot[axis][0]]
                made += [remote(mine, mine, *sems, here.along[axis][k]) for k in range(1, RING)]
        return made

    def start(self):
        begin(self.phase(0))

    def step(self, at):
        like = self.r1 if at in (0, 3) else self.r1.at[pl.ds(0, 3)]
        wait_bytes(like, self.recv.at[at])
        wait_bytes(like, self.send.at[at])
        core = self.here.core
        for t in range(3):
            one, two, three = (self.here.slot[(t + i) % 3][0] for i in range(3))
            if at == 0:
                self.x2[t, two] = added([self.src[t, one, core]] + [self.r1[k, t] for k in range(7)])
            if at == 1:
                self.x3[t, three] = added([self.x2[t, k] for k in range(RING)])
            if at == 2:
                self.out[t, one, core] = added([self.x3[t, k] for k in range(RING)])
        if at < 3:
            begin(self.phase(at + 1))


class PairSum:
    def __init__(self, here, out, refs):
        self.here, self.out = here, out
        self.src, self.other, self.a1, self.r1, self.x2, self.x3, self.send, self.recv = refs

    @staticmethod
    def scratch(tiles):
        n1 = tiles // 24
        dma = pltpu.SemaphoreType.DMA
        return [
            room(2, tiles // 2), room(tiles // 2),
            room(3, RING, n1), room(3, RING - 1, n1), room(3, RING, n1), room(3, RING, n1),
            dma((6,)), dma((6,)),
        ]

    def put(self, block, first):
        each = self.src.shape[1]
        for at, tile in enumerate(tiles_in(block), first):
            self.src[at // each, at % each] = tile

    def get(self):
        n1 = self.a1.shape[2]
        return [self.out[i // (12 * n1), i // (4 * n1) % 3, i // n1 % 4, i % n1] for i in range(24 * n1)]

    def copies(self, at, axis_of, source, target):
        made = []
        for t in range(3):
            axis = (t + axis_of) % 3
            slot = self.here.slot[axis]
            for k in range(1, RING):
                made.append(
                    remote(
                        source(t, slot[k], slot[0]), target(t, k - 1, slot[0]),
                        self.send.at[at], self.recv.at[at], self.here.along[axis][k],
                    )
                )
        return made

    def phase(self, at):
        core = self.here.core
        if at == 0:
            return [remote(self.src.at[1 - core], self.other, self.send.at[0], self.recv.at[0], self.here.sibling)]
        if at == 1:
            return self.copies(1, 0, lambda t, to, me: self.a1.at[t, to], lambda t, k, me: self.r1.at[t, k])
        if at == 2:
            return self.copies(2, 1, lambda t, to, me: self.x2.at[t, me], lambda t, k, me: self.x2.at[t, me])
        if at == 3:
            return self.copies(3, 2, lambda t, to, me: self.x3.at[t, me], lambda t, k, me: self.x3.at[t, me])
        if at == 4:
            out = self.out.at[core]
            return self.copies(4, 0, lambda t, to, me: out.at[t, me], lambda t, k, me: out.at[t, me])
        return [remote(self.out.at[core], self.out.at[core], self.send.at[5], self.recv.at[5], self.here.sibling)]

    def start(self):
        begin(self.phase(0))

    def step(self, at):
        like = self.other if at in (0, 5) else self.r1
        wait_bytes(like, self.recv.at[at])
        wait_bytes(like, self.send.at[at])
        core = self.here.core
        if at == 0:
            total = self.src[core].astype(F32) + self.other[...].astype(F32)
            self.a1[...] = total.astype(BF16).reshape(self.a1.shape)
        for t in range(3):
            one, two, three = (self.here.slot[(t + i) % 3][0] for i in range(3))
            if at == 1:
                total = self.a1[t, one].astype(F32)
                for k in range(RING - 1):
                    total = total + self.r1[t, k].astype(F32)
                self.x2[t, two] = total.astype(BF16)
            if at in (2, 3):
                came = self.x2 if at == 2 else self.x3
                total = came[t, 0].astype(F32)
                for k in range(1, RING):
                    total = total + came[t, k].astype(F32)
                if at == 2:
                    self.x3[t, three] = total.astype(BF16)
                else:
                    self.out[core, t, one] = total.astype(BF16)
        if at < 5:
            begin(self.phase(at + 1))


class BiasSum:
    def __init__(self, here, out, refs):
        self.here, self.out = here, out
        self.src, self.r1, self.x2, self.send, self.recv = refs

    @staticmethod
    def scratch():
        each = B_TILES // 8
        dma = pltpu.SemaphoreType.DMA
        return [room(RING, 2, each), room(7, each), room(2, each), dma((3,)), dma((3,))]

    def put(self, block):
        each = B_TILES // 8
        last = block[:, 256:]
        shared = last[0:B_ROWS]
        for g in range(1, 288 // B_ROWS):
            shared = shared + pltpu.roll(last[g * B_ROWS : (g + 1) * B_ROWS], g * B_LEFT, 1)
        tiles = [*tiles_in(block[:, :256]), *tiles_in(shared), jnp.zeros(TILE, BF16)]
        for at, tile in enumerate(tiles):
            self.src[at // (2 * each), at // each % 2, at % each] = tile

    def get(self):
        each = B_TILES // 8
        tiles = [self.out[at // (2 * each), at // each % 2, at % each] for at in range(B_TILES)]
        first = joined(tiles[:36], 2)
        shared = joined(tiles[36:39], 1)
        last = [shared]
        for g in range(1, 288 // B_ROWS):
            last.append(pltpu.roll(shared, 128 - g * B_LEFT, 1))
        return jnp.concatenate([first, jnp.concatenate(last, axis=0)], axis=1)

    def phase(self, at):
        here, made = self.here, []
        sems = self.send.at[at], self.recv.at[at]
        if at == 1:
            return [remote(self.x2.at[0], self.x2.at[1], *sems, here.facing)]
        mine = self.out.at[here.slot[1][0], here.core]
        for k, (device, slot, core) in enumerate(here.eight[1]):
            if at == 0:
                made.append(remote(self.src.at[slot, core], self.r1.at[k], *sems, device))
            else:
                made.append(remote(mine, mine, *sems, device))
        return made

    def start(self):
        begin(self.phase(0))

    def step(self, at):
        like = self.x2.at[1] if at == 1 else self.r1
        wait_bytes(like, self.recv.at[at])
        wait_bytes(like, self.send.at[at])
        slot, core = self.here.slot[1][0], self.here.core
        if at == 0:
            self.x2[0] = added([self.src[slot, core]] + [self.r1[k] for k in range(7)])
        if at == 1:
            self.out[slot, core] = added([self.x2[0], self.x2[1]])
        if at < 2:
            begin(self.phase(at + 1))


def layer_norm(x):
    centered = x - jnp.mean(x, axis=-1, keepdims=True)
    spread = jnp.mean(centered * centered, axis=-1, keepdims=True)
    rate = lax.rsqrt(spread + EPSILON)
    return centered * rate, rate


def layer_norm_back(cot, unit, rate):
    first = jnp.mean(cot, axis=-1, keepdims=True)
    second = jnp.mean(cot * unit, axis=-1, keepdims=True)
    return rate * (cot - first - unit * second)


def head_mask(head):
    lane = lax.broadcasted_iota(jnp.int32, (1, C), 1)
    return (lane >= head * 32) & (lane < head * 32 + 32)


def stacked(value):
    wide = value.astype(F32)
    parts = [jnp.where(head_mask(h), wide, 0.0).astype(BF16) for h in range(HEADS)]
    return jnp.concatenate(parts, axis=0)


def unstacked(value):
    total = jnp.where(head_mask(0), value[0:WIN], 0.0)
    for h in range(1, HEADS):
        total = total + jnp.where(head_mask(h), value[h * WIN : (h + 1) * WIN], 0.0)
    return total


def expand_bias(last_lat, table, columns, index_rows, lanes, tall_table, gathered, strips, scores):
    for head in range(HEADS):
        tall_table[head * LWIN : (head + 1) * LWIN, :] = table[head]
    for site in range(SITE):
        lev, a = site // WLAT, site % WLAT
        for other in range(WLEV):
            start = ((lev * WLEV + other) * WLAT + a) * RUN
            gathered[site * WH : (site + 1) * WH, other * RUN : (other + 1) * RUN] = tall_table[
                :, start : start + RUN
            ]
    moved = sum(dot(part, lanes[...]) for part in pieces(gathered[...], 3))
    rows = one_hot(columns[:, 1:2], WH * 2 * SITE, SITE * WH)
    moved = sum(dot(rows, part) for part in pieces(moved, 3))
    code = columns[:, 2:3]
    moved = jnp.where((code & 8) != 0, pltpu.roll(moved, LANES - SITE, 1), moved) * LOG2E
    seen = jnp.where((code & 4) != 0, 1, 0) + jnp.where(last_lat, 2, 0)
    apart = (code ^ index_rows[2:3, 0:LANES]) & seen
    strips[...] = jnp.where(apart != 0, MASKED, moved)

    def one(wh, carry):
        strip = strips[pl.ds(pl.multiple_of(wh * 2 * SITE, 8), 2 * SITE), :]
        start = lax.rem(wh, LWIN) * STACK + lax.div(wh, LWIN) * WIN
        for pair in range(WLON // 2):
            offset = (WLON - 2 - 2 * pair) * SITE
            scores[pl.ds(pl.multiple_of(start + pair * 24, 8), 24), :] = strip[
                :, offset : offset + WIN
            ]
        return carry

    lax.fori_loop(0, WH, one, 0)


def collapse_bias(first, last, scores, strips):
    def one(wh, carry):
        start = lax.rem(wh, LWIN) * STACK + lax.div(wh, LWIN) * WIN
        total = jnp.zeros((2 * SITE, LANES), F32)
        for pair in range(WLON // 2):
            offset = (WLON - 2 - 2 * pair) * SITE
            part = scores[pl.ds(pl.multiple_of(start + pair * 24, 8), 24), :]
            part = jnp.concatenate([part, jnp.zeros((2 * SITE, LANES - WIN), F32)], axis=1)
            total = total + (pltpu.roll(part, offset, 1) if offset else part)
        strips[pl.ds(pl.multiple_of(wh * 2 * SITE, 8), 2 * SITE), :] = total
        return carry

    lax.fori_loop(first, last, one, 0)


def join_strips(strips, columns, index_rows):
    total = strips[...]
    total = jnp.where((columns[:, 2:3] & 8) != 0, pltpu.roll(total, SITE, 1), total)
    rows = one_hot(index_rows[1:2, :], SITE * WH, WH * 2 * SITE)
    return sum(dot(rows, part) for part in pieces(total, 2))


def block_kernel(n_lon, n_lat, *refs):
    loaded = refs[:9]
    out_field, grad_field, qkv, proj, fc1, fc2, bias = refs[9:16]
    field, cot, w_qkv, w_proj, w_fc1, w_fc2, table, columns, index_rows, load_sem = refs[16:26]
    (
        out, e_out, l_out, b_out, sent, came, cot_sent, cot_came, back, halo_send, halo_recv,
        xw, uw, scores, normed, query, key, value, unit, rate, blended, normed_two, hidden,
        cot_first, cot_mid, cot_q, cot_k, cot_v, ow, gw, tall_table, gathered, strips, w3,
        places_in, places_out, lanes,
    ) = refs[26:63]
    here = Here(n_lon, n_lat)
    early = PairSum(here, e_out, refs[63:71])
    late = WeightSum(here, l_out, refs[71:77])
    strip_sum = BiasSum(here, b_out, refs[77:82])

    loads = [
        pltpu.make_async_copy(src, dst, load_sem.at[i]) for i, (src, dst) in enumerate(zip(loaded, refs[16:25]))
    ]
    loads[0].start()
    greeted = here.greet()
    begin(loads[6:9])
    loads[0].wait()
    for index in range(3):
        for part, chunk in enumerate(split(field, index)):
            sent[part, index] = pack(chunk)
    greeted()
    inward = [
        halo(here, sent.at[i], came.at[i], halo_send.at[i], halo_recv.at[i], -1) for i in range(2)
    ]
    cot_inward = halo(here, cot_sent, cot_came, halo_send.at[2], halo_recv.at[2], -1)
    outward = [
        halo(here, back.at[i], out.at[i], halo_send.at[3 + i], halo_recv.at[3 + i], 1) for i in range(2)
    ]
    begin(inward[0])
    begin(inward[1])
    begin(loads[1:6])
    end(loads[6:9])
    lanes[...] = one_hot(columns[0:STRIP, 3:4], STRIP, LANES)
    last_lat = here.lat == n_lat - 1
    expand_bias(last_lat, table, columns, index_rows, lanes, tall_table, gathered, strips, scores)
    places_in[...] = one_hot(columns[0:PAIR, 0:1], PAIR, PAIR)
    places_out[...] = one_hot(index_rows[0:1, 0:PAIR], PAIR, PAIR)
    loads[1].wait()
    for index in range(3):
        for part, chunk in enumerate(split(cot, index)):
            cot_sent[index, part] = pack(chunk)
    own = [split(ref, 3) for ref in (field, cot)]
    loads[2].wait()
    for third in range(3):
        w3[third] = w_qkv[:, third * C : (third + 1) * C]

    def gather(kind, part):
        if kind:
            arrived = [cot_came[i, part] for i in range(1, 4)]
        else:
            arrived = [came[part, i] for i in range(1, 4)]
        parts = [own[kind][part]] + [unpack(value) for value in arrived]
        return dot(places_in[...], jnp.concatenate(parts, axis=0).astype(BF16)).astype(BF16)

    def scatter(kind, ref):
        for part in range(2):
            whole = dot(places_out[...], ref[part * PAIR : (part + 1) * PAIR, :])
            out[kind, 3, part] = pack(whole[:CHUNK])
            for i in range(1, 4):
                back[kind, i, part] = pack(whole[i * CHUNK : (i + 1) * CHUNK])
        begin(outward[kind])

    def places(w):
        return pl.ds(w * WIN, WIN), pl.ds(w * STACK, STACK)

    def attend(w):
        rows, tall = places(w)
        unit_x, rate_x = layer_norm(xw[rows, :].astype(F32))
        unit[rows, :] = unit_x
        rate[rows, :] = rate_x
        norm = unit_x.astype(BF16)
        normed[rows, :] = norm
        q = dot(norm, w3[0]).astype(BF16)
        k = dot(norm, w3[1]).astype(BF16)
        v = dot(norm, w3[2]).astype(BF16)
        query[rows, :] = q
        key[rows, :] = k
        value[rows, :] = v
        s = dot_nt(stacked(q), k) * (SCALE * LOG2E) + scores[tall, :]
        e = jnp.exp2(s - jnp.max(s, axis=-1, keepdims=True))
        p = e * (1.0 / jnp.sum(e, axis=-1, keepdims=True))
        scores[tall, :] = p
        blended[rows, :] = unstacked(dot(p.astype(BF16), v)).astype(BF16)

    def feed(w):
        rows = pl.ds(w * 2 * WIN, 2 * WIN)
        middle = xw[rows, :].astype(F32) + dot(blended[rows, :], w_proj[...])
        middle = middle.astype(BF16).astype(F32)
        unit_m, rate_m = layer_norm(middle)
        norm_m = unit_m.astype(BF16)
        normed_two[rows, :] = norm_m
        first = dot(norm_m, w_fc1[...])
        phi = 0.5 + 0.5 * lax.erf(first * math.sqrt(0.5))
        hid = (first * phi).astype(BF16)
        hidden[rows, :] = hid
        bell = jnp.exp2(first * first * (-0.5 * LOG2E)) * (1.0 / math.sqrt(2.0 * math.pi))
        slope = phi + first * bell
        ow[rows, :] = (middle + dot_nt(hid, w_fc2[...])).astype(BF16)
        up = uw[rows, :]
        c_first = (dot(up, w_fc2[...]).astype(BF16).astype(F32) * slope).astype(BF16)
        cot_first[rows, :] = c_first
        c_norm = dot_nt(c_first, w_fc1[...]).astype(BF16).astype(F32)
        c_mid = layer_norm_back(c_norm, unit_m, rate_m).astype(BF16).astype(F32)
        cot_mid[rows, :] = (up.astype(F32) + c_mid).astype(BF16)

    def backward(w):
        rows, tall = places(w)
        up = cot_mid[rows, :]
        c_blend = stacked(dot_nt(up, w_proj[...]).astype(BF16))
        p = scores[tall, :]
        c_p = dot_nt(c_blend, value[rows, :])
        c_s = p * (c_p - jnp.sum(p * c_p, axis=-1, keepdims=True))
        scores[tall, :] = c_s
        c_v = dot_tn(p.astype(BF16), c_blend).astype(BF16)
        narrow = c_s.astype(BF16)
        c_q = (unstacked(dot(narrow, key[rows, :])) * SCALE).astype(BF16)
        c_k = (dot_tn(narrow, stacked(query[rows, :])) * SCALE).astype(BF16)
        cot_q[rows, :] = c_q
        cot_k[rows, :] = c_k
        cot_v[rows, :] = c_v

    def inputs_back(w):
        rows = pl.ds(w * 2 * WIN, 2 * WIN)
        c_norm = dot_nt(cot_q[rows, :], w3[0]) + dot_nt(cot_k[rows, :], w3[1])
        c_norm = (c_norm + dot_nt(cot_v[rows, :], w3[2])).astype(BF16).astype(F32)
        c_x = layer_norm_back(c_norm, unit[rows, :], rate[rows, :]).astype(BF16)
        gw[rows, :] = (cot_mid[rows, :].astype(F32) + c_x.astype(F32)).astype(BF16)

    for part in range(2):
        end(inward[part])
        xw[part * PAIR : (part + 1) * PAIR, :] = gather(0, part)
        if part:
            begin(cot_inward)
        attend(2 * part)
        attend(2 * part + 1)
    end(loads[3:6])
    end(cot_inward)
    for part in range(2):
        uw[part * PAIR : (part + 1) * PAIR, :] = gather(1, part)
    feed(0)
    feed(1)
    early.put(dot_tn(normed_two[...], cot_first[...]), 0)
    early.put(dot_tn(uw[...], hidden[...]), 72)
    early.start()
    scatter(0, ow)
    backward(0)
    backward(1)
    early.step(0)
    backward(2)
    backward(3)
    early.step(1)
    norm = normed[...]
    late.put(jnp.concatenate([dot_tn(norm, cot_q[...]), dot_tn(norm, cot_k[...])], axis=1), 0)
    c_proj = dot_tn(blended[...], cot_mid[...])
    late.put(jnp.concatenate([dot_tn(norm, cot_v[...]), c_proj], axis=1), 36)
    late.start()
    collapse_bias(0, WH, scores, strips)
    strip_sum.put(join_strips(strips, columns, index_rows))
    strip_sum.start()
    early.step(2)
    inputs_back(0)
    inputs_back(1)
    late.step(0)
    scatter(1, gw)
    early.step(3)
    strip_sum.step(0)
    late.step(1)
    early.step(4)
    strip_sum.step(1)
    end(outward[0])
    for index in range(4):
        merge(out_field, index, [unpack(out[0, index, part]) for part in range(2)])
    late.step(2)
    early.step(5)
    fc1[...] = joined(early.get()[:72], 6)
    fc2[...] = joined(early.get()[72:], 6)
    strip_sum.step(2)
    finish_bias(strip_sum.get(), lanes, tall_table, bias)
    end(outward[1])
    for index in range(4):
        merge(grad_field, index, [unpack(out[1, index, part]) for part in range(2)])
    late.step(3)
    qkv[:, 0:384] = joined(tiles_of(l_out)[:36], 3)
    right = joined(tiles_of(l_out)[36:], 3)
    qkv[:, 384:576] = right[:, 0:C]
    proj[...] = right[:, C:]


def joined(tiles, columns):
    rows = len(tiles) // columns
    cols = [jnp.concatenate(tiles[c * rows : (c + 1) * rows], axis=0) for c in range(columns)]
    return jnp.concatenate(cols, axis=1).astype(F32)


def tiles_of(ref):
    n1 = ref.shape[3]
    return [ref[i // (8 * n1), i // (2 * n1) % RING, i // n1 % 2, i % n1] for i in range(24 * n1)]


def finish_bias(strip, lanes, tall_table, bias):
    runs = dot_nt(strip.astype(BF16), lanes[...])
    for site in range(SITE):
        lev, a = site // WLAT, site % WLAT
        for other in range(WLEV):
            start = ((lev * WLEV + other) * WLAT + a) * RUN
            tall_table[:, start : start + RUN] = runs[
                site * WH : (site + 1) * WH, other * RUN : (other + 1) * RUN
            ]
    for head in range(HEADS):
        bias[head] = tall_table[head * LWIN : (head + 1) * LWIN, :]


def finish_kernel(*refs):
    count = len(refs) // 2
    copies = [pltpu.make_async_copy(refs[i], refs[count + i], refs[-1].at[i]) for i in range(count)]
    begin(copies)
    end(copies)


def per_device(n_lon, n_lat, field, w_qkv, w_proj, w_fc1, w_fc2, bias_table, cotangent):
    vmem, hbm = pl.BlockSpec(memory_space=pltpu.VMEM), pl.BlockSpec(memory_space=pltpu.HBM)
    shape = jax.ShapeDtypeStruct
    dma = pltpu.SemaphoreType.DMA
    rows = row_places()
    columns = columns_of(token_places(), rows, row_codes(), lane_places())
    index_rows = columns_of(token_places(), rows, lane_codes()).T.copy()
    inputs = (
        field, cotangent, w_qkv, w_proj, w_fc1, w_fc2.T, bias_table[0].transpose(1, 0, 2), columns, index_rows
    )
    inputs = [pltpu.with_memory_space_constraint(jnp.asarray(a), pltpu.HBM) for a in inputs]
    tile = shape((WLON, WLAT, LEV, C), BF16)
    outputs = (
        tile,
        tile,
        shape((C, 3 * C), F32),
        shape((C, C), F32),
        shape((C, HIDDEN), F32),
        shape((C, HIDDEN), F32),
        shape((HEADS, LWIN, POS), F32),
    )
    wide = lambda dtype, n=1: [pltpu.VMEM((TOK, C), dtype)] * n
    results = pl.pallas_call(
        functools.partial(block_kernel, n_lon, n_lat),
        out_shape=outputs,
        in_specs=[hbm] * len(inputs),
        out_specs=[vmem] * len(outputs),
        scratch_shapes=[
            *[pltpu.VMEM(a.shape, a.dtype) for a in inputs],
            dma((len(inputs),)),
            pltpu.VMEM((2, 4, 2, PACKED, 128), BF16),
            room(2, 3, RING, E_TILES // 24),
            room(3, RING, 2, L_TILES // 24),
            room(RING, 2, B_TILES // 8),
            pltpu.VMEM((2, 3, PACKED, 128), BF16),
            pltpu.VMEM((2, 4, PACKED, 128), BF16),
            pltpu.VMEM((3, 2, PACKED, 128), BF16),
            pltpu.VMEM((4, 2, PACKED, 128), BF16),
            pltpu.VMEM((2, 4, 2, PACKED, 128), BF16),
            dma((5, 3)),
            dma((5, 3)),
            *wide(BF16, 2),
            pltpu.VMEM((LWIN * STACK, WIN), F32),
            *wide(BF16, 4),
            *wide(F32),
            pltpu.VMEM((TOK, 1), F32),
            *wide(BF16, 2),
            pltpu.VMEM((TOK, HIDDEN), BF16),
            pltpu.VMEM((TOK, HIDDEN), BF16),
            *wide(BF16, 6),
            pltpu.VMEM((WH, POS), F32),
            pltpu.VMEM((SITE * WH, STRIP), F32),
            pltpu.VMEM((WH * 2 * SITE, LANES), F32),
            pltpu.VMEM((3, C, C), BF16),
            pltpu.VMEM((PAIR, PAIR), BF16),
            pltpu.VMEM((PAIR, PAIR), BF16),
            pltpu.VMEM((STRIP, LANES), BF16),
            *PairSum.scratch(E_TILES),
            *WeightSum.scratch(L_TILES),
            *BiasSum.scratch(),
        ],
        compiler_params=pltpu.CompilerParams(
            vmem_limit_bytes=VMEM_LIMIT, collective_id=0, has_side_effects=True
        ),
        name="block",
    )(*inputs)
    *results, fc2, bias = pl.pallas_call(
        finish_kernel,
        out_shape=outputs,
        in_specs=[vmem] * len(outputs),
        out_specs=[hbm] * len(outputs),
        scratch_shapes=[dma((len(outputs),))],
        compiler_params=pltpu.CompilerParams(vmem_limit_bytes=VMEM_LIMIT),
        name="finish",
    )(*results)
    return (*results, fc2.T, bias.transpose(1, 0, 2)[None])


def solution(mesh):
    whole, tiles, banded = P(), P("lon", "lat", None, None), P("lat", None, None, None)
    return jax.shard_map(
        functools.partial(per_device, mesh.shape["lon"], mesh.shape["lat"]),
        mesh=mesh,
        in_specs=(tiles, whole, whole, whole, whole, banded, tiles),
        out_specs=(tiles, tiles, whole, whole, whole, whole, banded),
        check_vma=False,
    )
```

```python
import functools
import math

import jax
import jax.numpy as jnp
import numpy as np
from jax import lax
from jax.experimental import pallas as pl
from jax.experimental.pallas import tpu as pltpu
from jax.sharding import PartitionSpec as P

C = 192
HEADS = 6
HIDDEN = 768
LEV = 8
WLON = 12
WLAT = 6
WLEV = 2
LWIN = LEV // WLEV
WH = LWIN * HEADS
WIN = WLEV * WLAT * WLON
TOK = LWIN * WIN
QUAD = TOK // 4
SITE = WLEV * WLAT
SHIFTS = 2 * WLON - 1
STRIP = SHIFTS * SITE
POS = WLEV * WLEV * WLAT * WLAT * SHIFTS
RUN = WLAT * SHIFTS
LANES = 384
STACK = HEADS * WIN
EPSILON = 1e-05
MASKED = -1000000000.0
LOG2E = math.log2(math.e)
SCALE = 1.0 / math.sqrt(C // HEADS)
RING = 4
E_TILES = 144
L_TILES = 72
B_TILES = 40
B_LEFT = STRIP - 256
B_ROWS = 48
CHUNK = QUAD // 2
PAIR = 4 * CHUNK
PACKED = 112
TILE = (16, 128)
BF16 = jnp.bfloat16
F32 = jnp.float32
MESH = pl.DeviceIdType.MESH
VMEM_LIMIT = 30 * 1024 * 1024


def token_places():
    w, o, lev, a = np.meshgrid(
        np.arange(2), np.arange(WLON), np.arange(WLEV), np.arange(WLAT), indexing="ij"
    )
    site = (o % 6) * 3 + a % 3
    row = (site % 9) * 8 + (site // 9) * 4 + 2 * w + lev
    return (((o // 6) * 2 + a // 3) * CHUNK + row).reshape(PAIR).astype(np.int32)


def lane_places():
    lev, a, d = np.meshgrid(np.arange(WLEV), np.arange(WLAT), np.arange(SHIFTS), indexing="ij")
    return ((SHIFTS - 1 - d) * SITE + lev * WLAT + a).reshape(STRIP).astype(np.int32)


def row_places():
    wh, _, site = np.meshgrid(np.arange(WH), np.arange(2), np.arange(SITE), indexing="ij")
    return (site * WH + wh).reshape(WH * 2 * SITE).astype(np.int32)


def row_codes():
    _, w, p, lev, a = np.meshgrid(
        np.arange(HEADS), np.arange(LWIN), np.arange(2), np.arange(WLEV), np.arange(WLAT), indexing="ij"
    )
    code = lev + 2 * (a >= WLAT // 2) + 4 * (w == LWIN - 1) + 8 * (p == 0)
    return code.reshape(WH * 2 * SITE).astype(np.int32)


def lane_codes():
    site = np.arange(LANES) % SITE
    return (site // WLAT + 2 * (site % WLAT >= WLAT // 2)).astype(np.int32)


def columns_of(*arrays):
    made = np.zeros((TOK, 8), np.int32)
    for i, array in enumerate(arrays):
        made[: len(array), i] = array
    return made


def dot(a, b):
    return jnp.dot(a, b, preferred_element_type=F32)


def dot_nt(a, b):
    return lax.dot_general(a, b, (((1,), (1,)), ((), ())), preferred_element_type=F32)


def dot_tn(a, b):
    return lax.dot_general(a, b, (((0,), (0,)), ((), ())), preferred_element_type=F32)


def one_hot(places, rows, cols):
    along = 1 if places.shape[1] == 1 else 0
    index = lax.broadcasted_iota(jnp.int32, (rows, cols), along)
    return jnp.where(index == places, 1.0, 0.0).astype(BF16)


def pieces(value, count):
    found = []
    for _ in range(count):
        part = value.astype(BF16)
        found.append(part)
        value = value - part.astype(F32)
    return found


def split(ref, index):
    part = ref[pl.ds((index // 2) * 6, 6), pl.ds((index % 2) * 3, 3)]
    part = pltpu.roll(part.astype(F32).reshape(18, LEV, C), LEV - 1, 1)
    low, high = part[:9], part[9:]
    upper = lax.broadcasted_iota(jnp.int32, low.shape, 1) < LEV // 2
    first = jnp.where(upper, low, pltpu.roll(high, LEV // 2, 1))
    second = jnp.where(upper, pltpu.roll(low, LEV // 2, 1), high)
    return first.reshape(CHUNK, C), second.reshape(CHUNK, C)


def merge(ref, index, chunks):
    first, second = (chunk.reshape(9, LEV, C) for chunk in chunks)
    upper = lax.broadcasted_iota(jnp.int32, first.shape, 1) < LEV // 2
    low = jnp.where(upper, first, pltpu.roll(second, LEV // 2, 1))
    high = jnp.where(upper, pltpu.roll(first, LEV // 2, 1), second)
    part = pltpu.roll(jnp.concatenate([low, high], axis=0), 1, 1)
    ref[pl.ds((index // 2) * 6, 6), pl.ds((index % 2) * 3, 3)] = part.reshape(6, 3, LEV, C).astype(BF16)


def pack(value):
    rest = jnp.concatenate([value[:40, 128:], value[32:, 128:]], axis=1)
    return jnp.concatenate([value[:, :128], rest], axis=0).astype(BF16)


def unpack(value):
    wide = value.astype(F32)
    rest = wide[CHUNK:]
    right = jnp.concatenate([rest[:, :64], rest[8:, 64:]], axis=0)
    return jnp.concatenate([wide[:CHUNK], right], axis=1)


def place_of(lon, lat):
    x = lax.rem(lat, 2) * 2 + lax.div(lon, 8)
    return (x, lax.rem(lax.div(lon, 2), RING), lax.div(lat, 2)), lax.rem(lon, 2)


def device_at(chip, core):
    x, y, z = chip
    return ((lax.rem(x, 2) * RING + y) * 2 + core, z * 2 + lax.div(x, 2))


def moved(chip, axis, step):
    return tuple(lax.rem(c + step, RING) if i == axis else c for i, c in enumerate(chip))


def remote(src, dst, send, recv, device):
    return pltpu.make_async_remote_copy(
        src_ref=src, dst_ref=dst, send_sem=send, recv_sem=recv, device_id=device, device_id_type=MESH
    )


class Here:
    def __init__(self, n_lon, n_lat):
        self.lon, self.lat = lax.axis_index("lon"), lax.axis_index("lat")
        self.chip, self.core = place_of(self.lon, self.lat)
        self.sibling = (self.lon + 1 - 2 * self.core, self.lat)
        self.slot = [[lax.rem(c + k, RING) for k in range(RING)] for c in self.chip]
        chips = [[moved(self.chip, axis, k) for k in range(RING)] for axis in range(3)]
        self.along = [[device_at(chip, self.core) for chip in ring] for ring in chips]
        other = 1 - self.core
        self.eight = []
        for axis in range(3):
            found = []
            for k in range(RING):
                if k:
                    found.append((self.along[axis][k], self.slot[axis][k], self.core))
                found.append((device_at(chips[axis][k], other), self.slot[axis][k], other))
            self.eight.append(found)
        self.facing = (lax.rem(self.lon + 8, 16), self.lat)
        self.across = {}
        for step in (-1, 1):
            to_lon = lax.rem(self.lon + n_lon + step, n_lon)
            to_lat = lax.rem(self.lat + n_lat + step, n_lat)
            self.across[step] = ((to_lon, to_lat), (to_lon, self.lat), (self.lon, to_lat))

    def greet(self):
        others = [*self.across[-1], *self.across[1], self.sibling]
        for axis in range(3):
            others += [device for device, _, _ in self.eight[axis][1:]]
        barrier = pltpu.get_barrier_semaphore()
        for device in others:
            pl.semaphore_signal(barrier, inc=1, device_id=device, device_id_type=MESH)
        return lambda: pl.semaphore_wait(barrier, len(others))


def halo(here, source, target, send, recv, step):
    copies = []
    for index in range(3):
        src = index if step < 0 else 3 - index
        device = here.across[step][index]
        copies.append(remote(source.at[src], target.at[3 - src], send.at[index], recv.at[index], device))
    return copies


def begin(copies):
    for copy in copies:
        copy.start()


def end(copies):
    for copy in copies:
        copy.wait()


def wait_bytes(like, sem):
    pltpu.make_async_copy(like, like, sem).wait()


def room(*dims):
    return pltpu.VMEM((*dims, *TILE), BF16)


def tiles_in(block):
    narrow = block.astype(BF16)
    for c in range(block.shape[1] // 128):
        for r in range(block.shape[0] // 16):
            yield narrow[r * 16 : (r + 1) * 16, c * 128 : (c + 1) * 128]


def added(terms):
    total = terms[0].astype(F32)
    for term in terms[1:]:
        total = total + term.astype(F32)
    return total.astype(BF16)


class WeightSum:
    def __init__(self, here, out, refs):
        self.here, self.out = here, out
        self.src, self.r1, self.x2, self.x3, self.send, self.recv = refs

    @staticmethod
    def scratch(tiles):
        n1 = tiles // 24
        dma = pltpu.SemaphoreType.DMA
        return [room(3, RING, 2, n1), room(7, 3, n1), room(3, RING, n1), room(3, RING, n1), dma((4,)), dma((4,))]

    def put(self, block, first):
        n1 = self.src.shape[3]
        for at, tile in enumerate(tiles_in(block), first):
            self.src[at // (8 * n1), at // (2 * n1) % RING, at // n1 % 2, at % n1] = tile

    def phase(self, at):
        here, made = self.here, []
        sems = self.send.at[at], self.recv.at[at]
        for t in range(3):
            if at in (0, 3):
                mine = self.out.at[t, here.slot[t][0], here.core]
                for k, (device, slot, core) in enumerate(here.eight[t]):
                    if at == 0:
                        made.append(remote(self.src.at[t, slot, core], self.r1.at[k, t], *sems, device))
                    else:
                        made.append(remote(mine, mine, *sems, device))
            else:
                axis = (t + at) % 3
                mine = (self.x2 if at == 1 else self.x3).at[t, here.slot[axis][0]]
                made += [remote(mine, mine, *sems, here.along[axis][k]) for k in range(1, RING)]
        return made

    def start(self):
        begin(self.phase(0))

    def step(self, at):
        like = self.r1 if at in (0, 3) else self.r1.at[pl.ds(0, 3)]
        wait_bytes(like, self.recv.at[at])
        wait_bytes(like, self.send.at[at])
        core = self.here.core
        for t in range(3):
            one, two, three = (self.here.slot[(t + i) % 3][0] for i in range(3))
            if at == 0:
                self.x2[t, two] = added([self.src[t, one, core]] + [self.r1[k, t] for k in range(7)])
            if at == 1:
                self.x3[t, three] = added([self.x2[t, k] for k in range(RING)])
            if at == 2:
                self.out[t, one, core] = added([self.x3[t, k] for k in range(RING)])
        if at < 3:
            begin(self.phase(at + 1))


class PairSum:
    def __init__(self, here, out, refs):
        self.here, self.out = here, out
        self.src, self.other, self.a1, self.r1, self.x2, self.x3, self.send, self.recv = refs

    @staticmethod
    def scratch(tiles):
        n1 = tiles // 24
        dma = pltpu.SemaphoreType.DMA
        return [
            room(2, tiles // 2), room(tiles // 2),
            room(3, RING, n1), room(3, RING - 1, n1), room(3, RING, n1), room(3, RING, n1),
            dma((6,)), dma((6,)),
        ]

    def put(self, block, first):
        each = self.src.shape[1]
        for at, tile in enumerate(tiles_in(block), first):
            self.src[at // each, at % each] = tile

    def get(self):
        n1 = self.a1.shape[2]
        return [self.out[i // (12 * n1), i // (4 * n1) % 3, i // n1 % 4, i % n1] for i in range(24 * n1)]

    def copies(self, at, axis_of, source, target):
        made = []
        for t in range(3):
            axis = (t + axis_of) % 3
            slot = self.here.slot[axis]
            for k in range(1, RING):
                made.append(
                    remote(
                        source(t, slot[k], slot[0]), target(t, k - 1, slot[0]),
                        self.send.at[at], self.recv.at[at], self.here.along[axis][k],
                    )
                )
        return made

    def phase(self, at):
        core = self.here.core
        if at == 0:
            return [remote(self.src.at[1 - core], self.other, self.send.at[0], self.recv.at[0], self.here.sibling)]
        if at == 1:
            return self.copies(1, 0, lambda t, to, me: self.a1.at[t, to], lambda t, k, me: self.r1.at[t, k])
        if at == 2:
            return self.copies(2, 1, lambda t, to, me: self.x2.at[t, me], lambda t, k, me: self.x2.at[t, me])
        if at == 3:
            return self.copies(3, 2, lambda t, to, me: self.x3.at[t, me], lambda t, k, me: self.x3.at[t, me])
        if at == 4:
            out = self.out.at[core]
            return self.copies(4, 0, lambda t, to, me: out.at[t, me], lambda t, k, me: out.at[t, me])
        return [remote(self.out.at[core], self.out.at[core], self.send.at[5], self.recv.at[5], self.here.sibling)]

    def start(self):
        begin(self.phase(0))

    def step(self, at):
        like = self.other if at in (0, 5) else self.r1
        wait_bytes(like, self.recv.at[at])
        wait_bytes(like, self.send.at[at])
        core = self.here.core
        if at == 0:
            total = self.src[core].astype(F32) + self.other[...].astype(F32)
            self.a1[...] = total.astype(BF16).reshape(self.a1.shape)
        for t in range(3):
            one, two, three = (self.here.slot[(t + i) % 3][0] for i in range(3))
            if at == 1:
                total = self.a1[t, one].astype(F32)
                for k in range(RING - 1):
                    total = total + self.r1[t, k].astype(F32)
                self.x2[t, two] = total.astype(BF16)
            if at in (2, 3):
                came = self.x2 if at == 2 else self.x3
                total = came[t, 0].astype(F32)
                for k in range(1, RING):
                    total = total + came[t, k].astype(F32)
                if at == 2:
                    self.x3[t, three] = total.astype(BF16)
                else:
                    self.out[core, t, one] = total.astype(BF16)
        if at < 5:
            begin(self.phase(at + 1))


class BiasSum:
    def __init__(self, here, out, refs):
        self.here, self.out = here, out
        self.src, self.r1, self.x2, self.send, self.recv = refs

    @staticmethod
    def scratch():
        each = B_TILES // 8
        dma = pltpu.SemaphoreType.DMA
        return [room(RING, 2, each), room(7, each), room(2, each), dma((3,)), dma((3,))]

    def put(self, block):
        each = B_TILES // 8
        last = block[:, 256:]
        shared = last[0:B_ROWS]
        for g in range(1, 288 // B_ROWS):
            shared = shared + pltpu.roll(last[g * B_ROWS : (g + 1) * B_ROWS], g * B_LEFT, 1)
        tiles = [*tiles_in(block[:, :256]), *tiles_in(shared), jnp.zeros(TILE, BF16)]
        for at, tile in enumerate(tiles):
            self.src[at // (2 * each), at // each % 2, at % each] = tile

    def get(self):
        each = B_TILES // 8
        tiles = [self.out[at // (2 * each), at // each % 2, at % each] for at in range(B_TILES)]
        first = joined(tiles[:36], 2)
        shared = joined(tiles[36:39], 1)
        last = [shared]
        for g in range(1, 288 // B_ROWS):
            last.append(pltpu.roll(shared, 128 - g * B_LEFT, 1))
        return jnp.concatenate([first, jnp.concatenate(last, axis=0)], axis=1)

    def phase(self, at):
        here, made = self.here, []
        sems = self.send.at[at], self.recv.at[at]
        if at == 1:
            return [remote(self.x2.at[0], self.x2.at[1], *sems, here.facing)]
        mine = self.out.at[here.slot[1][0], here.core]
        for k, (device, slot, core) in enumerate(here.eight[1]):
            if at == 0:
                made.append(remote(self.src.at[slot, core], self.r1.at[k], *sems, device))
            else:
                made.append(remote(mine, mine, *sems, device))
        return made

    def start(self):
        begin(self.phase(0))

    def step(self, at):
        like = self.x2.at[1] if at == 1 else self.r1
        wait_bytes(like, self.recv.at[at])
        wait_bytes(like, self.send.at[at])
        slot, core = self.here.slot[1][0], self.here.core
        if at == 0:
            self.x2[0] = added([self.src[slot, core]] + [self.r1[k] for k in range(7)])
        if at == 1:
            self.out[slot, core] = added([self.x2[0], self.x2[1]])
        if at < 2:
            begin(self.phase(at + 1))


def layer_norm(x):
    centered = x - jnp.mean(x, axis=-1, keepdims=True)
    spread = jnp.mean(centered * centered, axis=-1, keepdims=True)
    rate = lax.rsqrt(spread + EPSILON)
    return centered * rate, rate


def layer_norm_back(cot, unit, rate):
    first = jnp.mean(cot, axis=-1, keepdims=True)
    second = jnp.mean(cot * unit, axis=-1, keepdims=True)
    return rate * (cot - first - unit * second)


def head_mask(head):
    lane = lax.broadcasted_iota(jnp.int32, (1, C), 1)
    return (lane >= head * 32) & (lane < head * 32 + 32)


def stacked(value):
    wide = value.astype(F32)
    parts = [jnp.where(head_mask(h), wide, 0.0).astype(BF16) for h in range(HEADS)]
    return jnp.concatenate(parts, axis=0)


def unstacked(value):
    total = jnp.where(head_mask(0), value[0:WIN], 0.0)
    for h in range(1, HEADS):
        total = total + jnp.where(head_mask(h), value[h * WIN : (h + 1) * WIN], 0.0)
    return total


def expand_bias(last_lat, table, columns, index_rows, lanes, tall_table, gathered, strips, scores):
    for head in range(HEADS):
        tall_table[head * LWIN : (head + 1) * LWIN, :] = table[head]
    for site in range(SITE):
        lev, a = site // WLAT, site % WLAT
        for other in range(WLEV):
            start = ((lev * WLEV + other) * WLAT + a) * RUN
            gathered[site * WH : (site + 1) * WH, other * RUN : (other + 1) * RUN] = tall_table[
                :, start : start + RUN
            ]
    moved = sum(dot(part, lanes[...]) for part in pieces(gathered[...], 3))
    rows = one_hot(columns[:, 1:2], WH * 2 * SITE, SITE * WH)
    moved = sum(dot(rows, part) for part in pieces(moved, 3))
    code = columns[:, 2:3]
    moved = jnp.where((code & 8) != 0, pltpu.roll(moved, LANES - SITE, 1), moved) * LOG2E
    seen = jnp.where((code & 4) != 0, 1, 0) + jnp.where(last_lat, 2, 0)
    apart = (code ^ index_rows[2:3, 0:LANES]) & seen
    strips[...] = jnp.where(apart != 0, MASKED, moved)

    def one(wh, carry):
        strip = strips[pl.ds(pl.multiple_of(wh * 2 * SITE, 8), 2 * SITE), :]
        start = lax.rem(wh, LWIN) * STACK + lax.div(wh, LWIN) * WIN
        for pair in range(WLON // 2):
            offset = (WLON - 2 - 2 * pair) * SITE
            scores[pl.ds(pl.multiple_of(start + pair * 24, 8), 24), :] = strip[
                :, offset : offset + WIN
            ]
        return carry

    lax.fori_loop(0, WH, one, 0)


def collapse_bias(first, last, scores, strips):
    def one(wh, carry):
        start = lax.rem(wh, LWIN) * STACK + lax.div(wh, LWIN) * WIN
        total = jnp.zeros((2 * SITE, LANES), F32)
        for pair in range(WLON // 2):
            offset = (WLON - 2 - 2 * pair) * SITE
            part = scores[pl.ds(pl.multiple_of(start + pair * 24, 8), 24), :]
            part = jnp.concatenate([part, jnp.zeros((2 * SITE, LANES - WIN), F32)], axis=1)
            total = total + (pltpu.roll(part, offset, 1) if offset else part)
        strips[pl.ds(pl.multiple_of(wh * 2 * SITE, 8), 2 * SITE), :] = total
        return carry

    lax.fori_loop(first, last, one, 0)


def join_strips(strips, columns, index_rows):
    total = strips[...]
    total = jnp.where((columns[:, 2:3] & 8) != 0, pltpu.roll(total, SITE, 1), total)
    rows = one_hot(index_rows[1:2, :], SITE * WH, WH * 2 * SITE)
    return sum(dot(rows, part) for part in pieces(total, 2))


def block_kernel(n_lon, n_lat, *refs):
    loaded = refs[:9]
    out_field, grad_field, qkv, proj, fc1, fc2, bias = refs[9:16]
    field, cot, w_qkv, w_proj, w_fc1, w_fc2, table, columns, index_rows, load_sem = refs[16:26]
    (
        out, e_out, l_out, b_out, sent, came, cot_sent, cot_came, back, halo_send, halo_recv,
        xw, uw, scores, normed, query, key, value, unit, rate, blended, normed_two, hidden,
        cot_first, cot_mid, cot_q, cot_k, cot_v, ow, gw, tall_table, gathered, strips, w3,
        places_in, places_out, lanes, slope, unit_two, rate_two,
    ) = refs[26:66]
    here = Here(n_lon, n_lat)
    early = PairSum(here, e_out, refs[66:74])
    late = WeightSum(here, l_out, refs[74:80])
    strip_sum = BiasSum(here, b_out, refs[80:85])

    loads = [
        pltpu.make_async_copy(src, dst, load_sem.at[i]) for i, (src, dst) in enumerate(zip(loaded, refs[16:25]))
    ]
    loads[0].start()
    greeted = here.greet()
    begin(loads[6:9])
    loads[0].wait()
    for index in range(3):
        for part, chunk in enumerate(split(field, index)):
            sent[part, index] = pack(chunk)
    greeted()
    inward = [
        halo(here, sent.at[i], came.at[i], halo_send.at[i], halo_recv.at[i], -1) for i in range(2)
    ]
    cot_inward = halo(here, cot_sent, cot_came, halo_send.at[2], halo_recv.at[2], -1)
    outward = [
        halo(here, back.at[i], out.at[i], halo_send.at[3 + i], halo_recv.at[3 + i], 1) for i in range(2)
    ]
    begin(inward[0])
    begin(inward[1])
    begin(loads[1:6])
    end(loads[6:9])
    lanes[...] = one_hot(columns[0:STRIP, 3:4], STRIP, LANES)
    last_lat = here.lat == n_lat - 1
    expand_bias(last_lat, table, columns, index_rows, lanes, tall_table, gathered, strips, scores)
    places_in[...] = one_hot(columns[0:PAIR, 0:1], PAIR, PAIR)
    places_out[...] = one_hot(index_rows[0:1, 0:PAIR], PAIR, PAIR)
    loads[1].wait()
    for index in range(3):
        for part, chunk in enumerate(split(cot, index)):
            cot_sent[index, part] = pack(chunk)
    own = [split(ref, 3) for ref in (field, cot)]
    loads[2].wait()
    for third in range(3):
        w3[third] = w_qkv[:, third * C : (third + 1) * C]

    def gather(kind, part):
        if kind:
            arrived = [cot_came[i, part] for i in range(1, 4)]
        else:
            arrived = [came[part, i] for i in range(1, 4)]
        parts = [own[kind][part]] + [unpack(value) for value in arrived]
        return dot(places_in[...], jnp.concatenate(parts, axis=0).astype(BF16)).astype(BF16)

    def scatter(kind, ref):
        for part in range(2):
            whole = dot(places_out[...], ref[part * PAIR : (part + 1) * PAIR, :])
            out[kind, 3, part] = pack(whole[:CHUNK])
            for i in range(1, 4):
                back[kind, i, part] = pack(whole[i * CHUNK : (i + 1) * CHUNK])
        begin(outward[kind])

    def places(w):
        return pl.ds(w * WIN, WIN), pl.ds(w * STACK, STACK)

    def attend(w):
        rows, tall = places(w)
        unit_x, rate_x = layer_norm(xw[rows, :].astype(F32))
        unit[rows, :] = unit_x
        rate[rows, :] = rate_x
        norm = unit_x.astype(BF16)
        normed[rows, :] = norm
        q = dot(norm, w3[0]).astype(BF16)
        k = dot(norm, w3[1]).astype(BF16)
        v = dot(norm, w3[2]).astype(BF16)
        query[rows, :] = q
        key[rows, :] = k
        value[rows, :] = v
        s = dot_nt(stacked(q), k) * (SCALE * LOG2E) + scores[tall, :]
        e = jnp.exp2(s - jnp.max(s, axis=-1, keepdims=True))
        p = e * (1.0 / jnp.sum(e, axis=-1, keepdims=True))
        scores[tall, :] = p
        blended[rows, :] = unstacked(dot(p.astype(BF16), v)).astype(BF16)

    def feed(w):
        rows = pl.ds(w * 2 * WIN, 2 * WIN)
        middle = xw[rows, :].astype(F32) + dot(blended[rows, :], w_proj[...])
        middle = middle.astype(BF16).astype(F32)
        unit_m, rate_m = layer_norm(middle)
        norm_m = unit_m.astype(BF16)
        normed_two[rows, :] = norm_m
        first = dot(norm_m, w_fc1[...])
        phi = 0.5 + 0.5 * lax.erf(first * math.sqrt(0.5))
        hid = (first * phi).astype(BF16)
        hidden[rows, :] = hid
        bell = jnp.exp2(first * first * (-0.5 * LOG2E)) * (1.0 / math.sqrt(2.0 * math.pi))
        slope[rows, :] = phi + first * bell
        unit_two[rows, :] = unit_m
        rate_two[rows, :] = rate_m
        ow[rows, :] = (middle + dot_nt(hid, w_fc2[...])).astype(BF16)

    def feed_back(w):
        rows = pl.ds(w * 2 * WIN, 2 * WIN)
        up = uw[rows, :]
        c_first = (dot(up, w_fc2[...]).astype(BF16).astype(F32) * slope[rows, :]).astype(BF16)
        cot_first[rows, :] = c_first
        c_norm = dot_nt(c_first, w_fc1[...]).astype(BF16).astype(F32)
        c_mid = layer_norm_back(c_norm, unit_two[rows, :], rate_two[rows, :]).astype(BF16).astype(F32)
        cot_mid[rows, :] = (up.astype(F32) + c_mid).astype(BF16)

    def backward(w):
        rows, tall = places(w)
        up = cot_mid[rows, :]
        c_blend = stacked(dot_nt(up, w_proj[...]).astype(BF16))
        p = scores[tall, :]
        c_p = dot_nt(c_blend, value[rows, :])
        c_s = p * (c_p - jnp.sum(p * c_p, axis=-1, keepdims=True))
        scores[tall, :] = c_s
        c_v = dot_tn(p.astype(BF16), c_blend).astype(BF16)
        narrow = c_s.astype(BF16)
        c_q = (unstacked(dot(narrow, key[rows, :])) * SCALE).astype(BF16)
        c_k = (dot_tn(narrow, stacked(query[rows, :])) * SCALE).astype(BF16)
        cot_q[rows, :] = c_q
        cot_k[rows, :] = c_k
        cot_v[rows, :] = c_v

    def inputs_back(w):
        rows = pl.ds(w * 2 * WIN, 2 * WIN)
        c_norm = dot_nt(cot_q[rows, :], w3[0]) + dot_nt(cot_k[rows, :], w3[1])
        c_norm = (c_norm + dot_nt(cot_v[rows, :], w3[2])).astype(BF16).astype(F32)
        c_x = layer_norm_back(c_norm, unit[rows, :], rate[rows, :]).astype(BF16)
        gw[rows, :] = (cot_mid[rows, :].astype(F32) + c_x.astype(F32)).astype(BF16)

    for part in range(2):
        end(inward[part])
        xw[part * PAIR : (part + 1) * PAIR, :] = gather(0, part)
        if not part:
            begin(cot_inward)
        attend(2 * part)
        attend(2 * part + 1)
    end(loads[3:6])
    feed(0)
    feed(1)
    scatter(0, ow)
    end(cot_inward)
    for part in range(2):
        uw[part * PAIR : (part + 1) * PAIR, :] = gather(1, part)
        feed_back(part)
    early.put(dot_tn(normed_two[...], cot_first[...]), 0)
    early.put(dot_tn(uw[...], hidden[...]), 72)
    early.start()
    backward(0)
    backward(1)
    early.step(0)
    backward(2)
    backward(3)
    early.step(1)
    norm = normed[...]
    late.put(jnp.concatenate([dot_tn(norm, cot_q[...]), dot_tn(norm, cot_k[...])], axis=1), 0)
    c_proj = dot_tn(blended[...], cot_mid[...])
    late.put(jnp.concatenate([dot_tn(norm, cot_v[...]), c_proj], axis=1), 36)
    late.start()
    collapse_bias(0, WH, scores, strips)
    strip_sum.put(join_strips(strips, columns, index_rows))
    strip_sum.start()
    early.step(2)
    inputs_back(0)
    inputs_back(1)
    late.step(0)
    scatter(1, gw)
    early.step(3)
    strip_sum.step(0)
    late.step(1)
    early.step(4)
    strip_sum.step(1)
    end(outward[0])
    for index in range(4):
        merge(out_field, index, [unpack(out[0, index, part]) for part in range(2)])
    late.step(2)
    early.step(5)
    fc1[...] = joined(early.get()[:72], 6)
    fc2[...] = joined(early.get()[72:], 6)
    strip_sum.step(2)
    finish_bias(strip_sum.get(), lanes, tall_table, bias)
    end(outward[1])
    for index in range(4):
        merge(grad_field, index, [unpack(out[1, index, part]) for part in range(2)])
    late.step(3)
    qkv[:, 0:384] = joined(tiles_of(l_out)[:36], 3)
    right = joined(tiles_of(l_out)[36:], 3)
    qkv[:, 384:576] = right[:, 0:C]
    proj[...] = right[:, C:]


def joined(tiles, columns):
    rows = len(tiles) // columns
    cols = [jnp.concatenate(tiles[c * rows : (c + 1) * rows], axis=0) for c in range(columns)]
    return jnp.concatenate(cols, axis=1).astype(F32)


def tiles_of(ref):
    n1 = ref.shape[3]
    return [ref[i // (8 * n1), i // (2 * n1) % RING, i // n1 % 2, i % n1] for i in range(24 * n1)]


def finish_bias(strip, lanes, tall_table, bias):
    runs = dot_nt(strip.astype(BF16), lanes[...])
    for site in range(SITE):
        lev, a = site // WLAT, site % WLAT
        for other in range(WLEV):
            start = ((lev * WLEV + other) * WLAT + a) * RUN
            tall_table[:, start : start + RUN] = runs[
                site * WH : (site + 1) * WH, other * RUN : (other + 1) * RUN
            ]
    for head in range(HEADS):
        bias[head] = tall_table[head * LWIN : (head + 1) * LWIN, :]


def finish_kernel(*refs):
    count = len(refs) // 2
    copies = [pltpu.make_async_copy(refs[i], refs[count + i], refs[-1].at[i]) for i in range(count)]
    begin(copies)
    end(copies)


def per_device(n_lon, n_lat, field, w_qkv, w_proj, w_fc1, w_fc2, bias_table, cotangent):
    vmem, hbm = pl.BlockSpec(memory_space=pltpu.VMEM), pl.BlockSpec(memory_space=pltpu.HBM)
    shape = jax.ShapeDtypeStruct
    dma = pltpu.SemaphoreType.DMA
    rows = row_places()
    columns = columns_of(token_places(), rows, row_codes(), lane_places())
    index_rows = columns_of(token_places(), rows, lane_codes()).T.copy()
    inputs = (
        field, cotangent, w_qkv, w_proj, w_fc1, w_fc2.T, bias_table[0].transpose(1, 0, 2), columns, index_rows
    )
    inputs = [pltpu.with_memory_space_constraint(jnp.asarray(a), pltpu.HBM) for a in inputs]
    tile = shape((WLON, WLAT, LEV, C), BF16)
    outputs = (
        tile,
        tile,
        shape((C, 3 * C), F32),
        shape((C, C), F32),
        shape((C, HIDDEN), F32),
        shape((C, HIDDEN), F32),
        shape((HEADS, LWIN, POS), F32),
    )
    wide = lambda dtype, n=1: [pltpu.VMEM((TOK, C), dtype)] * n
    results = pl.pallas_call(
        functools.partial(block_kernel, n_lon, n_lat),
        out_shape=outputs,
        in_specs=[hbm] * len(inputs),
        out_specs=[vmem] * len(outputs),
        scratch_shapes=[
            *[pltpu.VMEM(a.shape, a.dtype) for a in inputs],
            dma((len(inputs),)),
            pltpu.VMEM((2, 4, 2, PACKED, 128), BF16),
            room(2, 3, RING, E_TILES // 24),
            room(3, RING, 2, L_TILES // 24),
            room(RING, 2, B_TILES // 8),
            pltpu.VMEM((2, 3, PACKED, 128), BF16),
            pltpu.VMEM((2, 4, PACKED, 128), BF16),
            pltpu.VMEM((3, 2, PACKED, 128), BF16),
            pltpu.VMEM((4, 2, PACKED, 128), BF16),
            pltpu.VMEM((2, 4, 2, PACKED, 128), BF16),
            dma((5, 3)),
            dma((5, 3)),
            *wide(BF16, 2),
            pltpu.VMEM((LWIN * STACK, WIN), F32),
            *wide(BF16, 4),
            *wide(F32),
            pltpu.VMEM((TOK, 1), F32),
            *wide(BF16, 2),
            pltpu.VMEM((TOK, HIDDEN), BF16),
            pltpu.VMEM((TOK, HIDDEN), BF16),
            *wide(BF16, 6),
            pltpu.VMEM((WH, POS), F32),
            pltpu.VMEM((SITE * WH, STRIP), F32),
            pltpu.VMEM((WH * 2 * SITE, LANES), F32),
            pltpu.VMEM((3, C, C), BF16),
            pltpu.VMEM((PAIR, PAIR), BF16),
            pltpu.VMEM((PAIR, PAIR), BF16),
            pltpu.VMEM((STRIP, LANES), BF16),
            pltpu.VMEM((TOK, HIDDEN), F32),
            *wide(F32),
            pltpu.VMEM((TOK, 1), F32),
            *PairSum.scratch(E_TILES),
            *WeightSum.scratch(L_TILES),
            *BiasSum.scratch(),
        ],
        compiler_params=pltpu.CompilerParams(
            vmem_limit_bytes=VMEM_LIMIT, collective_id=0, has_side_effects=True
        ),
        name="block",
    )(*inputs)
    *results, fc2, bias = pl.pallas_call(
        finish_kernel,
        out_shape=outputs,
        in_specs=[vmem] * len(outputs),
        out_specs=[hbm] * len(outputs),
        scratch_shapes=[dma((len(outputs),))],
        compiler_params=pltpu.CompilerParams(vmem_limit_bytes=VMEM_LIMIT),
        name="finish",
    )(*results)
    return (*results, fc2.T, bias.transpose(1, 0, 2)[None])


def solution(mesh):
    whole, tiles, banded = P(), P("lon", "lat", None, None), P("lat", None, None, None)
    return jax.shard_map(
        functools.partial(per_device, mesh.shape["lon"], mesh.shape["lat"]),
        mesh=mesh,
        in_specs=(tiles, whole, whole, whole, whole, banded, tiles),
        out_specs=(tiles, tiles, whole, whole, whole, whole, banded),
        check_vma=False,
    )
```

```python
import functools
import math

import jax
import jax.numpy as jnp
import numpy as np
from jax import lax
from jax.experimental import pallas as pl
from jax.experimental.pallas import tpu as pltpu
from jax.sharding import PartitionSpec as P

C = 192
HEADS = 6
HIDDEN = 768
LEV = 8
WLON = 12
WLAT = 6
WLEV = 2
LWIN = LEV // WLEV
WH = LWIN * HEADS
WIN = WLEV * WLAT * WLON
TOK = LWIN * WIN
QUAD = TOK // 4
SITE = WLEV * WLAT
SHIFTS = 2 * WLON - 1
STRIP = SHIFTS * SITE
POS = WLEV * WLEV * WLAT * WLAT * SHIFTS
RUN = WLAT * SHIFTS
LANES = 384
STACK = HEADS * WIN
EPSILON = 1e-05
MASKED = -1000000000.0
LOG2E = math.log2(math.e)
SCALE = 1.0 / math.sqrt(C // HEADS)
RING = 4
E_TILES = 144
L_TILES = 72
B_TILES = 40
B_LEFT = STRIP - 256
B_ROWS = 48
CHUNK = QUAD // 2
PAIR = 4 * CHUNK
PACKED = 112
TILE = (16, 128)
BF16 = jnp.bfloat16
F32 = jnp.float32
MESH = pl.DeviceIdType.MESH
VMEM_LIMIT = 30 * 1024 * 1024


def token_places():
    w, o, lev, a = np.meshgrid(
        np.arange(2), np.arange(WLON), np.arange(WLEV), np.arange(WLAT), indexing="ij"
    )
    site = (o % 6) * 3 + a % 3
    row = (site % 9) * 8 + (site // 9) * 4 + 2 * w + lev
    return (((o // 6) * 2 + a // 3) * CHUNK + row).reshape(PAIR).astype(np.int32)


def lane_places():
    lev, a, d = np.meshgrid(np.arange(WLEV), np.arange(WLAT), np.arange(SHIFTS), indexing="ij")
    return ((SHIFTS - 1 - d) * SITE + lev * WLAT + a).reshape(STRIP).astype(np.int32)


def row_places():
    wh, _, site = np.meshgrid(np.arange(WH), np.arange(2), np.arange(SITE), indexing="ij")
    return (site * WH + wh).reshape(WH * 2 * SITE).astype(np.int32)


def row_codes():
    _, w, p, lev, a = np.meshgrid(
        np.arange(HEADS), np.arange(LWIN), np.arange(2), np.arange(WLEV), np.arange(WLAT), indexing="ij"
    )
    code = lev + 2 * (a >= WLAT // 2) + 4 * (w == LWIN - 1) + 8 * (p == 0)
    return code.reshape(WH * 2 * SITE).astype(np.int32)


def lane_codes():
    site = np.arange(LANES) % SITE
    return (site // WLAT + 2 * (site % WLAT >= WLAT // 2)).astype(np.int32)


def columns_of(*arrays):
    made = np.zeros((TOK, 8), np.int32)
    for i, array in enumerate(arrays):
        made[: len(array), i] = array
    return made


def dot(a, b):
    return jnp.dot(a, b, preferred_element_type=F32)


def dot_nt(a, b):
    return lax.dot_general(a, b, (((1,), (1,)), ((), ())), preferred_element_type=F32)


def dot_tn(a, b):
    return lax.dot_general(a, b, (((0,), (0,)), ((), ())), preferred_element_type=F32)


def one_hot(places, rows, cols):
    along = 1 if places.shape[1] == 1 else 0
    index = lax.broadcasted_iota(jnp.int32, (rows, cols), along)
    return jnp.where(index == places, 1.0, 0.0).astype(BF16)


def pieces(value, count):
    found = []
    for _ in range(count):
        part = value.astype(BF16)
        found.append(part)
        value = value - part.astype(F32)
    return found


def split(ref, index):
    part = ref[pl.ds((index // 2) * 6, 6), pl.ds((index % 2) * 3, 3)]
    part = pltpu.roll(part.astype(F32).reshape(18, LEV, C), LEV - 1, 1)
    low, high = part[:9], part[9:]
    upper = lax.broadcasted_iota(jnp.int32, low.shape, 1) < LEV // 2
    first = jnp.where(upper, low, pltpu.roll(high, LEV // 2, 1))
    second = jnp.where(upper, pltpu.roll(low, LEV // 2, 1), high)
    return first.reshape(CHUNK, C), second.reshape(CHUNK, C)


def merge(ref, index, chunks):
    first, second = (chunk.reshape(9, LEV, C) for chunk in chunks)
    upper = lax.broadcasted_iota(jnp.int32, first.shape, 1) < LEV // 2
    low = jnp.where(upper, first, pltpu.roll(second, LEV // 2, 1))
    high = jnp.where(upper, pltpu.roll(first, LEV // 2, 1), second)
    part = pltpu.roll(jnp.concatenate([low, high], axis=0), 1, 1)
    ref[pl.ds((index // 2) * 6, 6), pl.ds((index % 2) * 3, 3)] = part.reshape(6, 3, LEV, C).astype(BF16)


def pack(value):
    rest = jnp.concatenate([value[:40, 128:], value[32:, 128:]], axis=1)
    return jnp.concatenate([value[:, :128], rest], axis=0).astype(BF16)


def unpack(value):
    wide = value.astype(F32)
    rest = wide[CHUNK:]
    right = jnp.concatenate([rest[:, :64], rest[8:, 64:]], axis=0)
    return jnp.concatenate([wide[:CHUNK], right], axis=1)


def place_of(lon, lat):
    x = lax.rem(lat, 2) * 2 + lax.div(lon, 8)
    return (x, lax.rem(lax.div(lon, 2), RING), lax.div(lat, 2)), lax.rem(lon, 2)


def device_at(chip, core):
    x, y, z = chip
    return ((lax.rem(x, 2) * RING + y) * 2 + core, z * 2 + lax.div(x, 2))


def moved(chip, axis, step):
    return tuple(lax.rem(c + step, RING) if i == axis else c for i, c in enumerate(chip))


def remote(src, dst, send, recv, device):
    return pltpu.make_async_remote_copy(
        src_ref=src, dst_ref=dst, send_sem=send, recv_sem=recv, device_id=device, device_id_type=MESH
    )


class Here:
    def __init__(self, n_lon, n_lat):
        self.lon, self.lat = lax.axis_index("lon"), lax.axis_index("lat")
        self.chip, self.core = place_of(self.lon, self.lat)
        self.sibling = (self.lon + 1 - 2 * self.core, self.lat)
        self.slot = [[lax.rem(c + k, RING) for k in range(RING)] for c in self.chip]
        chips = [[moved(self.chip, axis, k) for k in range(RING)] for axis in range(3)]
        self.along = [[device_at(chip, self.core) for chip in ring] for ring in chips]
        other = 1 - self.core
        self.eight = []
        for axis in range(3):
            found = []
            for k in range(RING):
                if k:
                    found.append((self.along[axis][k], self.slot[axis][k], self.core))
                found.append((device_at(chips[axis][k], other), self.slot[axis][k], other))
            self.eight.append(found)
        self.facing = (lax.rem(self.lon + 8, 16), self.lat)
        self.across = {}
        for step in (-1, 1):
            to_lon = lax.rem(self.lon + n_lon + step, n_lon)
            to_lat = lax.rem(self.lat + n_lat + step, n_lat)
            self.across[step] = ((to_lon, to_lat), (to_lon, self.lat), (self.lon, to_lat))

    def greet(self):
        others = [*self.across[-1], *self.across[1], self.sibling]
        for axis in range(3):
            others += [device for device, _, _ in self.eight[axis][1:]]
        barrier = pltpu.get_barrier_semaphore()
        for device in others:
            pl.semaphore_signal(barrier, inc=1, device_id=device, device_id_type=MESH)
        return lambda: pl.semaphore_wait(barrier, len(others))


def halo(here, source, target, send, recv, step):
    copies = []
    for index in range(3):
        src = index if step < 0 else 3 - index
        device = here.across[step][index]
        copies.append(remote(source.at[src], target.at[3 - src], send.at[index], recv.at[index], device))
    return copies


def begin(copies):
    for copy in copies:
        copy.start()


def end(copies):
    for copy in copies:
        copy.wait()


def wait_bytes(like, sem):
    pltpu.make_async_copy(like, like, sem).wait()


def room(*dims):
    return pltpu.VMEM((*dims, *TILE), BF16)


def tiles_in(block):
    narrow = block.astype(BF16)
    for c in range(block.shape[1] // 128):
        for r in range(block.shape[0] // 16):
            yield narrow[r * 16 : (r + 1) * 16, c * 128 : (c + 1) * 128]


def added(terms):
    total = terms[0].astype(F32)
    for term in terms[1:]:
        total = total + term.astype(F32)
    return total.astype(BF16)


class WeightSum:
    def __init__(self, here, out, refs):
        self.here, self.out = here, out
        self.src, self.r1, self.x2, self.x3, self.send, self.recv = refs

    @staticmethod
    def scratch(tiles):
        n1 = tiles // 24
        dma = pltpu.SemaphoreType.DMA
        return [room(3, RING, 2, n1), room(7, 3, n1), room(3, RING, n1), room(3, RING, n1), dma((4,)), dma((4,))]

    def put(self, block, first):
        n1 = self.src.shape[3]
        for at, tile in enumerate(tiles_in(block), first):
            self.src[at // (8 * n1), at // (2 * n1) % RING, at // n1 % 2, at % n1] = tile

    def phase(self, at):
        here, made = self.here, []
        sems = self.send.at[at], self.recv.at[at]
        for t in range(3):
            if at in (0, 3):
                mine = self.out.at[t, here.slot[t][0], here.core]
                for k, (device, slot, core) in enumerate(here.eight[t]):
                    if at == 0:
                        made.append(remote(self.src.at[t, slot, core], self.r1.at[k, t], *sems, device))
                    else:
                        made.append(remote(mine, mine, *sems, device))
            else:
                axis = (t + at) % 3
                mine = (self.x2 if at == 1 else self.x3).at[t, here.slot[axis][0]]
                made += [remote(mine, mine, *sems, here.along[axis][k]) for k in range(1, RING)]
        return made

    def start(self):
        begin(self.phase(0))

    def step(self, at):
        like = self.r1 if at in (0, 3) else self.r1.at[pl.ds(0, 3)]
        wait_bytes(like, self.recv.at[at])
        wait_bytes(like, self.send.at[at])
        core = self.here.core
        for t in range(3):
            one, two, three = (self.here.slot[(t + i) % 3][0] for i in range(3))
            if at == 0:
                self.x2[t, two] = added([self.src[t, one, core]] + [self.r1[k, t] for k in range(7)])
            if at == 1:
                self.x3[t, three] = added([self.x2[t, k] for k in range(RING)])
            if at == 2:
                self.out[t, one, core] = added([self.x3[t, k] for k in range(RING)])
        if at < 3:
            begin(self.phase(at + 1))


class PairSum:
    def __init__(self, here, out, refs):
        self.here, self.out = here, out
        self.src, self.other, self.a1, self.r1, self.x2, self.x3, self.send, self.recv = refs

    @staticmethod
    def scratch(tiles):
        n1 = tiles // 24
        dma = pltpu.SemaphoreType.DMA
        return [
            room(2, tiles // 2), room(tiles // 2),
            room(3, RING, n1), room(3, RING - 1, n1), room(3, RING, n1), room(3, RING, n1),
            dma((6,)), dma((6,)),
        ]

    def put(self, block, first):
        each = self.src.shape[1]
        for at, tile in enumerate(tiles_in(block), first):
            self.src[at // each, at % each] = tile

    def get(self):
        n1 = self.a1.shape[2]
        return [self.out[i // (12 * n1), i // (4 * n1) % 3, i // n1 % 4, i % n1] for i in range(24 * n1)]

    def copies(self, at, axis_of, source, target):
        made = []
        for t in range(3):
            axis = (t + axis_of) % 3
            slot = self.here.slot[axis]
            for k in range(1, RING):
                made.append(
                    remote(
                        source(t, slot[k], slot[0]), target(t, k - 1, slot[0]),
                        self.send.at[at], self.recv.at[at], self.here.along[axis][k],
                    )
                )
        return made

    def phase(self, at):
        core = self.here.core
        if at == 0:
            return [remote(self.src.at[1 - core], self.other, self.send.at[0], self.recv.at[0], self.here.sibling)]
        if at == 1:
            return self.copies(1, 0, lambda t, to, me: self.a1.at[t, to], lambda t, k, me: self.r1.at[t, k])
        if at == 2:
            return self.copies(2, 1, lambda t, to, me: self.x2.at[t, me], lambda t, k, me: self.x2.at[t, me])
        if at == 3:
            return self.copies(3, 2, lambda t, to, me: self.x3.at[t, me], lambda t, k, me: self.x3.at[t, me])
        if at == 4:
            out = self.out.at[core]
            return self.copies(4, 0, lambda t, to, me: out.at[t, me], lambda t, k, me: out.at[t, me])
        return [remote(self.out.at[core], self.out.at[core], self.send.at[5], self.recv.at[5], self.here.sibling)]

    def start(self):
        begin(self.phase(0))

    def step(self, at):
        like = self.other if at in (0, 5) else self.r1
        wait_bytes(like, self.recv.at[at])
        wait_bytes(like, self.send.at[at])
        core = self.here.core
        if at == 0:
            total = self.src[core].astype(F32) + self.other[...].astype(F32)
            self.a1[...] = total.astype(BF16).reshape(self.a1.shape)
        for t in range(3):
            one, two, three = (self.here.slot[(t + i) % 3][0] for i in range(3))
            if at == 1:
                total = self.a1[t, one].astype(F32)
                for k in range(RING - 1):
                    total = total + self.r1[t, k].astype(F32)
                self.x2[t, two] = total.astype(BF16)
            if at in (2, 3):
                came = self.x2 if at == 2 else self.x3
                total = came[t, 0].astype(F32)
                for k in range(1, RING):
                    total = total + came[t, k].astype(F32)
                if at == 2:
                    self.x3[t, three] = total.astype(BF16)
                else:
                    self.out[core, t, one] = total.astype(BF16)
        if at < 5:
            begin(self.phase(at + 1))


class BiasSum:
    def __init__(self, here, out, refs):
        self.here, self.out = here, out
        self.src, self.r1, self.x2, self.send, self.recv = refs

    @staticmethod
    def scratch():
        each = B_TILES // 8
        dma = pltpu.SemaphoreType.DMA
        return [room(RING, 2, each), room(7, each), room(2, each), dma((3,)), dma((3,))]

    def put(self, block):
        each = B_TILES // 8
        last = block[:, 256:]
        shared = last[0:B_ROWS]
        for g in range(1, 288 // B_ROWS):
            shared = shared + pltpu.roll(last[g * B_ROWS : (g + 1) * B_ROWS], g * B_LEFT, 1)
        tiles = [*tiles_in(block[:, :256]), *tiles_in(shared), jnp.zeros(TILE, BF16)]
        for at, tile in enumerate(tiles):
            self.src[at // (2 * each), at // each % 2, at % each] = tile

    def get(self):
        each = B_TILES // 8
        tiles = [self.out[at // (2 * each), at // each % 2, at % each] for at in range(B_TILES)]
        first = joined(tiles[:36], 2)
        shared = joined(tiles[36:39], 1)
        last = [shared]
        for g in range(1, 288 // B_ROWS):
            last.append(pltpu.roll(shared, 128 - g * B_LEFT, 1))
        return jnp.concatenate([first, jnp.concatenate(last, axis=0)], axis=1)

    def phase(self, at):
        here, made = self.here, []
        sems = self.send.at[at], self.recv.at[at]
        if at == 1:
            return [remote(self.x2.at[0], self.x2.at[1], *sems, here.facing)]
        mine = self.out.at[here.slot[1][0], here.core]
        for k, (device, slot, core) in enumerate(here.eight[1]):
            if at == 0:
                made.append(remote(self.src.at[slot, core], self.r1.at[k], *sems, device))
            else:
                made.append(remote(mine, mine, *sems, device))
        return made

    def start(self):
        begin(self.phase(0))

    def step(self, at):
        like = self.x2.at[1] if at == 1 else self.r1
        wait_bytes(like, self.recv.at[at])
        wait_bytes(like, self.send.at[at])
        slot, core = self.here.slot[1][0], self.here.core
        if at == 0:
            self.x2[0] = added([self.src[slot, core]] + [self.r1[k] for k in range(7)])
        if at == 1:
            self.out[slot, core] = added([self.x2[0], self.x2[1]])
        if at < 2:
            begin(self.phase(at + 1))


def layer_norm(x):
    centered = x - jnp.mean(x, axis=-1, keepdims=True)
    spread = jnp.mean(centered * centered, axis=-1, keepdims=True)
    rate = lax.rsqrt(spread + EPSILON)
    return centered * rate, rate


def layer_norm_back(cot, unit, rate):
    first = jnp.mean(cot, axis=-1, keepdims=True)
    second = jnp.mean(cot * unit, axis=-1, keepdims=True)
    return rate * (cot - first - unit * second)


def head_mask(head):
    lane = lax.broadcasted_iota(jnp.int32, (1, C), 1)
    return (lane >= head * 32) & (lane < head * 32 + 32)


def stacked(value):
    wide = value.astype(F32)
    parts = [jnp.where(head_mask(h), wide, 0.0).astype(BF16) for h in range(HEADS)]
    return jnp.concatenate(parts, axis=0)


def unstacked(value):
    total = jnp.where(head_mask(0), value[0:WIN], 0.0)
    for h in range(1, HEADS):
        total = total + jnp.where(head_mask(h), value[h * WIN : (h + 1) * WIN], 0.0)
    return total


def expand_bias(last_lat, table, columns, index_rows, lanes, tall_table, gathered, strips, scores):
    for head in range(HEADS):
        tall_table[head * LWIN : (head + 1) * LWIN, :] = table[head]
    for site in range(SITE):
        lev, a = site // WLAT, site % WLAT
        for other in range(WLEV):
            start = ((lev * WLEV + other) * WLAT + a) * RUN
            gathered[site * WH : (site + 1) * WH, other * RUN : (other + 1) * RUN] = tall_table[
                :, start : start + RUN
            ]
    moved = sum(dot(part, lanes[...]) for part in pieces(gathered[...], 3))
    rows = one_hot(columns[:, 1:2], WH * 2 * SITE, SITE * WH)
    moved = sum(dot(rows, part) for part in pieces(moved, 3))
    code = columns[:, 2:3]
    moved = jnp.where((code & 8) != 0, pltpu.roll(moved, LANES - SITE, 1), moved) * LOG2E
    seen = jnp.where((code & 4) != 0, 1, 0) + jnp.where(last_lat, 2, 0)
    apart = (code ^ index_rows[2:3, 0:LANES]) & seen
    strips[...] = jnp.where(apart != 0, MASKED, moved)

    def one(wh, carry):
        strip = strips[pl.ds(pl.multiple_of(wh * 2 * SITE, 8), 2 * SITE), :]
        start = lax.rem(wh, LWIN) * STACK + lax.div(wh, LWIN) * WIN
        for pair in range(WLON // 2):
            offset = (WLON - 2 - 2 * pair) * SITE
            scores[pl.ds(pl.multiple_of(start + pair * 24, 8), 24), :] = strip[
                :, offset : offset + WIN
            ]
        return carry

    lax.fori_loop(0, WH, one, 0)


def collapse_bias(first, last, scores, strips):
    def one(wh, carry):
        start = lax.rem(wh, LWIN) * STACK + lax.div(wh, LWIN) * WIN
        total = jnp.zeros((2 * SITE, LANES), F32)
        for pair in range(WLON // 2):
            offset = (WLON - 2 - 2 * pair) * SITE
            part = scores[pl.ds(pl.multiple_of(start + pair * 24, 8), 24), :]
            part = jnp.concatenate([part, jnp.zeros((2 * SITE, LANES - WIN), F32)], axis=1)
            total = total + (pltpu.roll(part, offset, 1) if offset else part)
        strips[pl.ds(pl.multiple_of(wh * 2 * SITE, 8), 2 * SITE), :] = total
        return carry

    lax.fori_loop(first, last, one, 0)


def join_strips(strips, columns, index_rows):
    total = strips[...]
    total = jnp.where((columns[:, 2:3] & 8) != 0, pltpu.roll(total, SITE, 1), total)
    rows = one_hot(index_rows[1:2, :], SITE * WH, WH * 2 * SITE)
    return sum(dot(rows, part) for part in pieces(total, 2))


def block_kernel(n_lon, n_lat, *refs):
    loaded = refs[:9]
    out_field, grad_field, qkv, proj, fc1, fc2, bias = refs[9:16]
    field, cot, w_qkv, w_proj, w_fc1, w_fc2, table, columns, index_rows, load_sem = refs[16:26]
    (
        out, e_out, l_out, b_out, sent, came, cot_sent, cot_came, back, halo_send, halo_recv,
        xw, uw, scores, normed, query, key, value, unit, rate, blended, normed_two, hidden,
        cot_first, cot_mid, cot_q, cot_k, cot_v, ow, gw, tall_table, gathered, strips, w3,
        places_in, places_out, lanes, slope, unit_two, rate_two,
    ) = refs[26:66]
    here = Here(n_lon, n_lat)
    early = PairSum(here, e_out, refs[66:74])
    late = WeightSum(here, l_out, refs[74:80])
    strip_sum = BiasSum(here, b_out, refs[80:85])

    loads = [
        pltpu.make_async_copy(src, dst, load_sem.at[i]) for i, (src, dst) in enumerate(zip(loaded, refs[16:25]))
    ]
    loads[0].start()
    greeted = here.greet()
    begin(loads[6:9])
    loads[0].wait()
    for index in range(3):
        for part, chunk in enumerate(split(field, index)):
            sent[part, index] = pack(chunk)
    greeted()
    inward = [
        halo(here, sent.at[i], came.at[i], halo_send.at[i], halo_recv.at[i], -1) for i in range(2)
    ]
    cot_inward = halo(here, cot_sent, cot_came, halo_send.at[2], halo_recv.at[2], -1)
    outward = [
        halo(here, back.at[i], out.at[i], halo_send.at[3 + i], halo_recv.at[3 + i], 1) for i in range(2)
    ]
    begin(inward[0])
    begin(inward[1])
    begin(loads[1:6])
    end(loads[6:9])
    lanes[...] = one_hot(columns[0:STRIP, 3:4], STRIP, LANES)
    last_lat = here.lat == n_lat - 1
    expand_bias(last_lat, table, columns, index_rows, lanes, tall_table, gathered, strips, scores)
    places_in[...] = one_hot(columns[0:PAIR, 0:1], PAIR, PAIR)
    places_out[...] = one_hot(index_rows[0:1, 0:PAIR], PAIR, PAIR)
    loads[1].wait()
    for index in range(3):
        for part, chunk in enumerate(split(cot, index)):
            cot_sent[index, part] = pack(chunk)
    own = [split(ref, 3) for ref in (field, cot)]
    loads[2].wait()
    for third in range(3):
        w3[third] = w_qkv[:, third * C : (third + 1) * C]

    def gather(kind, part):
        if kind:
            arrived = [cot_came[i, part] for i in range(1, 4)]
        else:
            arrived = [came[part, i] for i in range(1, 4)]
        parts = [own[kind][part]] + [unpack(value) for value in arrived]
        return dot(places_in[...], jnp.concatenate(parts, axis=0).astype(BF16)).astype(BF16)

    def scatter(kind, ref):
        for part in range(2):
            whole = dot(places_out[...], ref[part * PAIR : (part + 1) * PAIR, :])
            out[kind, 3, part] = pack(whole[:CHUNK])
            for i in range(1, 4):
                back[kind, i, part] = pack(whole[i * CHUNK : (i + 1) * CHUNK])
        begin(outward[kind])

    def places(w):
        return pl.ds(w * WIN, WIN), pl.ds(w * STACK, STACK)

    def attend(w):
        rows, tall = places(w)
        unit_x, rate_x = layer_norm(xw[rows, :].astype(F32))
        unit[rows, :] = unit_x
        rate[rows, :] = rate_x
        norm = unit_x.astype(BF16)
        normed[rows, :] = norm
        q = dot(norm, w3[0]).astype(BF16)
        k = dot(norm, w3[1]).astype(BF16)
        v = dot(norm, w3[2]).astype(BF16)
        query[rows, :] = q
        key[rows, :] = k
        value[rows, :] = v
        s = dot_nt(stacked(q), k) * (SCALE * LOG2E) + scores[tall, :]
        e = jnp.exp2(s - jnp.max(s, axis=-1, keepdims=True))
        p = e * (1.0 / jnp.sum(e, axis=-1, keepdims=True))
        scores[tall, :] = p
        blended[rows, :] = unstacked(dot(p.astype(BF16), v)).astype(BF16)

    def feed(w):
        rows = pl.ds(w * 2 * WIN, 2 * WIN)
        middle = xw[rows, :].astype(F32) + dot(blended[rows, :], w_proj[...])
        middle = middle.astype(BF16).astype(F32)
        unit_m, rate_m = layer_norm(middle)
        norm_m = unit_m.astype(BF16)
        normed_two[rows, :] = norm_m
        first = dot(norm_m, w_fc1[...])
        phi = 0.5 + 0.5 * lax.erf(first * math.sqrt(0.5))
        hid = (first * phi).astype(BF16)
        hidden[rows, :] = hid
        bell = jnp.exp2(first * first * (-0.5 * LOG2E)) * (1.0 / math.sqrt(2.0 * math.pi))
        slope[rows, :] = phi + first * bell
        unit_two[rows, :] = unit_m
        rate_two[rows, :] = rate_m
        ow[rows, :] = (middle + dot_nt(hid, w_fc2[...])).astype(BF16)

    def feed_back(w):
        rows = pl.ds(w * 2 * WIN, 2 * WIN)
        up = uw[rows, :]
        c_first = (dot(up, w_fc2[...]).astype(BF16).astype(F32) * slope[rows, :]).astype(BF16)
        cot_first[rows, :] = c_first
        c_norm = dot_nt(c_first, w_fc1[...]).astype(BF16).astype(F32)
        c_mid = layer_norm_back(c_norm, unit_two[rows, :], rate_two[rows, :]).astype(BF16).astype(F32)
        cot_mid[rows, :] = (up.astype(F32) + c_mid).astype(BF16)

    def backward(w):
        rows, tall = places(w)
        up = cot_mid[rows, :]
        c_blend = stacked(dot_nt(up, w_proj[...]).astype(BF16))
        p = scores[tall, :]
        c_p = dot_nt(c_blend, value[rows, :])
        c_s = p * (c_p - jnp.sum(p * c_p, axis=-1, keepdims=True))
        scores[tall, :] = c_s
        c_v = dot_tn(p.astype(BF16), c_blend).astype(BF16)
        narrow = c_s.astype(BF16)
        c_q = (unstacked(dot(narrow, key[rows, :])) * SCALE).astype(BF16)
        c_k = (dot_tn(narrow, stacked(query[rows, :])) * SCALE).astype(BF16)
        cot_q[rows, :] = c_q
        cot_k[rows, :] = c_k
        cot_v[rows, :] = c_v

    def inputs_back(w):
        rows = pl.ds(w * 2 * WIN, 2 * WIN)
        c_norm = dot_nt(cot_q[rows, :], w3[0]) + dot_nt(cot_k[rows, :], w3[1])
        c_norm = (c_norm + dot_nt(cot_v[rows, :], w3[2])).astype(BF16).astype(F32)
        c_x = layer_norm_back(c_norm, unit[rows, :], rate[rows, :]).astype(BF16)
        gw[rows, :] = (cot_mid[rows, :].astype(F32) + c_x.astype(F32)).astype(BF16)

    for part in range(2):
        end(inward[part])
        xw[part * PAIR : (part + 1) * PAIR, :] = gather(0, part)
        if not part:
            begin(cot_inward)
        attend(2 * part)
        attend(2 * part + 1)
    end(loads[3:6])
    feed(0)
    feed(1)
    end(cot_inward)
    for part in range(2):
        uw[part * PAIR : (part + 1) * PAIR, :] = gather(1, part)
        feed_back(part)
    early.put(dot_tn(normed_two[...], cot_first[...]), 0)
    early.put(dot_tn(uw[...], hidden[...]), 72)
    early.start()
    backward(0)
    backward(1)
    backward(2)
    early.step(0)
    backward(3)
    norm = normed[...]
    late.put(jnp.concatenate([dot_tn(norm, cot_q[...]), dot_tn(norm, cot_k[...])], axis=1), 0)
    c_proj = dot_tn(blended[...], cot_mid[...])
    late.put(jnp.concatenate([dot_tn(norm, cot_v[...]), c_proj], axis=1), 36)
    late.start()
    collapse_bias(0, WH, scores, strips)
    strip_sum.put(join_strips(strips, columns, index_rows))
    strip_sum.start()
    early.step(1)
    inputs_back(0)
    inputs_back(1)
    late.step(0)
    scatter(1, gw)
    scatter(0, ow)
    early.step(2)
    strip_sum.step(0)
    late.step(1)
    early.step(3)
    strip_sum.step(1)
    late.step(2)
    early.step(4)
    end(outward[1])
    for index in range(4):
        merge(grad_field, index, [unpack(out[1, index, part]) for part in range(2)])
    end(outward[0])
    for index in range(4):
        merge(out_field, index, [unpack(out[0, index, part]) for part in range(2)])
    strip_sum.step(2)
    finish_bias(strip_sum.get(), lanes, tall_table, bias)
    early.step(5)
    fc1[...] = joined(early.get()[:72], 6)
    fc2[...] = joined(early.get()[72:], 6)
    late.step(3)
    qkv[:, 0:384] = joined(tiles_of(l_out)[:36], 3)
    right = joined(tiles_of(l_out)[36:], 3)
    qkv[:, 384:576] = right[:, 0:C]
    proj[...] = right[:, C:]


def joined(tiles, columns):
    rows = len(tiles) // columns
    cols = [jnp.concatenate(tiles[c * rows : (c + 1) * rows], axis=0) for c in range(columns)]
    return jnp.concatenate(cols, axis=1).astype(F32)


def tiles_of(ref):
    n1 = ref.shape[3]
    return [ref[i // (8 * n1), i // (2 * n1) % RING, i // n1 % 2, i % n1] for i in range(24 * n1)]


def finish_bias(strip, lanes, tall_table, bias):
    runs = dot_nt(strip.astype(BF16), lanes[...])
    for site in range(SITE):
        lev, a = site // WLAT, site % WLAT
        for other in range(WLEV):
            start = ((lev * WLEV + other) * WLAT + a) * RUN
            tall_table[:, start : start + RUN] = runs[
                site * WH : (site + 1) * WH, other * RUN : (other + 1) * RUN
            ]
    for head in range(HEADS):
        bias[head] = tall_table[head * LWIN : (head + 1) * LWIN, :]


def finish_kernel(*refs):
    count = len(refs) // 2
    copies = [pltpu.make_async_copy(refs[i], refs[count + i], refs[-1].at[i]) for i in range(count)]
    begin(copies)
    end(copies)


def per_device(n_lon, n_lat, field, w_qkv, w_proj, w_fc1, w_fc2, bias_table, cotangent):
    vmem, hbm = pl.BlockSpec(memory_space=pltpu.VMEM), pl.BlockSpec(memory_space=pltpu.HBM)
    shape = jax.ShapeDtypeStruct
    dma = pltpu.SemaphoreType.DMA
    rows = row_places()
    columns = columns_of(token_places(), rows, row_codes(), lane_places())
    index_rows = columns_of(token_places(), rows, lane_codes()).T.copy()
    inputs = (
        field, cotangent, w_qkv, w_proj, w_fc1, w_fc2.T, bias_table[0].transpose(1, 0, 2), columns, index_rows
    )
    inputs = [pltpu.with_memory_space_constraint(jnp.asarray(a), pltpu.HBM) for a in inputs]
    tile = shape((WLON, WLAT, LEV, C), BF16)
    outputs = (
        tile,
        tile,
        shape((C, 3 * C), F32),
        shape((C, C), F32),
        shape((C, HIDDEN), F32),
        shape((C, HIDDEN), F32),
        shape((HEADS, LWIN, POS), F32),
    )
    wide = lambda dtype, n=1: [pltpu.VMEM((TOK, C), dtype)] * n
    results = pl.pallas_call(
        functools.partial(block_kernel, n_lon, n_lat),
        out_shape=outputs,
        in_specs=[hbm] * len(inputs),
        out_specs=[vmem] * len(outputs),
        scratch_shapes=[
            *[pltpu.VMEM(a.shape, a.dtype) for a in inputs],
            dma((len(inputs),)),
            pltpu.VMEM((2, 4, 2, PACKED, 128), BF16),
            room(2, 3, RING, E_TILES // 24),
            room(3, RING, 2, L_TILES // 24),
            room(RING, 2, B_TILES // 8),
            pltpu.VMEM((2, 3, PACKED, 128), BF16),
            pltpu.VMEM((2, 4, PACKED, 128), BF16),
            pltpu.VMEM((3, 2, PACKED, 128), BF16),
            pltpu.VMEM((4, 2, PACKED, 128), BF16),
            pltpu.VMEM((2, 4, 2, PACKED, 128), BF16),
            dma((5, 3)),
            dma((5, 3)),
            *wide(BF16, 2),
            pltpu.VMEM((LWIN * STACK, WIN), F32),
            *wide(BF16, 4),
            *wide(F32),
            pltpu.VMEM((TOK, 1), F32),
            *wide(BF16, 2),
            pltpu.VMEM((TOK, HIDDEN), BF16),
            pltpu.VMEM((TOK, HIDDEN), BF16),
            *wide(BF16, 6),
            pltpu.VMEM((WH, POS), F32),
            pltpu.VMEM((SITE * WH, STRIP), F32),
            pltpu.VMEM((WH * 2 * SITE, LANES), F32),
            pltpu.VMEM((3, C, C), BF16),
            pltpu.VMEM((PAIR, PAIR), BF16),
            pltpu.VMEM((PAIR, PAIR), BF16),
            pltpu.VMEM((STRIP, LANES), BF16),
            pltpu.VMEM((TOK, HIDDEN), F32),
            *wide(F32),
            pltpu.VMEM((TOK, 1), F32),
            *PairSum.scratch(E_TILES),
            *WeightSum.scratch(L_TILES),
            *BiasSum.scratch(),
        ],
        compiler_params=pltpu.CompilerParams(
            vmem_limit_bytes=VMEM_LIMIT, collective_id=0, has_side_effects=True
        ),
        name="block",
    )(*inputs)
    *results, fc2, bias = pl.pallas_call(
        finish_kernel,
        out_shape=outputs,
        in_specs=[vmem] * len(outputs),
        out_specs=[hbm] * len(outputs),
        scratch_shapes=[dma((len(outputs),))],
        compiler_params=pltpu.CompilerParams(vmem_limit_bytes=VMEM_LIMIT),
        name="finish",
    )(*results)
    return (*results, fc2.T, bias.transpose(1, 0, 2)[None])


def solution(mesh):
    whole, tiles, banded = P(), P("lon", "lat", None, None), P("lat", None, None, None)
    return jax.shard_map(
        functools.partial(per_device, mesh.shape["lon"], mesh.shape["lat"]),
        mesh=mesh,
        in_specs=(tiles, whole, whole, whole, whole, banded, tiles),
        out_specs=(tiles, tiles, whole, whole, whole, whole, banded),
        check_vma=False,
    )
```

```python
import functools
import math

import jax
import jax.numpy as jnp
import numpy as np
from jax import lax
from jax.experimental import pallas as pl
from jax.experimental.pallas import tpu as pltpu
from jax.sharding import PartitionSpec as P

C = 192
HEADS = 6
HIDDEN = 768
LEV = 8
WLON = 12
WLAT = 6
WLEV = 2
LWIN = LEV // WLEV
WH = LWIN * HEADS
WIN = WLEV * WLAT * WLON
TOK = LWIN * WIN
QUAD = TOK // 4
SITE = WLEV * WLAT
SHIFTS = 2 * WLON - 1
STRIP = SHIFTS * SITE
POS = WLEV * WLEV * WLAT * WLAT * SHIFTS
RUN = WLAT * SHIFTS
LANES = 384
STACK = HEADS * WIN
EPSILON = 1e-05
MASKED = -1000000000.0
LOG2E = math.log2(math.e)
SCALE = 1.0 / math.sqrt(C // HEADS)
RING = 4
E_TILES = 144
L_TILES = 72
B_TILES = 40
B_LEFT = STRIP - 256
B_ROWS = 48
CHUNK = QUAD // 2
PAIR = 4 * CHUNK
PACKED = 112
TILE = (16, 128)
BF16 = jnp.bfloat16
F32 = jnp.float32
MESH = pl.DeviceIdType.MESH
VMEM_LIMIT = 30 * 1024 * 1024


def token_places():
    w, o, lev, a = np.meshgrid(
        np.arange(2), np.arange(WLON), np.arange(WLEV), np.arange(WLAT), indexing="ij"
    )
    site = (o % 6) * 3 + a % 3
    row = (site % 9) * 8 + (site // 9) * 4 + 2 * w + lev
    return (((o // 6) * 2 + a // 3) * CHUNK + row).reshape(PAIR).astype(np.int32)


def lane_places():
    lev, a, d = np.meshgrid(np.arange(WLEV), np.arange(WLAT), np.arange(SHIFTS), indexing="ij")
    return ((SHIFTS - 1 - d) * SITE + lev * WLAT + a).reshape(STRIP).astype(np.int32)


def row_codes():
    lev, a, _, w = np.meshgrid(
        np.arange(WLEV), np.arange(WLAT), np.arange(HEADS), np.arange(LWIN), indexing="ij"
    )
    code = lev + 2 * (a >= WLAT // 2) + 4 * (w == LWIN - 1)
    return code.reshape(SITE * WH).astype(np.int32)


def lane_codes():
    site = np.arange(LANES) % SITE
    return (site // WLAT + 2 * (site % WLAT >= WLAT // 2)).astype(np.int32)


def columns_of(*arrays):
    made = np.zeros((TOK, 8), np.int32)
    for i, array in enumerate(arrays):
        made[: len(array), i] = array
    return made


def dot(a, b):
    return jnp.dot(a, b, preferred_element_type=F32)


def dot_nt(a, b):
    return lax.dot_general(a, b, (((1,), (1,)), ((), ())), preferred_element_type=F32)


def dot_tn(a, b):
    return lax.dot_general(a, b, (((0,), (0,)), ((), ())), preferred_element_type=F32)


def one_hot(places, rows, cols):
    along = 1 if places.shape[1] == 1 else 0
    index = lax.broadcasted_iota(jnp.int32, (rows, cols), along)
    return jnp.where(index == places, 1.0, 0.0).astype(BF16)


def pieces(value, count):
    found = []
    for _ in range(count):
        part = value.astype(BF16)
        found.append(part)
        value = value - part.astype(F32)
    return found


def split(ref, index):
    part = ref[pl.ds((index // 2) * 6, 6), pl.ds((index % 2) * 3, 3)]
    part = pltpu.roll(part.astype(F32).reshape(18, LEV, C), LEV - 1, 1)
    low, high = part[:9], part[9:]
    upper = lax.broadcasted_iota(jnp.int32, low.shape, 1) < LEV // 2
    first = jnp.where(upper, low, pltpu.roll(high, LEV // 2, 1))
    second = jnp.where(upper, pltpu.roll(low, LEV // 2, 1), high)
    return first.reshape(CHUNK, C), second.reshape(CHUNK, C)


def merge(ref, index, chunks):
    first, second = (chunk.reshape(9, LEV, C) for chunk in chunks)
    upper = lax.broadcasted_iota(jnp.int32, first.shape, 1) < LEV // 2
    low = jnp.where(upper, first, pltpu.roll(second, LEV // 2, 1))
    high = jnp.where(upper, pltpu.roll(first, LEV // 2, 1), second)
    part = pltpu.roll(jnp.concatenate([low, high], axis=0), 1, 1)
    ref[pl.ds((index // 2) * 6, 6), pl.ds((index % 2) * 3, 3)] = part.reshape(6, 3, LEV, C).astype(BF16)


def pack(value):
    rest = jnp.concatenate([value[:40, 128:], value[32:, 128:]], axis=1)
    return jnp.concatenate([value[:, :128], rest], axis=0).astype(BF16)


def unpack(value):
    wide = value.astype(F32)
    rest = wide[CHUNK:]
    right = jnp.concatenate([rest[:, :64], rest[8:, 64:]], axis=0)
    return jnp.concatenate([wide[:CHUNK], right], axis=1)


def place_of(lon, lat):
    x = lax.rem(lat, 2) * 2 + lax.div(lon, 8)
    return (x, lax.rem(lax.div(lon, 2), RING), lax.div(lat, 2)), lax.rem(lon, 2)


def device_at(chip, core):
    x, y, z = chip
    return ((lax.rem(x, 2) * RING + y) * 2 + core, z * 2 + lax.div(x, 2))


def moved(chip, axis, step):
    return tuple(lax.rem(c + step, RING) if i == axis else c for i, c in enumerate(chip))


def remote(src, dst, send, recv, device):
    return pltpu.make_async_remote_copy(
        src_ref=src, dst_ref=dst, send_sem=send, recv_sem=recv, device_id=device, device_id_type=MESH
    )


class Here:
    def __init__(self, n_lon, n_lat):
        self.lon, self.lat = lax.axis_index("lon"), lax.axis_index("lat")
        self.chip, self.core = place_of(self.lon, self.lat)
        self.sibling = (self.lon + 1 - 2 * self.core, self.lat)
        self.slot = [[lax.rem(c + k, RING) for k in range(RING)] for c in self.chip]
        chips = [[moved(self.chip, axis, k) for k in range(RING)] for axis in range(3)]
        self.along = [[device_at(chip, self.core) for chip in ring] for ring in chips]
        other = 1 - self.core
        self.eight = []
        for axis in range(3):
            found = []
            for k in range(RING):
                if k:
                    found.append((self.along[axis][k], self.slot[axis][k], self.core))
                found.append((device_at(chips[axis][k], other), self.slot[axis][k], other))
            self.eight.append(found)
        self.facing = (lax.rem(self.lon + 8, 16), self.lat)
        self.across = {}
        for step in (-1, 1):
            to_lon = lax.rem(self.lon + n_lon + step, n_lon)
            to_lat = lax.rem(self.lat + n_lat + step, n_lat)
            self.across[step] = ((to_lon, to_lat), (to_lon, self.lat), (self.lon, to_lat))

    def greet(self):
        others = [*self.across[-1], *self.across[1], self.sibling]
        for axis in range(3):
            others += [device for device, _, _ in self.eight[axis][1:]]
        barrier = pltpu.get_barrier_semaphore()
        for device in others:
            pl.semaphore_signal(barrier, inc=1, device_id=device, device_id_type=MESH)
        return lambda: pl.semaphore_wait(barrier, len(others))


def halo(here, source, target, send, recv, step):
    copies = []
    for index in range(3):
        src = index if step < 0 else 3 - index
        device = here.across[step][index]
        copies.append(remote(source.at[src], target.at[3 - src], send.at[index], recv.at[index], device))
    return copies


def begin(copies):
    for copy in copies:
        copy.start()


def end(copies):
    for copy in copies:
        copy.wait()


def wait_bytes(like, sem):
    pltpu.make_async_copy(like, like, sem).wait()


def room(*dims):
    return pltpu.VMEM((*dims, *TILE), BF16)


def tiles_in(block):
    narrow = block.astype(BF16)
    for c in range(block.shape[1] // 128):
        for r in range(block.shape[0] // 16):
            yield narrow[r * 16 : (r + 1) * 16, c * 128 : (c + 1) * 128]


def added(terms):
    total = terms[0].astype(F32)
    for term in terms[1:]:
        total = total + term.astype(F32)
    return total.astype(BF16)


class WeightSum:
    def __init__(self, here, out, refs):
        self.here, self.out = here, out
        self.src, self.r1, self.x2, self.x3, self.send, self.recv = refs

    @staticmethod
    def scratch(tiles):
        n1 = tiles // 24
        dma = pltpu.SemaphoreType.DMA
        return [room(3, RING, 2, n1), room(7, 3, n1), room(3, RING, n1), room(3, RING, n1), dma((4,)), dma((4,))]

    def put(self, block, first):
        n1 = self.src.shape[3]
        for at, tile in enumerate(tiles_in(block), first):
            self.src[at // (8 * n1), at // (2 * n1) % RING, at // n1 % 2, at % n1] = tile

    def phase(self, at):
        here, made = self.here, []
        sems = self.send.at[at], self.recv.at[at]
        for t in range(3):
            if at in (0, 3):
                mine = self.out.at[t, here.slot[t][0], here.core]
                for k, (device, slot, core) in enumerate(here.eight[t]):
                    if at == 0:
                        made.append(remote(self.src.at[t, slot, core], self.r1.at[k, t], *sems, device))
                    else:
                        made.append(remote(mine, mine, *sems, device))
            else:
                axis = (t + at) % 3
                mine = (self.x2 if at == 1 else self.x3).at[t, here.slot[axis][0]]
                made += [remote(mine, mine, *sems, here.along[axis][k]) for k in range(1, RING)]
        return made

    def start(self):
        begin(self.phase(0))

    def step(self, at):
        like = self.r1 if at in (0, 3) else self.r1.at[pl.ds(0, 3)]
        wait_bytes(like, self.recv.at[at])
        wait_bytes(like, self.send.at[at])
        core = self.here.core
        for t in range(3):
            one, two, three = (self.here.slot[(t + i) % 3][0] for i in range(3))
            if at == 0:
                self.x2[t, two] = added([self.src[t, one, core]] + [self.r1[k, t] for k in range(7)])
            if at == 1:
                self.x3[t, three] = added([self.x2[t, k] for k in range(RING)])
            if at == 2:
                self.out[t, one, core] = added([self.x3[t, k] for k in range(RING)])
        if at < 3:
            begin(self.phase(at + 1))


class PairSum:
    def __init__(self, here, out, refs):
        self.here, self.out = here, out
        self.src, self.other, self.a1, self.r1, self.x2, self.x3, self.send, self.recv = refs

    @staticmethod
    def scratch(tiles):
        n1 = tiles // 24
        dma = pltpu.SemaphoreType.DMA
        return [
            room(2, tiles // 2), room(tiles // 2),
            room(3, RING, n1), room(3, RING - 1, n1), room(3, RING, n1), room(3, RING, n1),
            dma((6,)), dma((6,)),
        ]

    def put(self, block, first):
        each = self.src.shape[1]
        for at, tile in enumerate(tiles_in(block), first):
            self.src[at // each, at % each] = tile

    def get(self):
        n1 = self.a1.shape[2]
        return [self.out[i // (12 * n1), i // (4 * n1) % 3, i // n1 % 4, i % n1] for i in range(24 * n1)]

    def copies(self, at, axis_of, source, target):
        made = []
        for t in range(3):
            axis = (t + axis_of) % 3
            slot = self.here.slot[axis]
            for k in range(1, RING):
                made.append(
                    remote(
                        source(t, slot[k], slot[0]), target(t, k - 1, slot[0]),
                        self.send.at[at], self.recv.at[at], self.here.along[axis][k],
                    )
                )
        return made

    def phase(self, at):
        core = self.here.core
        if at == 0:
            return [remote(self.src.at[1 - core], self.other, self.send.at[0], self.recv.at[0], self.here.sibling)]
        if at == 1:
            return self.copies(1, 0, lambda t, to, me: self.a1.at[t, to], lambda t, k, me: self.r1.at[t, k])
        if at == 2:
            return self.copies(2, 1, lambda t, to, me: self.x2.at[t, me], lambda t, k, me: self.x2.at[t, me])
        if at == 3:
            return self.copies(3, 2, lambda t, to, me: self.x3.at[t, me], lambda t, k, me: self.x3.at[t, me])
        if at == 4:
            out = self.out.at[core]
            return self.copies(4, 0, lambda t, to, me: out.at[t, me], lambda t, k, me: out.at[t, me])
        return [remote(self.out.at[core], self.out.at[core], self.send.at[5], self.recv.at[5], self.here.sibling)]

    def start(self):
        begin(self.phase(0))

    def step(self, at):
        like = self.other if at in (0, 5) else self.r1
        wait_bytes(like, self.recv.at[at])
        wait_bytes(like, self.send.at[at])
        core = self.here.core
        if at == 0:
            total = self.src[core].astype(F32) + self.other[...].astype(F32)
            self.a1[...] = total.astype(BF16).reshape(self.a1.shape)
        for t in range(3):
            one, two, three = (self.here.slot[(t + i) % 3][0] for i in range(3))
            if at == 1:
                total = self.a1[t, one].astype(F32)
                for k in range(RING - 1):
                    total = total + self.r1[t, k].astype(F32)
                self.x2[t, two] = total.astype(BF16)
            if at in (2, 3):
                came = self.x2 if at == 2 else self.x3
                total = came[t, 0].astype(F32)
                for k in range(1, RING):
                    total = total + came[t, k].astype(F32)
                if at == 2:
                    self.x3[t, three] = total.astype(BF16)
                else:
                    self.out[core, t, one] = total.astype(BF16)
        if at < 5:
            begin(self.phase(at + 1))


class BiasSum:
    def __init__(self, here, out, refs):
        self.here, self.out = here, out
        self.src, self.r1, self.x2, self.send, self.recv = refs

    @staticmethod
    def scratch():
        each = B_TILES // 8
        dma = pltpu.SemaphoreType.DMA
        return [room(RING, 2, each), room(7, each), room(2, each), dma((3,)), dma((3,))]

    def put(self, block):
        each = B_TILES // 8
        last = block[:, 256:]
        shared = last[0:B_ROWS]
        for g in range(1, 288 // B_ROWS):
            shared = shared + pltpu.roll(last[g * B_ROWS : (g + 1) * B_ROWS], g * B_LEFT, 1)
        tiles = [*tiles_in(block[:, :256]), *tiles_in(shared), jnp.zeros(TILE, BF16)]
        for at, tile in enumerate(tiles):
            self.src[at // (2 * each), at // each % 2, at % each] = tile

    def get(self):
        each = B_TILES // 8
        tiles = [self.out[at // (2 * each), at // each % 2, at % each] for at in range(B_TILES)]
        first = joined(tiles[:36], 2)
        shared = joined(tiles[36:39], 1)
        last = [shared]
        for g in range(1, 288 // B_ROWS):
            last.append(pltpu.roll(shared, 128 - g * B_LEFT, 1))
        return jnp.concatenate([first, jnp.concatenate(last, axis=0)], axis=1)

    def phase(self, at):
        here, made = self.here, []
        sems = self.send.at[at], self.recv.at[at]
        if at == 1:
            return [remote(self.x2.at[0], self.x2.at[1], *sems, here.facing)]
        mine = self.out.at[here.slot[1][0], here.core]
        for k, (device, slot, core) in enumerate(here.eight[1]):
            if at == 0:
                made.append(remote(self.src.at[slot, core], self.r1.at[k], *sems, device))
            else:
                made.append(remote(mine, mine, *sems, device))
        return made

    def start(self):
        begin(self.phase(0))

    def step(self, at):
        like = self.x2.at[1] if at == 1 else self.r1
        wait_bytes(like, self.recv.at[at])
        wait_bytes(like, self.send.at[at])
        slot, core = self.here.slot[1][0], self.here.core
        if at == 0:
            self.x2[0] = added([self.src[slot, core]] + [self.r1[k] for k in range(7)])
        if at == 1:
            self.out[slot, core] = added([self.x2[0], self.x2[1]])
        if at < 2:
            begin(self.phase(at + 1))


def layer_norm(x):
    centered = x - jnp.mean(x, axis=-1, keepdims=True)
    spread = jnp.mean(centered * centered, axis=-1, keepdims=True)
    rate = lax.rsqrt(spread + EPSILON)
    return centered * rate, rate


def layer_norm_back(cot, unit, rate):
    first = jnp.mean(cot, axis=-1, keepdims=True)
    second = jnp.mean(cot * unit, axis=-1, keepdims=True)
    return rate * (cot - first - unit * second)


def head_mask(head):
    lane = lax.broadcasted_iota(jnp.int32, (1, C), 1)
    return (lane >= head * 32) & (lane < head * 32 + 32)


def stacked(value):
    wide = value.astype(F32)
    parts = [jnp.where(head_mask(h), wide, 0.0).astype(BF16) for h in range(HEADS)]
    return jnp.concatenate(parts, axis=0)


def unstacked(value):
    total = jnp.where(head_mask(0), value[0:WIN], 0.0)
    for h in range(1, HEADS):
        total = total + jnp.where(head_mask(h), value[h * WIN : (h + 1) * WIN], 0.0)
    return total


def expand_bias(last_lat, table, columns, index_rows, lanes, tall_table, gathered, strips, scores):
    for head in range(HEADS):
        tall_table[head * LWIN : (head + 1) * LWIN, :] = table[head]
    for site in range(SITE):
        lev, a = site // WLAT, site % WLAT
        for other in range(WLEV):
            start = ((lev * WLEV + other) * WLAT + a) * RUN
            gathered[site * WH : (site + 1) * WH, other * RUN : (other + 1) * RUN] = tall_table[
                :, start : start + RUN
            ]
    strip = sum(dot(part, lanes[...]) for part in pieces(gathered[...], 3)) * LOG2E
    code = columns[0 : SITE * WH, 2:3]
    seen = jnp.where((code & 4) != 0, 1, 0) + jnp.where(last_lat, 2, 0)
    apart = (code ^ index_rows[2:3, 0:LANES]) & seen
    strip = jnp.where(apart != 0, MASKED, strip)
    for c in range(LANES // 128):
        strips[c] = strip[:, c * 128 : (c + 1) * 128]

    def one(wh, carry):
        odd = jnp.concatenate([strips[c, pl.ds(wh, SITE, WH), :] for c in range(LANES // 128)], axis=1)
        both = jnp.concatenate([pltpu.roll(odd, LANES - SITE, 1), odd], axis=0)
        start = lax.rem(wh, LWIN) * STACK + lax.div(wh, LWIN) * WIN
        for pair in range(WLON // 2):
            offset = (WLON - 2 - 2 * pair) * SITE
            scores[pl.ds(pl.multiple_of(start + pair * 24, 8), 24), :] = both[:, offset : offset + WIN]
        return carry

    lax.fori_loop(0, WH, one, 0)


def collapse_bias(scores, strips):
    def one(wh, carry):
        start = lax.rem(wh, LWIN) * STACK + lax.div(wh, LWIN) * WIN
        total = jnp.zeros((2 * SITE, LANES), F32)
        for pair in range(WLON // 2):
            offset = (WLON - 2 - 2 * pair) * SITE
            part = scores[pl.ds(pl.multiple_of(start + pair * 24, 8), 24), :]
            part = jnp.concatenate([part, jnp.zeros((2 * SITE, LANES - WIN), F32)], axis=1)
            total = total + (pltpu.roll(part, offset, 1) if offset else part)
        total = pltpu.roll(total[:SITE], SITE, 1) + total[SITE:]
        for c in range(LANES // 128):
            strips[c, pl.ds(wh, SITE, WH), :] = total[:, c * 128 : (c + 1) * 128]
        return carry

    lax.fori_loop(0, WH, one, 0)


def block_kernel(n_lon, n_lat, *refs):
    loaded = refs[:9]
    out_field, grad_field, qkv, proj, fc1, fc2, bias = refs[9:16]
    field, cot, w_qkv, w_proj, w_fc1, w_fc2, table, columns, index_rows, load_sem = refs[16:26]
    (
        out, e_out, l_out, b_out, sent, came, cot_sent, cot_came, back, halo_send, halo_recv,
        xw, uw, scores, normed, query, key, value, unit, rate, blended, normed_two, hidden,
        cot_first, cot_mid, cot_q, cot_k, cot_v, ow, gw, tall_table, gathered, strips, w3,
        places_in, places_out, lanes, slope, unit_two, rate_two,
    ) = refs[26:66]
    here = Here(n_lon, n_lat)
    early = PairSum(here, e_out, refs[66:74])
    late = WeightSum(here, l_out, refs[74:80])
    strip_sum = BiasSum(here, b_out, refs[80:85])

    loads = [
        pltpu.make_async_copy(src, dst, load_sem.at[i]) for i, (src, dst) in enumerate(zip(loaded, refs[16:25]))
    ]
    loads[0].start()
    greeted = here.greet()
    begin(loads[6:9])
    loads[0].wait()
    for index in range(3):
        for part, chunk in enumerate(split(field, index)):
            sent[part, index] = pack(chunk)
    greeted()
    inward = [
        halo(here, sent.at[i], came.at[i], halo_send.at[i], halo_recv.at[i], -1) for i in range(2)
    ]
    cot_inward = halo(here, cot_sent, cot_came, halo_send.at[2], halo_recv.at[2], -1)
    outward = [
        halo(here, back.at[i], out.at[i], halo_send.at[3 + i], halo_recv.at[3 + i], 1) for i in range(2)
    ]
    begin(inward[0])
    begin(inward[1])
    begin(loads[1:6])
    end(loads[6:9])
    lanes[...] = one_hot(columns[0:STRIP, 3:4], STRIP, LANES)
    last_lat = here.lat == n_lat - 1
    expand_bias(last_lat, table, columns, index_rows, lanes, tall_table, gathered, strips, scores)
    places_in[...] = one_hot(columns[0:PAIR, 0:1], PAIR, PAIR)
    places_out[...] = one_hot(index_rows[0:1, 0:PAIR], PAIR, PAIR)
    loads[1].wait()
    for index in range(3):
        for part, chunk in enumerate(split(cot, index)):
            cot_sent[index, part] = pack(chunk)
    own = [split(ref, 3) for ref in (field, cot)]
    loads[2].wait()
    for third in range(3):
        w3[third] = w_qkv[:, third * C : (third + 1) * C]

    def gather(kind, part):
        if kind:
            arrived = [cot_came[i, part] for i in range(1, 4)]
        else:
            arrived = [came[part, i] for i in range(1, 4)]
        parts = [own[kind][part]] + [unpack(value) for value in arrived]
        return dot(places_in[...], jnp.concatenate(parts, axis=0).astype(BF16)).astype(BF16)

    def scatter(kind, ref):
        for part in range(2):
            whole = dot(places_out[...], ref[part * PAIR : (part + 1) * PAIR, :])
            out[kind, 3, part] = pack(whole[:CHUNK])
            for i in range(1, 4):
                back[kind, i, part] = pack(whole[i * CHUNK : (i + 1) * CHUNK])
        begin(outward[kind])

    def places(w):
        return pl.ds(w * WIN, WIN), pl.ds(w * STACK, STACK)

    def attend(w):
        rows, tall = places(w)
        unit_x, rate_x = layer_norm(xw[rows, :].astype(F32))
        unit[rows, :] = unit_x
        rate[rows, :] = rate_x
        norm = unit_x.astype(BF16)
        normed[rows, :] = norm
        q = dot(norm, w3[0]).astype(BF16)
        k = dot(norm, w3[1]).astype(BF16)
        v = dot(norm, w3[2]).astype(BF16)
        query[rows, :] = q
        key[rows, :] = k
        value[rows, :] = v
        s = dot_nt(stacked(q), k) * (SCALE * LOG2E) + scores[tall, :]
        e = jnp.exp2(s - jnp.max(s, axis=-1, keepdims=True))
        p = e * (1.0 / jnp.sum(e, axis=-1, keepdims=True))
        scores[tall, :] = p
        blended[rows, :] = unstacked(dot(p.astype(BF16), v)).astype(BF16)

    def feed(w):
        rows = pl.ds(w * 2 * WIN, 2 * WIN)
        middle = xw[rows, :].astype(F32) + dot(blended[rows, :], w_proj[...])
        middle = middle.astype(BF16).astype(F32)
        unit_m, rate_m = layer_norm(middle)
        norm_m = unit_m.astype(BF16)
        normed_two[rows, :] = norm_m
        first = dot(norm_m, w_fc1[...])
        phi = 0.5 + 0.5 * lax.erf(first * math.sqrt(0.5))
        hid = (first * phi).astype(BF16)
        hidden[rows, :] = hid
        bell = jnp.exp2(first * first * (-0.5 * LOG2E)) * (1.0 / math.sqrt(2.0 * math.pi))
        slope[rows, :] = phi + first * bell
        unit_two[rows, :] = unit_m
        rate_two[rows, :] = rate_m
        ow[rows, :] = (middle + dot_nt(hid, w_fc2[...])).astype(BF16)

    def feed_back(w):
        rows = pl.ds(w * 2 * WIN, 2 * WIN)
        up = uw[rows, :]
        c_first = (dot(up, w_fc2[...]).astype(BF16).astype(F32) * slope[rows, :]).astype(BF16)
        cot_first[rows, :] = c_first
        c_norm = dot_nt(c_first, w_fc1[...]).astype(BF16).astype(F32)
        c_mid = layer_norm_back(c_norm, unit_two[rows, :], rate_two[rows, :]).astype(BF16).astype(F32)
        cot_mid[rows, :] = (up.astype(F32) + c_mid).astype(BF16)

    def backward(w):
        rows, tall = places(w)
        up = cot_mid[rows, :]
        c_blend = stacked(dot_nt(up, w_proj[...]).astype(BF16))
        p = scores[tall, :]
        c_p = dot_nt(c_blend, value[rows, :])
        c_s = p * (c_p - jnp.sum(p * c_p, axis=-1, keepdims=True))
        scores[tall, :] = c_s
        c_v = dot_tn(p.astype(BF16), c_blend).astype(BF16)
        narrow = c_s.astype(BF16)
        c_q = (unstacked(dot(narrow, key[rows, :])) * SCALE).astype(BF16)
        c_k = (dot_tn(narrow, stacked(query[rows, :])) * SCALE).astype(BF16)
        cot_q[rows, :] = c_q
        cot_k[rows, :] = c_k
        cot_v[rows, :] = c_v

    def inputs_back(w):
        rows = pl.ds(w * 2 * WIN, 2 * WIN)
        c_norm = dot_nt(cot_q[rows, :], w3[0]) + dot_nt(cot_k[rows, :], w3[1])
        c_norm = (c_norm + dot_nt(cot_v[rows, :], w3[2])).astype(BF16).astype(F32)
        c_x = layer_norm_back(c_norm, unit[rows, :], rate[rows, :]).astype(BF16)
        gw[rows, :] = (cot_mid[rows, :].astype(F32) + c_x.astype(F32)).astype(BF16)

    for part in range(2):
        end(inward[part])
        xw[part * PAIR : (part + 1) * PAIR, :] = gather(0, part)
        if not part:
            begin(cot_inward)
        attend(2 * part)
        attend(2 * part + 1)
    end(loads[3:6])
    feed(0)
    feed(1)
    end(cot_inward)
    for part in range(2):
        uw[part * PAIR : (part + 1) * PAIR, :] = gather(1, part)
        feed_back(part)
    early.put(dot_tn(normed_two[...], cot_first[...]), 0)
    early.put(dot_tn(uw[...], hidden[...]), 72)
    early.start()
    backward(0)
    backward(1)
    backward(2)
    early.step(0)
    backward(3)
    norm = normed[...]
    late.put(jnp.concatenate([dot_tn(norm, cot_q[...]), dot_tn(norm, cot_k[...])], axis=1), 0)
    c_proj = dot_tn(blended[...], cot_mid[...])
    late.put(jnp.concatenate([dot_tn(norm, cot_v[...]), c_proj], axis=1), 36)
    late.start()
    collapse_bias(scores, strips)
    strip_sum.put(jnp.concatenate([strips[c] for c in range(LANES // 128)], axis=1))
    strip_sum.start()
    early.step(1)
    inputs_back(0)
    inputs_back(1)
    late.step(0)
    scatter(1, gw)
    scatter(0, ow)
    early.step(2)
    strip_sum.step(0)
    late.step(1)
    early.step(3)
    strip_sum.step(1)
    late.step(2)
    early.step(4)
    end(outward[1])
    for index in range(4):
        merge(grad_field, index, [unpack(out[1, index, part]) for part in range(2)])
    end(outward[0])
    for index in range(4):
        merge(out_field, index, [unpack(out[0, index, part]) for part in range(2)])
    strip_sum.step(2)
    finish_bias(strip_sum.get(), lanes, tall_table, bias)
    early.step(5)
    fc1[...] = joined(early.get()[:72], 6)
    fc2[...] = joined(early.get()[72:], 6)
    late.step(3)
    qkv[:, 0:384] = joined(tiles_of(l_out)[:36], 3)
    right = joined(tiles_of(l_out)[36:], 3)
    qkv[:, 384:576] = right[:, 0:C]
    proj[...] = right[:, C:]


def joined(tiles, columns):
    rows = len(tiles) // columns
    cols = [jnp.concatenate(tiles[c * rows : (c + 1) * rows], axis=0) for c in range(columns)]
    return jnp.concatenate(cols, axis=1).astype(F32)


def tiles_of(ref):
    n1 = ref.shape[3]
    return [ref[i // (8 * n1), i // (2 * n1) % RING, i // n1 % 2, i % n1] for i in range(24 * n1)]


def finish_bias(strip, lanes, tall_table, bias):
    runs = dot_nt(strip.astype(BF16), lanes[...])
    for site in range(SITE):
        lev, a = site // WLAT, site % WLAT
        for other in range(WLEV):
            start = ((lev * WLEV + other) * WLAT + a) * RUN
            tall_table[:, start : start + RUN] = runs[
                site * WH : (site + 1) * WH, other * RUN : (other + 1) * RUN
            ]
    for head in range(HEADS):
        bias[head] = tall_table[head * LWIN : (head + 1) * LWIN, :]


def finish_kernel(*refs):
    count = len(refs) // 2
    copies = [pltpu.make_async_copy(refs[i], refs[count + i], refs[-1].at[i]) for i in range(count)]
    begin(copies)
    end(copies)


def per_device(n_lon, n_lat, field, w_qkv, w_proj, w_fc1, w_fc2, bias_table, cotangent):
    vmem, hbm = pl.BlockSpec(memory_space=pltpu.VMEM), pl.BlockSpec(memory_space=pltpu.HBM)
    shape = jax.ShapeDtypeStruct
    dma = pltpu.SemaphoreType.DMA
    columns = columns_of(token_places(), [], row_codes(), lane_places())
    index_rows = columns_of(token_places(), [], lane_codes()).T.copy()
    inputs = (
        field, cotangent, w_qkv, w_proj, w_fc1, w_fc2.T, bias_table[0].transpose(1, 0, 2), columns, index_rows
    )
    inputs = [pltpu.with_memory_space_constraint(jnp.asarray(a), pltpu.HBM) for a in inputs]
    tile = shape((WLON, WLAT, LEV, C), BF16)
    outputs = (
        tile,
        tile,
        shape((C, 3 * C), F32),
        shape((C, C), F32),
        shape((C, HIDDEN), F32),
        shape((C, HIDDEN), F32),
        shape((HEADS, LWIN, POS), F32),
    )
    wide = lambda dtype, n=1: [pltpu.VMEM((TOK, C), dtype)] * n
    results = pl.pallas_call(
        functools.partial(block_kernel, n_lon, n_lat),
        out_shape=outputs,
        in_specs=[hbm] * len(inputs),
        out_specs=[vmem] * len(outputs),
        scratch_shapes=[
            *[pltpu.VMEM(a.shape, a.dtype) for a in inputs],
            dma((len(inputs),)),
            pltpu.VMEM((2, 4, 2, PACKED, 128), BF16),
            room(2, 3, RING, E_TILES // 24),
            room(3, RING, 2, L_TILES // 24),
            room(RING, 2, B_TILES // 8),
            pltpu.VMEM((2, 3, PACKED, 128), BF16),
            pltpu.VMEM((2, 4, PACKED, 128), BF16),
            pltpu.VMEM((3, 2, PACKED, 128), BF16),
            pltpu.VMEM((4, 2, PACKED, 128), BF16),
            pltpu.VMEM((2, 4, 2, PACKED, 128), BF16),
            dma((5, 3)),
            dma((5, 3)),
            *wide(BF16, 2),
            pltpu.VMEM((LWIN * STACK, WIN), F32),
            *wide(BF16, 4),
            *wide(F32),
            pltpu.VMEM((TOK, 1), F32),
            *wide(BF16, 2),
            pltpu.VMEM((TOK, HIDDEN), BF16),
            pltpu.VMEM((TOK, HIDDEN), BF16),
            *wide(BF16, 6),
            pltpu.VMEM((WH, POS), F32),
            pltpu.VMEM((SITE * WH, STRIP), F32),
            pltpu.VMEM((LANES // 128, SITE * WH, 128), F32),
            pltpu.VMEM((3, C, C), BF16),
            pltpu.VMEM((PAIR, PAIR), BF16),
            pltpu.VMEM((PAIR, PAIR), BF16),
            pltpu.VMEM((STRIP, LANES), BF16),
            pltpu.VMEM((TOK, HIDDEN), F32),
            *wide(F32),
            pltpu.VMEM((TOK, 1), F32),
            *PairSum.scratch(E_TILES),
            *WeightSum.scratch(L_TILES),
            *BiasSum.scratch(),
        ],
        compiler_params=pltpu.CompilerParams(
            vmem_limit_bytes=VMEM_LIMIT, collective_id=0, has_side_effects=True
        ),
        name="block",
    )(*inputs)
    *results, fc2, bias = pl.pallas_call(
        finish_kernel,
        out_shape=outputs,
        in_specs=[vmem] * len(outputs),
        out_specs=[hbm] * len(outputs),
        scratch_shapes=[dma((len(outputs),))],
        compiler_params=pltpu.CompilerParams(vmem_limit_bytes=VMEM_LIMIT),
        name="finish",
    )(*results)
    return (*results, fc2.T, bias.transpose(1, 0, 2)[None])


def solution(mesh):
    whole, tiles, banded = P(), P("lon", "lat", None, None), P("lat", None, None, None)
    return jax.shard_map(
        functools.partial(per_device, mesh.shape["lon"], mesh.shape["lat"]),
        mesh=mesh,
        in_specs=(tiles, whole, whole, whole, whole, banded, tiles),
        out_specs=(tiles, tiles, whole, whole, whole, whole, banded),
        check_vma=False,
    )
```

```python
import functools
import math

import jax
import jax.numpy as jnp
import numpy as np
from jax import lax
from jax.experimental import pallas as pl
from jax.experimental.pallas import tpu as pltpu
from jax.sharding import PartitionSpec as P

C = 192
HEADS = 6
HIDDEN = 768
LEV = 8
WLON = 12
WLAT = 6
WLEV = 2
LWIN = LEV // WLEV
WH = LWIN * HEADS
WIN = WLEV * WLAT * WLON
TOK = LWIN * WIN
QUAD = TOK // 4
SITE = WLEV * WLAT
SHIFTS = 2 * WLON - 1
STRIP = SHIFTS * SITE
POS = WLEV * WLEV * WLAT * WLAT * SHIFTS
RUN = WLAT * SHIFTS
LANES = 384
STACK = HEADS * WIN
EPSILON = 1e-05
MASKED = -1000000000.0
LOG2E = math.log2(math.e)
SCALE = 1.0 / math.sqrt(C // HEADS)
RING = 4
FAR_FIRST = (2, 1, 3)
E_TILES = 144
L_TILES = 72
B_TILES = 40
B_LEFT = STRIP - 256
B_ROWS = 48
CHUNK = QUAD // 2
PAIR = 4 * CHUNK
PACKED = 112
TILE = (16, 128)
BF16 = jnp.bfloat16
F32 = jnp.float32
MESH = pl.DeviceIdType.MESH
VMEM_LIMIT = 30 * 1024 * 1024


def token_places():
    w, o, lev, a = np.meshgrid(
        np.arange(2), np.arange(WLON), np.arange(WLEV), np.arange(WLAT), indexing="ij"
    )
    site = (o % 6) * 3 + a % 3
    row = (site % 9) * 8 + (site // 9) * 4 + 2 * w + lev
    return (((o // 6) * 2 + a // 3) * CHUNK + row).reshape(PAIR).astype(np.int32)


def lane_places():
    lev, a, d = np.meshgrid(np.arange(WLEV), np.arange(WLAT), np.arange(SHIFTS), indexing="ij")
    return ((SHIFTS - 1 - d) * SITE + lev * WLAT + a).reshape(STRIP).astype(np.int32)


def row_places():
    wh, _, site = np.meshgrid(np.arange(WH), np.arange(2), np.arange(SITE), indexing="ij")
    return (site * WH + wh).reshape(WH * 2 * SITE).astype(np.int32)


def row_codes():
    _, w, p, lev, a = np.meshgrid(
        np.arange(HEADS), np.arange(LWIN), np.arange(2), np.arange(WLEV), np.arange(WLAT), indexing="ij"
    )
    code = lev + 2 * (a >= WLAT // 2) + 4 * (w == LWIN - 1) + 8 * (p == 0)
    return code.reshape(WH * 2 * SITE).astype(np.int32)


def lane_codes():
    site = np.arange(LANES) % SITE
    return (site // WLAT + 2 * (site % WLAT >= WLAT // 2)).astype(np.int32)


def columns_of(*arrays):
    made = np.zeros((TOK, 8), np.int32)
    for i, array in enumerate(arrays):
        made[: len(array), i] = array
    return made


def dot(a, b):
    return jnp.dot(a, b, preferred_element_type=F32)


def dot_nt(a, b):
    return lax.dot_general(a, b, (((1,), (1,)), ((), ())), preferred_element_type=F32)


def dot_tn(a, b):
    return lax.dot_general(a, b, (((0,), (0,)), ((), ())), preferred_element_type=F32)


def one_hot(places, rows, cols):
    along = 1 if places.shape[1] == 1 else 0
    index = lax.broadcasted_iota(jnp.int32, (rows, cols), along)
    return jnp.where(index == places, 1.0, 0.0).astype(BF16)


def pieces(value, count):
    found = []
    for _ in range(count):
        part = value.astype(BF16)
        found.append(part)
        value = value - part.astype(F32)
    return found


def split(ref, index):
    part = ref[pl.ds((index // 2) * 6, 6), pl.ds((index % 2) * 3, 3)]
    part = pltpu.roll(part.astype(F32).reshape(18, LEV, C), LEV - 1, 1)
    low, high = part[:9], part[9:]
    upper = lax.broadcasted_iota(jnp.int32, low.shape, 1) < LEV // 2
    first = jnp.where(upper, low, pltpu.roll(high, LEV // 2, 1))
    second = jnp.where(upper, pltpu.roll(low, LEV // 2, 1), high)
    return first.reshape(CHUNK, C), second.reshape(CHUNK, C)


def merge(ref, index, chunks):
    first, second = (chunk.reshape(9, LEV, C) for chunk in chunks)
    upper = lax.broadcasted_iota(jnp.int32, first.shape, 1) < LEV // 2
    low = jnp.where(upper, first, pltpu.roll(second, LEV // 2, 1))
    high = jnp.where(upper, pltpu.roll(first, LEV // 2, 1), second)
    part = pltpu.roll(jnp.concatenate([low, high], axis=0), 1, 1)
    ref[pl.ds((index // 2) * 6, 6), pl.ds((index % 2) * 3, 3)] = part.reshape(6, 3, LEV, C).astype(BF16)


def pack(value):
    rest = jnp.concatenate([value[:40, 128:], value[32:, 128:]], axis=1)
    return jnp.concatenate([value[:, :128], rest], axis=0).astype(BF16)


def unpack(value):
    wide = value.astype(F32)
    rest = wide[CHUNK:]
    right = jnp.concatenate([rest[:, :64], rest[8:, 64:]], axis=0)
    return jnp.concatenate([wide[:CHUNK], right], axis=1)


def place_of(lon, lat):
    x = lax.rem(lat, 2) * 2 + lax.div(lon, 8)
    return (x, lax.rem(lax.div(lon, 2), RING), lax.div(lat, 2)), lax.rem(lon, 2)


def device_at(chip, core):
    x, y, z = chip
    return ((lax.rem(x, 2) * RING + y) * 2 + core, z * 2 + lax.div(x, 2))


def moved(chip, axis, step):
    return tuple(lax.rem(c + step, RING) if i == axis else c for i, c in enumerate(chip))


def remote(src, dst, send, recv, device):
    return pltpu.make_async_remote_copy(
        src_ref=src, dst_ref=dst, send_sem=send, recv_sem=recv, device_id=device, device_id_type=MESH
    )


class Here:
    def __init__(self, n_lon, n_lat):
        self.lon, self.lat = lax.axis_index("lon"), lax.axis_index("lat")
        self.chip, self.core = place_of(self.lon, self.lat)
        self.sibling = (self.lon + 1 - 2 * self.core, self.lat)
        self.slot = [[lax.rem(c + k, RING) for k in range(RING)] for c in self.chip]
        chips = [[moved(self.chip, axis, k) for k in range(RING)] for axis in range(3)]
        self.along = [[device_at(chip, self.core) for chip in ring] for ring in chips]
        other = 1 - self.core
        self.eight = []
        for axis in range(3):
            found = []
            for k in FAR_FIRST + (0,):
                if k:
                    found.append((self.along[axis][k], self.slot[axis][k], self.core))
                found.append((device_at(chips[axis][k], other), self.slot[axis][k], other))
            self.eight.append(found)
        self.facing = (lax.rem(self.lon + 8, 16), self.lat)
        self.across = {}
        for step in (-1, 1):
            to_lon = lax.rem(self.lon + n_lon + step, n_lon)
            to_lat = lax.rem(self.lat + n_lat + step, n_lat)
            self.across[step] = ((to_lon, to_lat), (to_lon, self.lat), (self.lon, to_lat))

    def greet(self):
        others = [*self.across[-1], *self.across[1], self.sibling]
        for axis in range(3):
            others += [device for device, _, _ in self.eight[axis][:-1]]
        barrier = pltpu.get_barrier_semaphore()
        for device in others:
            pl.semaphore_signal(barrier, inc=1, device_id=device, device_id_type=MESH)
        return lambda: pl.semaphore_wait(barrier, len(others))


def halo(here, source, target, send, recv, step):
    copies = []
    for index in (0, 2, 1):
        src = index if step < 0 else 3 - index
        device = here.across[step][index]
        copies.append(remote(source.at[src], target.at[3 - src], send.at[index], recv.at[index], device))
    return copies


def begin(copies):
    for copy in copies:
        copy.start()


def end(copies):
    for copy in copies:
        copy.wait()


def wait_bytes(like, sem):
    pltpu.make_async_copy(like, like, sem).wait()


def room(*dims):
    return pltpu.VMEM((*dims, *TILE), BF16)


def tiles_in(block):
    narrow = block.astype(BF16)
    for c in range(block.shape[1] // 128):
        for r in range(block.shape[0] // 16):
            yield narrow[r * 16 : (r + 1) * 16, c * 128 : (c + 1) * 128]


def added(terms):
    total = terms[0].astype(F32)
    for term in terms[1:]:
        total = total + term.astype(F32)
    return total.astype(BF16)


class WeightSum:
    def __init__(self, here, out, refs):
        self.here, self.out = here, out
        self.src, self.r1, self.x2, self.x3, self.send, self.recv = refs

    @staticmethod
    def scratch(tiles):
        n1 = tiles // 24
        dma = pltpu.SemaphoreType.DMA
        return [room(3, RING, 2, n1), room(7, 3, n1), room(3, RING, n1), room(3, RING, n1), dma((4,)), dma((4,))]

    def put(self, block, first):
        n1 = self.src.shape[3]
        for at, tile in enumerate(tiles_in(block), first):
            self.src[at // (8 * n1), at // (2 * n1) % RING, at // n1 % 2, at % n1] = tile

    def phase(self, at):
        here, made = self.here, []
        sems = self.send.at[at], self.recv.at[at]
        if at in (0, 3):
            for k in range(7):
                for t in range(3):
                    device, slot, core = here.eight[t][k]
                    mine = self.out.at[t, here.slot[t][0], here.core]
                    if at == 0:
                        made.append(remote(self.src.at[t, slot, core], self.r1.at[k, t], *sems, device))
                    else:
                        made.append(remote(mine, mine, *sems, device))
        else:
            for k in FAR_FIRST:
                for t in range(3):
                    axis = (t + at) % 3
                    mine = (self.x2 if at == 1 else self.x3).at[t, here.slot[axis][0]]
                    made.append(remote(mine, mine, *sems, here.along[axis][k]))
        return made

    def start(self):
        begin(self.phase(0))

    def step(self, at):
        like = self.r1 if at in (0, 3) else self.r1.at[pl.ds(0, 3)]
        wait_bytes(like, self.recv.at[at])
        wait_bytes(like, self.send.at[at])
        core = self.here.core
        for t in range(3):
            one, two, three = (self.here.slot[(t + i) % 3][0] for i in range(3))
            if at == 0:
                self.x2[t, two] = added([self.src[t, one, core]] + [self.r1[k, t] for k in range(7)])
            if at == 1:
                self.x3[t, three] = added([self.x2[t, k] for k in range(RING)])
            if at == 2:
                self.out[t, one, core] = added([self.x3[t, k] for k in range(RING)])
        if at < 3:
            begin(self.phase(at + 1))


class PairSum:
    def __init__(self, here, out, refs):
        self.here, self.out = here, out
        self.src, self.other, self.a1, self.r1, self.x2, self.x3, self.send, self.recv = refs

    @staticmethod
    def scratch(tiles):
        n1 = tiles // 24
        dma = pltpu.SemaphoreType.DMA
        return [
            room(2, tiles // 2), room(tiles // 2),
            room(3, RING, n1), room(3, RING - 1, n1), room(3, RING, n1), room(3, RING, n1),
            dma((6,)), dma((6,)),
        ]

    def put(self, block, first):
        each = self.src.shape[1]
        for at, tile in enumerate(tiles_in(block), first):
            self.src[at // each, at % each] = tile

    def get(self):
        n1 = self.a1.shape[2]
        return [self.out[i // (12 * n1), i // (4 * n1) % 3, i // n1 % 4, i % n1] for i in range(24 * n1)]

    def copies(self, at, axis_of, source, target):
        made = []
        for k in FAR_FIRST:
            for t in range(3):
                axis = (t + axis_of) % 3
                slot = self.here.slot[axis]
                made.append(
                    remote(
                        source(t, slot[k], slot[0]), target(t, k - 1, slot[0]),
                        self.send.at[at], self.recv.at[at], self.here.along[axis][k],
                    )
                )
        return made

    def phase(self, at):
        core = self.here.core
        if at == 0:
            return [remote(self.src.at[1 - core], self.other, self.send.at[0], self.recv.at[0], self.here.sibling)]
        if at == 1:
            return self.copies(1, 0, lambda t, to, me: self.a1.at[t, to], lambda t, k, me: self.r1.at[t, k])
        if at == 2:
            return self.copies(2, 1, lambda t, to, me: self.x2.at[t, me], lambda t, k, me: self.x2.at[t, me])
        if at == 3:
            return self.copies(3, 2, lambda t, to, me: self.x3.at[t, me], lambda t, k, me: self.x3.at[t, me])
        if at == 4:
            out = self.out.at[core]
            return self.copies(4, 0, lambda t, to, me: out.at[t, me], lambda t, k, me: out.at[t, me])
        return [remote(self.out.at[core], self.out.at[core], self.send.at[5], self.recv.at[5], self.here.sibling)]

    def start(self):
        begin(self.phase(0))

    def step(self, at):
        like = self.other if at in (0, 5) else self.r1
        wait_bytes(like, self.recv.at[at])
        wait_bytes(like, self.send.at[at])
        core = self.here.core
        if at == 0:
            total = self.src[core].astype(F32) + self.other[...].astype(F32)
            self.a1[...] = total.astype(BF16).reshape(self.a1.shape)
        for t in range(3):
            one, two, three = (self.here.slot[(t + i) % 3][0] for i in range(3))
            if at == 1:
                total = self.a1[t, one].astype(F32)
                for k in range(RING - 1):
                    total = total + self.r1[t, k].astype(F32)
                self.x2[t, two] = total.astype(BF16)
            if at in (2, 3):
                came = self.x2 if at == 2 else self.x3
                total = came[t, 0].astype(F32)
                for k in range(1, RING):
                    total = total + came[t, k].astype(F32)
                if at == 2:
                    self.x3[t, three] = total.astype(BF16)
                else:
                    self.out[core, t, one] = total.astype(BF16)
        if at < 5:
            begin(self.phase(at + 1))


class BiasSum:
    def __init__(self, here, out, refs):
        self.here, self.out = here, out
        self.src, self.r1, self.x2, self.send, self.recv = refs

    @staticmethod
    def scratch():
        each = B_TILES // 8
        dma = pltpu.SemaphoreType.DMA
        return [room(RING, 2, each), room(7, each), room(2, each), dma((3,)), dma((3,))]

    def put(self, block):
        each = B_TILES // 8
        last = block[:, 256:]
        shared = last[0:B_ROWS]
        for g in range(1, 288 // B_ROWS):
            shared = shared + pltpu.roll(last[g * B_ROWS : (g + 1) * B_ROWS], g * B_LEFT, 1)
        tiles = [*tiles_in(block[:, :256]), *tiles_in(shared), jnp.zeros(TILE, BF16)]
        for at, tile in enumerate(tiles):
            self.src[at // (2 * each), at // each % 2, at % each] = tile

    def get(self):
        each = B_TILES // 8
        tiles = [self.out[at // (2 * each), at // each % 2, at % each] for at in range(B_TILES)]
        first = joined(tiles[:36], 2)
        shared = joined(tiles[36:39], 1)
        last = [shared]
        for g in range(1, 288 // B_ROWS):
            last.append(pltpu.roll(shared, 128 - g * B_LEFT, 1))
        return jnp.concatenate([first, jnp.concatenate(last, axis=0)], axis=1)

    def phase(self, at):
        here, made = self.here, []
        sems = self.send.at[at], self.recv.at[at]
        if at == 1:
            return [remote(self.x2.at[0], self.x2.at[1], *sems, here.facing)]
        mine = self.out.at[here.slot[1][0], here.core]
        for k, (device, slot, core) in enumerate(here.eight[1]):
            if at == 0:
                made.append(remote(self.src.at[slot, core], self.r1.at[k], *sems, device))
            else:
                made.append(remote(mine, mine, *sems, device))
        return made

    def start(self):
        begin(self.phase(0))

    def step(self, at):
        like = self.x2.at[1] if at == 1 else self.r1
        wait_bytes(like, self.recv.at[at])
        wait_bytes(like, self.send.at[at])
        slot, core = self.here.slot[1][0], self.here.core
        if at == 0:
            self.x2[0] = added([self.src[slot, core]] + [self.r1[k] for k in range(7)])
        if at == 1:
            self.out[slot, core] = added([self.x2[0], self.x2[1]])
        if at < 2:
            begin(self.phase(at + 1))


def layer_norm(x):
    centered = x - jnp.mean(x, axis=-1, keepdims=True)
    spread = jnp.mean(centered * centered, axis=-1, keepdims=True)
    rate = lax.rsqrt(spread + EPSILON)
    return centered * rate, rate


def layer_norm_back(cot, unit, rate):
    first = jnp.mean(cot, axis=-1, keepdims=True)
    second = jnp.mean(cot * unit, axis=-1, keepdims=True)
    return rate * (cot - first - unit * second)


def head_mask(head):
    lane = lax.broadcasted_iota(jnp.int32, (1, C), 1)
    return (lane >= head * 32) & (lane < head * 32 + 32)


def stacked(value):
    wide = value.astype(F32)
    parts = [jnp.where(head_mask(h), wide, 0.0).astype(BF16) for h in range(HEADS)]
    return jnp.concatenate(parts, axis=0)


def unstacked(value):
    total = jnp.where(head_mask(0), value[0:WIN], 0.0)
    for h in range(1, HEADS):
        total = total + jnp.where(head_mask(h), value[h * WIN : (h + 1) * WIN], 0.0)
    return total


def expand_bias(last_lat, table, columns, index_rows, lanes, tall_table, gathered, strips, scores):
    for head in range(HEADS):
        tall_table[head * LWIN : (head + 1) * LWIN, :] = table[head]
    for site in range(SITE):
        lev, a = site // WLAT, site % WLAT
        for other in range(WLEV):
            start = ((lev * WLEV + other) * WLAT + a) * RUN
            gathered[site * WH : (site + 1) * WH, other * RUN : (other + 1) * RUN] = tall_table[
                :, start : start + RUN
            ]
    moved = sum(dot(part, lanes[...]) for part in pieces(gathered[...], 3))
    rows = one_hot(columns[:, 1:2], WH * 2 * SITE, SITE * WH)
    moved = sum(dot(rows, part) for part in pieces(moved, 3))
    code = columns[:, 2:3]
    moved = jnp.where((code & 8) != 0, pltpu.roll(moved, LANES - SITE, 1), moved) * LOG2E
    seen = jnp.where((code & 4) != 0, 1, 0) + jnp.where(last_lat, 2, 0)
    apart = (code ^ index_rows[2:3, 0:LANES]) & seen
    strips[...] = jnp.where(apart != 0, MASKED, moved)

    def one(wh, carry):
        strip = strips[pl.ds(pl.multiple_of(wh * 2 * SITE, 8), 2 * SITE), :]
        start = lax.rem(wh, LWIN) * STACK + lax.div(wh, LWIN) * WIN
        for pair in range(WLON // 2):
            offset = (WLON - 2 - 2 * pair) * SITE
            scores[pl.ds(pl.multiple_of(start + pair * 24, 8), 24), :] = strip[
                :, offset : offset + WIN
            ]
        return carry

    lax.fori_loop(0, WH, one, 0)


def collapse_bias(first, last, scores, strips):
    def one(wh, carry):
        start = lax.rem(wh, LWIN) * STACK + lax.div(wh, LWIN) * WIN
        total = jnp.zeros((2 * SITE, LANES), F32)
        for pair in range(WLON // 2):
            offset = (WLON - 2 - 2 * pair) * SITE
            part = scores[pl.ds(pl.multiple_of(start + pair * 24, 8), 24), :]
            part = jnp.concatenate([part, jnp.zeros((2 * SITE, LANES - WIN), F32)], axis=1)
            total = total + (pltpu.roll(part, offset, 1) if offset else part)
        strips[pl.ds(pl.multiple_of(wh * 2 * SITE, 8), 2 * SITE), :] = total
        return carry

    lax.fori_loop(first, last, one, 0)


def join_strips(strips, columns, index_rows):
    total = strips[...]
    total = jnp.where((columns[:, 2:3] & 8) != 0, pltpu.roll(total, SITE, 1), total)
    rows = one_hot(index_rows[1:2, :], SITE * WH, WH * 2 * SITE)
    return sum(dot(rows, part) for part in pieces(total, 2))


def block_kernel(n_lon, n_lat, *refs):
    loaded = refs[:9]
    out_field, grad_field, qkv, proj, fc1, fc2, bias = refs[9:16]
    field, cot, w_qkv, w_proj, w_fc1, w_fc2, table, columns, index_rows, load_sem = refs[16:26]
    (
        out, e_out, l_out, b_out, sent, came, cot_sent, cot_came, back, halo_send, halo_recv,
        xw, uw, scores, normed, query, key, value, unit, rate, blended, normed_two, hidden,
        cot_first, cot_mid, cot_q, cot_k, cot_v, ow, gw, tall_table, gathered, strips, w3,
        places_in, places_out, lanes, slope, unit_two, rate_two,
    ) = refs[26:66]
    here = Here(n_lon, n_lat)
    early = PairSum(here, e_out, refs[66:74])
    late = WeightSum(here, l_out, refs[74:80])
    strip_sum = BiasSum(here, b_out, refs[80:85])

    loads = [
        pltpu.make_async_copy(src, dst, load_sem.at[i]) for i, (src, dst) in enumerate(zip(loaded, refs[16:25]))
    ]
    loads[0].start()
    greeted = here.greet()
    begin(loads[6:9])
    loads[0].wait()
    for index in range(3):
        for part, chunk in enumerate(split(field, index)):
            sent[part, index] = pack(chunk)
    greeted()
    inward = [
        halo(here, sent.at[i], came.at[i], halo_send.at[i], halo_recv.at[i], -1) for i in range(2)
    ]
    cot_inward = halo(here, cot_sent, cot_came, halo_send.at[2], halo_recv.at[2], -1)
    outward = [
        halo(here, back.at[i], out.at[i], halo_send.at[3 + i], halo_recv.at[3 + i], 1) for i in range(2)
    ]
    begin(inward[0])
    begin(inward[1])
    begin(loads[1:6])
    end(loads[6:9])
    lanes[...] = one_hot(columns[0:STRIP, 3:4], STRIP, LANES)
    last_lat = here.lat == n_lat - 1
    expand_bias(last_lat, table, columns, index_rows, lanes, tall_table, gathered, strips, scores)
    places_in[...] = one_hot(columns[0:PAIR, 0:1], PAIR, PAIR)
    places_out[...] = one_hot(index_rows[0:1, 0:PAIR], PAIR, PAIR)
    loads[1].wait()
    for index in range(3):
        for part, chunk in enumerate(split(cot, index)):
            cot_sent[index, part] = pack(chunk)
    own = [split(ref, 3) for ref in (field, cot)]
    loads[2].wait()
    for third in range(3):
        w3[third] = w_qkv[:, third * C : (third + 1) * C]

    def gather(kind, part):
        if kind:
            arrived = [cot_came[i, part] for i in range(1, 4)]
        else:
            arrived = [came[part, i] for i in range(1, 4)]
        parts = [own[kind][part]] + [unpack(value) for value in arrived]
        return dot(places_in[...], jnp.concatenate(parts, axis=0).astype(BF16)).astype(BF16)

    def scatter(kind, ref):
        for part in range(2):
            whole = dot(places_out[...], ref[part * PAIR : (part + 1) * PAIR, :])
            out[kind, 3, part] = pack(whole[:CHUNK])
            for i in range(1, 4):
                back[kind, i, part] = pack(whole[i * CHUNK : (i + 1) * CHUNK])
        begin(outward[kind])

    def places(w):
        return pl.ds(w * WIN, WIN), pl.ds(w * STACK, STACK)

    def attend(w):
        rows, tall = places(w)
        unit_x, rate_x = layer_norm(xw[rows, :].astype(F32))
        unit[rows, :] = unit_x
        rate[rows, :] = rate_x
        norm = unit_x.astype(BF16)
        normed[rows, :] = norm
        q = dot(norm, w3[0]).astype(BF16)
        k = dot(norm, w3[1]).astype(BF16)
        v = dot(norm, w3[2]).astype(BF16)
        query[rows, :] = q
        key[rows, :] = k
        value[rows, :] = v
        s = dot_nt(stacked(q), k) * (SCALE * LOG2E) + scores[tall, :]
        e = jnp.exp2(s - jnp.max(s, axis=-1, keepdims=True))
        p = e * (1.0 / jnp.sum(e, axis=-1, keepdims=True))
        scores[tall, :] = p
        blended[rows, :] = unstacked(dot(p.astype(BF16), v)).astype(BF16)

    def feed(w):
        rows = pl.ds(w * 2 * WIN, 2 * WIN)
        middle = xw[rows, :].astype(F32) + dot(blended[rows, :], w_proj[...])
        middle = middle.astype(BF16).astype(F32)
        unit_m, rate_m = layer_norm(middle)
        norm_m = unit_m.astype(BF16)
        normed_two[rows, :] = norm_m
        first = dot(norm_m, w_fc1[...])
        phi = 0.5 + 0.5 * lax.erf(first * math.sqrt(0.5))
        hid = (first * phi).astype(BF16)
        hidden[rows, :] = hid
        bell = jnp.exp2(first * first * (-0.5 * LOG2E)) * (1.0 / math.sqrt(2.0 * math.pi))
        slope[rows, :] = phi + first * bell
        unit_two[rows, :] = unit_m
        rate_two[rows, :] = rate_m
        ow[rows, :] = (middle + dot_nt(hid, w_fc2[...])).astype(BF16)

    def feed_back(w):
        rows = pl.ds(w * 2 * WIN, 2 * WIN)
        up = uw[rows, :]
        c_first = (dot(up, w_fc2[...]).astype(BF16).astype(F32) * slope[rows, :]).astype(BF16)
        cot_first[rows, :] = c_first
        c_norm = dot_nt(c_first, w_fc1[...]).astype(BF16).astype(F32)
        c_mid = layer_norm_back(c_norm, unit_two[rows, :], rate_two[rows, :]).astype(BF16).astype(F32)
        cot_mid[rows, :] = (up.astype(F32) + c_mid).astype(BF16)

    def backward(w):
        rows, tall = places(w)
        up = cot_mid[rows, :]
        c_blend = stacked(dot_nt(up, w_proj[...]).astype(BF16))
        p = scores[tall, :]
        c_p = dot_nt(c_blend, value[rows, :])
        c_s = p * (c_p - jnp.sum(p * c_p, axis=-1, keepdims=True))
        scores[tall, :] = c_s
        c_v = dot_tn(p.astype(BF16), c_blend).astype(BF16)
        narrow = c_s.astype(BF16)
        c_q = (unstacked(dot(narrow, key[rows, :])) * SCALE).astype(BF16)
        c_k = (dot_tn(narrow, stacked(query[rows, :])) * SCALE).astype(BF16)
        cot_q[rows, :] = c_q
        cot_k[rows, :] = c_k
        cot_v[rows, :] = c_v

    def inputs_back(w):
        rows = pl.ds(w * 2 * WIN, 2 * WIN)
        c_norm = dot_nt(cot_q[rows, :], w3[0]) + dot_nt(cot_k[rows, :], w3[1])
        c_norm = (c_norm + dot_nt(cot_v[rows, :], w3[2])).astype(BF16).astype(F32)
        c_x = layer_norm_back(c_norm, unit[rows, :], rate[rows, :]).astype(BF16)
        gw[rows, :] = (cot_mid[rows, :].astype(F32) + c_x.astype(F32)).astype(BF16)

    for part in range(2):
        end(inward[part])
        xw[part * PAIR : (part + 1) * PAIR, :] = gather(0, part)
        if not part:
            begin(cot_inward)
        attend(2 * part)
        attend(2 * part + 1)
    end(loads[3:6])
    feed(0)
    feed(1)
    end(cot_inward)
    for part in range(2):
        uw[part * PAIR : (part + 1) * PAIR, :] = gather(1, part)
        feed_back(part)
    early.put(dot_tn(normed_two[...], cot_first[...]), 0)
    early.put(dot_tn(uw[...], hidden[...]), 72)
    early.start()
    backward(0)
    backward(1)
    backward(2)
    early.step(0)
    backward(3)
    norm = normed[...]
    late.put(jnp.concatenate([dot_tn(norm, cot_q[...]), dot_tn(norm, cot_k[...])], axis=1), 0)
    c_proj = dot_tn(blended[...], cot_mid[...])
    late.put(jnp.concatenate([dot_tn(norm, cot_v[...]), c_proj], axis=1), 36)
    late.start()
    collapse_bias(0, WH, scores, strips)
    strip_sum.put(join_strips(strips, columns, index_rows))
    strip_sum.start()
    early.step(1)
    inputs_back(0)
    inputs_back(1)
    late.step(0)
    scatter(1, gw)
    scatter(0, ow)
    early.step(2)
    strip_sum.step(0)
    late.step(1)
    early.step(3)
    strip_sum.step(1)
    late.step(2)
    early.step(4)
    end(outward[1])
    for index in range(4):
        merge(grad_field, index, [unpack(out[1, index, part]) for part in range(2)])
    end(outward[0])
    for index in range(4):
        merge(out_field, index, [unpack(out[0, index, part]) for part in range(2)])
    strip_sum.step(2)
    finish_bias(strip_sum.get(), lanes, tall_table, bias)
    early.step(5)
    fc1[...] = joined(early.get()[:72], 6)
    fc2[...] = joined(early.get()[72:], 6)
    late.step(3)
    qkv[:, 0:384] = joined(tiles_of(l_out)[:36], 3)
    right = joined(tiles_of(l_out)[36:], 3)
    qkv[:, 384:576] = right[:, 0:C]
    proj[...] = right[:, C:]


def joined(tiles, columns):
    rows = len(tiles) // columns
    cols = [jnp.concatenate(tiles[c * rows : (c + 1) * rows], axis=0) for c in range(columns)]
    return jnp.concatenate(cols, axis=1).astype(F32)


def tiles_of(ref):
    n1 = ref.shape[3]
    return [ref[i // (8 * n1), i // (2 * n1) % RING, i // n1 % 2, i % n1] for i in range(24 * n1)]


def finish_bias(strip, lanes, tall_table, bias):
    runs = dot_nt(strip.astype(BF16), lanes[...])
    for site in range(SITE):
        lev, a = site // WLAT, site % WLAT
        for other in range(WLEV):
            start = ((lev * WLEV + other) * WLAT + a) * RUN
            tall_table[:, start : start + RUN] = runs[
                site * WH : (site + 1) * WH, other * RUN : (other + 1) * RUN
            ]
    for head in range(HEADS):
        bias[head] = tall_table[head * LWIN : (head + 1) * LWIN, :]


def finish_kernel(*refs):
    count = len(refs) // 2
    copies = [pltpu.make_async_copy(refs[i], refs[count + i], refs[-1].at[i]) for i in range(count)]
    copies.sort(key=lambda copy: -math.prod(copy.src_ref.shape))
    begin(copies)
    end(copies)


def per_device(n_lon, n_lat, field, w_qkv, w_proj, w_fc1, w_fc2, bias_table, cotangent):
    vmem, hbm = pl.BlockSpec(memory_space=pltpu.VMEM), pl.BlockSpec(memory_space=pltpu.HBM)
    shape = jax.ShapeDtypeStruct
    dma = pltpu.SemaphoreType.DMA
    rows = row_places()
    columns = columns_of(token_places(), rows, row_codes(), lane_places())
    index_rows = columns_of(token_places(), rows, lane_codes()).T.copy()
    inputs = (
        field, cotangent, w_qkv, w_proj, w_fc1, w_fc2.T, bias_table[0].transpose(1, 0, 2), columns, index_rows
    )
    inputs = [pltpu.with_memory_space_constraint(jnp.asarray(a), pltpu.HBM) for a in inputs]
    tile = shape((WLON, WLAT, LEV, C), BF16)
    outputs = (
        tile,
        tile,
        shape((C, 3 * C), F32),
        shape((C, C), F32),
        shape((C, HIDDEN), F32),
        shape((C, HIDDEN), F32),
        shape((HEADS, LWIN, POS), F32),
    )
    wide = lambda dtype, n=1: [pltpu.VMEM((TOK, C), dtype)] * n
    results = pl.pallas_call(
        functools.partial(block_kernel, n_lon, n_lat),
        out_shape=outputs,
        in_specs=[hbm] * len(inputs),
        out_specs=[vmem] * len(outputs),
        scratch_shapes=[
            *[pltpu.VMEM(a.shape, a.dtype) for a in inputs],
            dma((len(inputs),)),
            pltpu.VMEM((2, 4, 2, PACKED, 128), BF16),
            room(2, 3, RING, E_TILES // 24),
            room(3, RING, 2, L_TILES // 24),
            room(RING, 2, B_TILES // 8),
            pltpu.VMEM((2, 3, PACKED, 128), BF16),
            pltpu.VMEM((2, 4, PACKED, 128), BF16),
            pltpu.VMEM((3, 2, PACKED, 128), BF16),
            pltpu.VMEM((4, 2, PACKED, 128), BF16),
            pltpu.VMEM((2, 4, 2, PACKED, 128), BF16),
            dma((5, 3)),
            dma((5, 3)),
            *wide(BF16, 2),
            pltpu.VMEM((LWIN * STACK, WIN), F32),
            *wide(BF16, 4),
            *wide(F32),
            pltpu.VMEM((TOK, 1), F32),
            *wide(BF16, 2),
            pltpu.VMEM((TOK, HIDDEN), BF16),
            pltpu.VMEM((TOK, HIDDEN), BF16),
            *wide(BF16, 6),
            pltpu.VMEM((WH, POS), F32),
            pltpu.VMEM((SITE * WH, STRIP), F32),
            pltpu.VMEM((WH * 2 * SITE, LANES), F32),
            pltpu.VMEM((3, C, C), BF16),
            pltpu.VMEM((PAIR, PAIR), BF16),
            pltpu.VMEM((PAIR, PAIR), BF16),
            pltpu.VMEM((STRIP, LANES), BF16),
            pltpu.VMEM((TOK, HIDDEN), F32),
            *wide(F32),
            pltpu.VMEM((TOK, 1), F32),
            *PairSum.scratch(E_TILES),
            *WeightSum.scratch(L_TILES),
            *BiasSum.scratch(),
        ],
        compiler_params=pltpu.CompilerParams(
            vmem_limit_bytes=VMEM_LIMIT, collective_id=0, has_side_effects=True
        ),
        name="block",
    )(*inputs)
    *results, fc2, bias = pl.pallas_call(
        finish_kernel,
        out_shape=outputs,
        in_specs=[vmem] * len(outputs),
        out_specs=[hbm] * len(outputs),
        scratch_shapes=[dma((len(outputs),))],
        compiler_params=pltpu.CompilerParams(vmem_limit_bytes=VMEM_LIMIT),
        name="finish",
    )(*results)
    return (*results, fc2.T, bias.transpose(1, 0, 2)[None])


def solution(mesh):
    whole, tiles, banded = P(), P("lon", "lat", None, None), P("lat", None, None, None)
    return jax.shard_map(
        functools.partial(per_device, mesh.shape["lon"], mesh.shape["lat"]),
        mesh=mesh,
        in_specs=(tiles, whole, whole, whole, whole, banded, tiles),
        out_specs=(tiles, tiles, whole, whole, whole, whole, banded),
        check_vma=False,
    )
```

```python
import functools
import math

import jax
import jax.numpy as jnp
import numpy as np
from jax import lax
from jax.experimental import pallas as pl
from jax.experimental.pallas import tpu as pltpu
from jax.sharding import PartitionSpec as P

C = 192
HEADS = 6
HIDDEN = 768
LEV = 8
WLON = 12
WLAT = 6
WLEV = 2
LWIN = LEV // WLEV
WH = LWIN * HEADS
WIN = WLEV * WLAT * WLON
TOK = LWIN * WIN
QUAD = TOK // 4
SITE = WLEV * WLAT
SHIFTS = 2 * WLON - 1
STRIP = SHIFTS * SITE
POS = WLEV * WLEV * WLAT * WLAT * SHIFTS
RUN = WLAT * SHIFTS
LANES = 384
STACK = HEADS * WIN
EPSILON = 1e-05
MASKED = -1000000000.0
LOG2E = math.log2(math.e)
SCALE = 1.0 / math.sqrt(C // HEADS)
RING = 4
FAR_FIRST = (2, 1, 3)
E_TILES = 144
L_TILES = 72
B_TILES = 40
B_LEFT = STRIP - 256
B_ROWS = 48
CHUNK = QUAD // 2
PAIR = 4 * CHUNK
PACKED = 112
TILE = (16, 128)
BF16 = jnp.bfloat16
F32 = jnp.float32
MESH = pl.DeviceIdType.MESH
VMEM_LIMIT = 30 * 1024 * 1024


def token_places():
    w, o, lev, a = np.meshgrid(
        np.arange(2), np.arange(WLON), np.arange(WLEV), np.arange(WLAT), indexing="ij"
    )
    site = (o % 6) * 3 + a % 3
    row = (site % 9) * 8 + (site // 9) * 4 + 2 * w + lev
    return (((o // 6) * 2 + a // 3) * CHUNK + row).reshape(PAIR).astype(np.int32)


def lane_places():
    lev, a, d = np.meshgrid(np.arange(WLEV), np.arange(WLAT), np.arange(SHIFTS), indexing="ij")
    return ((SHIFTS - 1 - d) * SITE + lev * WLAT + a).reshape(STRIP).astype(np.int32)


def row_places():
    wh, _, site = np.meshgrid(np.arange(WH), np.arange(2), np.arange(SITE), indexing="ij")
    return (site * WH + wh).reshape(WH * 2 * SITE).astype(np.int32)


def row_codes():
    _, w, p, lev, a = np.meshgrid(
        np.arange(HEADS), np.arange(LWIN), np.arange(2), np.arange(WLEV), np.arange(WLAT), indexing="ij"
    )
    code = lev + 2 * (a >= WLAT // 2) + 4 * (w == LWIN - 1) + 8 * (p == 0)
    return code.reshape(WH * 2 * SITE).astype(np.int32)


def lane_codes():
    site = np.arange(LANES) % SITE
    return (site // WLAT + 2 * (site % WLAT >= WLAT // 2)).astype(np.int32)


def columns_of(*arrays):
    made = np.zeros((TOK, 8), np.int32)
    for i, array in enumerate(arrays):
        made[: len(array), i] = array
    return made


def dot(a, b):
    return jnp.dot(a, b, preferred_element_type=F32)


def dot_nt(a, b):
    return lax.dot_general(a, b, (((1,), (1,)), ((), ())), preferred_element_type=F32)


def dot_tn(a, b):
    return lax.dot_general(a, b, (((0,), (0,)), ((), ())), preferred_element_type=F32)


def one_hot(places, rows, cols):
    along = 1 if places.shape[1] == 1 else 0
    index = lax.broadcasted_iota(jnp.int32, (rows, cols), along)
    return jnp.where(index == places, 1.0, 0.0).astype(BF16)


def pieces(value, count):
    found = []
    for _ in range(count):
        part = value.astype(BF16)
        found.append(part)
        value = value - part.astype(F32)
    return found


def split(ref, index):
    part = ref[pl.ds((index // 2) * 6, 6), pl.ds((index % 2) * 3, 3)]
    part = pltpu.roll(part.astype(F32).reshape(18, LEV, C), LEV - 1, 1)
    low, high = part[:9], part[9:]
    upper = lax.broadcasted_iota(jnp.int32, low.shape, 1) < LEV // 2
    first = jnp.where(upper, low, pltpu.roll(high, LEV // 2, 1))
    second = jnp.where(upper, pltpu.roll(low, LEV // 2, 1), high)
    return first.reshape(CHUNK, C), second.reshape(CHUNK, C)


def merge(ref, index, chunks):
    first, second = (chunk.reshape(9, LEV, C) for chunk in chunks)
    upper = lax.broadcasted_iota(jnp.int32, first.shape, 1) < LEV // 2
    low = jnp.where(upper, first, pltpu.roll(second, LEV // 2, 1))
    high = jnp.where(upper, pltpu.roll(first, LEV // 2, 1), second)
    part = pltpu.roll(jnp.concatenate([low, high], axis=0), 1, 1)
    ref[pl.ds((index // 2) * 6, 6), pl.ds((index % 2) * 3, 3)] = part.reshape(6, 3, LEV, C).astype(BF16)


def pack(value):
    rest = jnp.concatenate([value[:40, 128:], value[32:, 128:]], axis=1)
    return jnp.concatenate([value[:, :128], rest], axis=0).astype(BF16)


def unpack(value):
    wide = value.astype(F32)
    rest = wide[CHUNK:]
    right = jnp.concatenate([rest[:, :64], rest[8:, 64:]], axis=0)
    return jnp.concatenate([wide[:CHUNK], right], axis=1)


def place_of(lon, lat):
    x = lax.rem(lat, 2) * 2 + lax.div(lon, 8)
    return (x, lax.rem(lax.div(lon, 2), RING), lax.div(lat, 2)), lax.rem(lon, 2)


def device_at(chip, core):
    x, y, z = chip
    return ((lax.rem(x, 2) * RING + y) * 2 + core, z * 2 + lax.div(x, 2))


def moved(chip, axis, step):
    return tuple(lax.rem(c + step, RING) if i == axis else c for i, c in enumerate(chip))


def remote(src, dst, send, recv, device):
    return pltpu.make_async_remote_copy(
        src_ref=src, dst_ref=dst, send_sem=send, recv_sem=recv, device_id=device, device_id_type=MESH
    )


class Here:
    def __init__(self, n_lon, n_lat):
        self.lon, self.lat = lax.axis_index("lon"), lax.axis_index("lat")
        self.chip, self.core = place_of(self.lon, self.lat)
        self.sibling = (self.lon + 1 - 2 * self.core, self.lat)
        self.slot = [[lax.rem(c + k, RING) for k in range(RING)] for c in self.chip]
        chips = [[moved(self.chip, axis, k) for k in range(RING)] for axis in range(3)]
        self.along = [[device_at(chip, self.core) for chip in ring] for ring in chips]
        other = 1 - self.core
        self.eight = []
        for axis in range(3):
            found = []
            for k in FAR_FIRST + (0,):
                if k:
                    found.append((self.along[axis][k], self.slot[axis][k], self.core))
                found.append((device_at(chips[axis][k], other), self.slot[axis][k], other))
            self.eight.append(found)
        self.facing = (lax.rem(self.lon + 8, 16), self.lat)
        self.across = {}
        for step in (-1, 1):
            to_lon = lax.rem(self.lon + n_lon + step, n_lon)
            to_lat = lax.rem(self.lat + n_lat + step, n_lat)
            self.across[step] = ((to_lon, to_lat), (to_lon, self.lat), (self.lon, to_lat))

    def greet(self):
        others = [*self.across[-1], *self.across[1], self.sibling]
        for axis in range(3):
            others += [device for device, _, _ in self.eight[axis][:-1]]
        barrier = pltpu.get_barrier_semaphore()
        for device in others:
            pl.semaphore_signal(barrier, inc=1, device_id=device, device_id_type=MESH)
        return lambda: pl.semaphore_wait(barrier, len(others))


def halo(here, source, target, send, recv, step):
    copies = []
    for index in (0, 2, 1):
        src = index if step < 0 else 3 - index
        device = here.across[step][index]
        copies.append(remote(source.at[src], target.at[3 - src], send.at[index], recv.at[index], device))
    return copies


def begin(copies):
    for copy in copies:
        copy.start()


def end(copies):
    for copy in copies:
        copy.wait()


def wait_bytes(like, sem):
    pltpu.make_async_copy(like, like, sem).wait()


def room(*dims):
    return pltpu.VMEM((*dims, *TILE), BF16)


def tiles_in(block):
    narrow = block.astype(BF16)
    for c in range(block.shape[1] // 128):
        for r in range(block.shape[0] // 16):
            yield narrow[r * 16 : (r + 1) * 16, c * 128 : (c + 1) * 128]


def added(terms):
    total = terms[0].astype(F32)
    for term in terms[1:]:
        total = total + term.astype(F32)
    return total.astype(BF16)


class WeightSum:
    def __init__(self, here, out, refs):
        self.here, self.out = here, out
        self.src, self.r1, self.x2, self.x3, self.send, self.recv = refs

    @staticmethod
    def scratch(tiles):
        n1 = tiles // 24
        dma = pltpu.SemaphoreType.DMA
        return [room(3, RING, 2, n1), room(7, 3, n1), room(3, RING, n1), room(3, RING, n1), dma((4,)), dma((4,))]

    def put(self, block, first):
        n1 = self.src.shape[3]
        for at, tile in enumerate(tiles_in(block), first):
            self.src[at // (8 * n1), at // (2 * n1) % RING, at // n1 % 2, at % n1] = tile

    def phase(self, at, thirds=(0, 1, 2)):
        here, made = self.here, []
        sems = self.send.at[at], self.recv.at[at]
        if at in (0, 3):
            for k in range(7):
                for t in thirds:
                    device, slot, core = here.eight[t][k]
                    mine = self.out.at[t, here.slot[t][0], here.core]
                    if at == 0:
                        made.append(remote(self.src.at[t, slot, core], self.r1.at[k, t], *sems, device))
                    else:
                        made.append(remote(mine, mine, *sems, device))
        else:
            for k in FAR_FIRST:
                for t in range(3):
                    axis = (t + at) % 3
                    mine = (self.x2 if at == 1 else self.x3).at[t, here.slot[axis][0]]
                    made.append(remote(mine, mine, *sems, here.along[axis][k]))
        return made

    def start(self, *thirds):
        begin(self.phase(0, thirds))

    def step(self, at):
        like = self.r1 if at in (0, 3) else self.r1.at[pl.ds(0, 3)]
        wait_bytes(like, self.recv.at[at])
        wait_bytes(like, self.send.at[at])
        core = self.here.core
        for t in range(3):
            one, two, three = (self.here.slot[(t + i) % 3][0] for i in range(3))
            if at == 0:
                self.x2[t, two] = added([self.src[t, one, core]] + [self.r1[k, t] for k in range(7)])
            if at == 1:
                self.x3[t, three] = added([self.x2[t, k] for k in range(RING)])
            if at == 2:
                self.out[t, one, core] = added([self.x3[t, k] for k in range(RING)])
        if at < 3:
            begin(self.phase(at + 1))


class PairSum:
    def __init__(self, here, out, refs):
        self.here, self.out = here, out
        self.src, self.other, self.a1, self.r1, self.x2, self.x3, self.send, self.recv = refs

    @staticmethod
    def scratch(tiles):
        n1 = tiles // 24
        dma = pltpu.SemaphoreType.DMA
        return [
            room(2, tiles // 2), room(tiles // 2),
            room(3, RING, n1), room(3, RING - 1, n1), room(3, RING, n1), room(3, RING, n1),
            dma((6,)), dma((6,)),
        ]

    def put(self, block, first):
        each = self.src.shape[1]
        for at, tile in enumerate(tiles_in(block), first):
            self.src[at // each, at % each] = tile

    def get(self):
        n1 = self.a1.shape[2]
        return [self.out[i // (12 * n1), i // (4 * n1) % 3, i // n1 % 4, i % n1] for i in range(24 * n1)]

    def copies(self, at, axis_of, source, target):
        made = []
        for k in FAR_FIRST:
            for t in range(3):
                axis = (t + axis_of) % 3
                slot = self.here.slot[axis]
                made.append(
                    remote(
                        source(t, slot[k], slot[0]), target(t, k - 1, slot[0]),
                        self.send.at[at], self.recv.at[at], self.here.along[axis][k],
                    )
                )
        return made

    def phase(self, at):
        core = self.here.core
        if at == 0:
            return [remote(self.src.at[1 - core], self.other, self.send.at[0], self.recv.at[0], self.here.sibling)]
        if at == 1:
            return self.copies(1, 0, lambda t, to, me: self.a1.at[t, to], lambda t, k, me: self.r1.at[t, k])
        if at == 2:
            return self.copies(2, 1, lambda t, to, me: self.x2.at[t, me], lambda t, k, me: self.x2.at[t, me])
        if at == 3:
            return self.copies(3, 2, lambda t, to, me: self.x3.at[t, me], lambda t, k, me: self.x3.at[t, me])
        if at == 4:
            out = self.out.at[core]
            return self.copies(4, 0, lambda t, to, me: out.at[t, me], lambda t, k, me: out.at[t, me])
        return [remote(self.out.at[core], self.out.at[core], self.send.at[5], self.recv.at[5], self.here.sibling)]

    def start(self):
        begin(self.phase(0))

    def step(self, at):
        like = self.other if at in (0, 5) else self.r1
        wait_bytes(like, self.recv.at[at])
        wait_bytes(like, self.send.at[at])
        core = self.here.core
        if at == 0:
            total = self.src[core].astype(F32) + self.other[...].astype(F32)
            self.a1[...] = total.astype(BF16).reshape(self.a1.shape)
        for t in range(3):
            one, two, three = (self.here.slot[(t + i) % 3][0] for i in range(3))
            if at == 1:
                total = self.a1[t, one].astype(F32)
                for k in range(RING - 1):
                    total = total + self.r1[t, k].astype(F32)
                self.x2[t, two] = total.astype(BF16)
            if at in (2, 3):
                came = self.x2 if at == 2 else self.x3
                total = came[t, 0].astype(F32)
                for k in range(1, RING):
                    total = total + came[t, k].astype(F32)
                if at == 2:
                    self.x3[t, three] = total.astype(BF16)
                else:
                    self.out[core, t, one] = total.astype(BF16)
        if at < 5:
            begin(self.phase(at + 1))


class BiasSum:
    def __init__(self, here, out, refs):
        self.here, self.out = here, out
        self.src, self.r1, self.x2, self.send, self.recv = refs

    @staticmethod
    def scratch():
        each = B_TILES // 8
        dma = pltpu.SemaphoreType.DMA
        return [room(RING, 2, each), room(7, each), room(2, each), dma((3,)), dma((3,))]

    def put(self, block):
        each = B_TILES // 8
        last = block[:, 256:]
        shared = last[0:B_ROWS]
        for g in range(1, 288 // B_ROWS):
            shared = shared + pltpu.roll(last[g * B_ROWS : (g + 1) * B_ROWS], g * B_LEFT, 1)
        tiles = [*tiles_in(block[:, :256]), *tiles_in(shared), jnp.zeros(TILE, BF16)]
        for at, tile in enumerate(tiles):
            self.src[at // (2 * each), at // each % 2, at % each] = tile

    def get(self):
        each = B_TILES // 8
        tiles = [self.out[at // (2 * each), at // each % 2, at % each] for at in range(B_TILES)]
        first = joined(tiles[:36], 2)
        shared = joined(tiles[36:39], 1)
        last = [shared]
        for g in range(1, 288 // B_ROWS):
            last.append(pltpu.roll(shared, 128 - g * B_LEFT, 1))
        return jnp.concatenate([first, jnp.concatenate(last, axis=0)], axis=1)

    def phase(self, at):
        here, made = self.here, []
        sems = self.send.at[at], self.recv.at[at]
        if at == 1:
            return [remote(self.x2.at[0], self.x2.at[1], *sems, here.facing)]
        mine = self.out.at[here.slot[1][0], here.core]
        for k, (device, slot, core) in enumerate(here.eight[1]):
            if at == 0:
                made.append(remote(self.src.at[slot, core], self.r1.at[k], *sems, device))
            else:
                made.append(remote(mine, mine, *sems, device))
        return made

    def start(self):
        begin(self.phase(0))

    def step(self, at):
        like = self.x2.at[1] if at == 1 else self.r1
        wait_bytes(like, self.recv.at[at])
        wait_bytes(like, self.send.at[at])
        slot, core = self.here.slot[1][0], self.here.core
        if at == 0:
            self.x2[0] = added([self.src[slot, core]] + [self.r1[k] for k in range(7)])
        if at == 1:
            self.out[slot, core] = added([self.x2[0], self.x2[1]])
        if at < 2:
            begin(self.phase(at + 1))


def layer_norm(x):
    centered = x - jnp.mean(x, axis=-1, keepdims=True)
    spread = jnp.mean(centered * centered, axis=-1, keepdims=True)
    rate = lax.rsqrt(spread + EPSILON)
    return centered * rate, rate


def layer_norm_back(cot, unit, rate):
    first = jnp.mean(cot, axis=-1, keepdims=True)
    second = jnp.mean(cot * unit, axis=-1, keepdims=True)
    return rate * (cot - first - unit * second)


def head_mask(head):
    lane = lax.broadcasted_iota(jnp.int32, (1, C), 1)
    return (lane >= head * 32) & (lane < head * 32 + 32)


def stacked(value):
    wide = value.astype(F32)
    parts = [jnp.where(head_mask(h), wide, 0.0).astype(BF16) for h in range(HEADS)]
    return jnp.concatenate(parts, axis=0)


def unstacked(value):
    total = jnp.where(head_mask(0), value[0:WIN], 0.0)
    for h in range(1, HEADS):
        total = total + jnp.where(head_mask(h), value[h * WIN : (h + 1) * WIN], 0.0)
    return total


def expand_bias(last_lat, table, columns, index_rows, lanes, tall_table, gathered, strips, scores):
    for head in range(HEADS):
        tall_table[head * LWIN : (head + 1) * LWIN, :] = table[head]
    for site in range(SITE):
        lev, a = site // WLAT, site % WLAT
        for other in range(WLEV):
            start = ((lev * WLEV + other) * WLAT + a) * RUN
            gathered[site * WH : (site + 1) * WH, other * RUN : (other + 1) * RUN] = tall_table[
                :, start : start + RUN
            ]
    moved = sum(dot(part, lanes[...]) for part in pieces(gathered[...], 3))
    rows = one_hot(columns[:, 1:2], WH * 2 * SITE, SITE * WH)
    moved = sum(dot(rows, part) for part in pieces(moved, 3))
    code = columns[:, 2:3]
    moved = jnp.where((code & 8) != 0, pltpu.roll(moved, LANES - SITE, 1), moved) * LOG2E
    seen = jnp.where((code & 4) != 0, 1, 0) + jnp.where(last_lat, 2, 0)
    apart = (code ^ index_rows[2:3, 0:LANES]) & seen
    strips[...] = jnp.where(apart != 0, MASKED, moved)

    def one(wh, carry):
        strip = strips[pl.ds(pl.multiple_of(wh * 2 * SITE, 8), 2 * SITE), :]
        start = lax.rem(wh, LWIN) * STACK + lax.div(wh, LWIN) * WIN
        for pair in range(WLON // 2):
            offset = (WLON - 2 - 2 * pair) * SITE
            scores[pl.ds(pl.multiple_of(start + pair * 24, 8), 24), :] = strip[
                :, offset : offset + WIN
            ]
        return carry

    lax.fori_loop(0, WH, one, 0)


def collapse_bias(first, last, scores, strips):
    def one(wh, carry):
        start = lax.rem(wh, LWIN) * STACK + lax.div(wh, LWIN) * WIN
        total = jnp.zeros((2 * SITE, LANES), F32)
        for pair in range(WLON // 2):
            offset = (WLON - 2 - 2 * pair) * SITE
            part = scores[pl.ds(pl.multiple_of(start + pair * 24, 8), 24), :]
            part = jnp.concatenate([part, jnp.zeros((2 * SITE, LANES - WIN), F32)], axis=1)
            total = total + (pltpu.roll(part, offset, 1) if offset else part)
        strips[pl.ds(pl.multiple_of(wh * 2 * SITE, 8), 2 * SITE), :] = total
        return carry

    lax.fori_loop(first, last, one, 0)


def join_strips(strips, columns, index_rows):
    total = strips[...]
    total = jnp.where((columns[:, 2:3] & 8) != 0, pltpu.roll(total, SITE, 1), total)
    rows = one_hot(index_rows[1:2, :], SITE * WH, WH * 2 * SITE)
    return sum(dot(rows, part) for part in pieces(total, 2))


def block_kernel(n_lon, n_lat, *refs):
    loaded = refs[:9]
    out_field, grad_field, qkv, proj, fc1, fc2, bias = refs[9:16]
    field, cot, w_qkv, w_proj, w_fc1, w_fc2, table, columns, index_rows, load_sem = refs[16:26]
    (
        out, e_out, l_out, b_out, sent, came, cot_sent, cot_came, back, halo_send, halo_recv,
        xw, uw, scores, normed, query, key, value, unit, rate, blended, normed_two, hidden,
        cot_first, cot_mid, cot_q, cot_k, cot_v, ow, gw, tall_table, gathered, strips, w3,
        places_in, places_out, lanes, slope, unit_two, rate_two,
    ) = refs[26:66]
    here = Here(n_lon, n_lat)
    early = PairSum(here, e_out, refs[66:74])
    late = WeightSum(here, l_out, refs[74:80])
    strip_sum = BiasSum(here, b_out, refs[80:85])

    loads = [
        pltpu.make_async_copy(src, dst, load_sem.at[i]) for i, (src, dst) in enumerate(zip(loaded, refs[16:25]))
    ]
    loads[0].start()
    greeted = here.greet()
    begin(loads[6:9])
    loads[0].wait()
    for index in range(3):
        for part, chunk in enumerate(split(field, index)):
            sent[part, index] = pack(chunk)
    greeted()
    inward = [
        halo(here, sent.at[i], came.at[i], halo_send.at[i], halo_recv.at[i], -1) for i in range(2)
    ]
    cot_inward = halo(here, cot_sent, cot_came, halo_send.at[2], halo_recv.at[2], -1)
    outward = [
        halo(here, back.at[i], out.at[i], halo_send.at[3 + i], halo_recv.at[3 + i], 1) for i in range(2)
    ]
    begin(inward[0])
    begin(inward[1])
    begin(loads[1:6])
    end(loads[6:9])
    lanes[...] = one_hot(columns[0:STRIP, 3:4], STRIP, LANES)
    last_lat = here.lat == n_lat - 1
    expand_bias(last_lat, table, columns, index_rows, lanes, tall_table, gathered, strips, scores)
    places_in[...] = one_hot(columns[0:PAIR, 0:1], PAIR, PAIR)
    places_out[...] = one_hot(index_rows[0:1, 0:PAIR], PAIR, PAIR)
    loads[1].wait()
    for index in range(3):
        for part, chunk in enumerate(split(cot, index)):
            cot_sent[index, part] = pack(chunk)
    own = [split(ref, 3) for ref in (field, cot)]
    loads[2].wait()
    for third in range(3):
        w3[third] = w_qkv[:, third * C : (third + 1) * C]

    def gather(kind, part):
        if kind:
            arrived = [cot_came[i, part] for i in range(1, 4)]
        else:
            arrived = [came[part, i] for i in range(1, 4)]
        parts = [own[kind][part]] + [unpack(value) for value in arrived]
        return dot(places_in[...], jnp.concatenate(parts, axis=0).astype(BF16)).astype(BF16)

    def scatter(kind, ref):
        for part in range(2):
            whole = dot(places_out[...], ref[part * PAIR : (part + 1) * PAIR, :])
            out[kind, 3, part] = pack(whole[:CHUNK])
            for i in range(1, 4):
                back[kind, i, part] = pack(whole[i * CHUNK : (i + 1) * CHUNK])
        begin(outward[kind])

    def places(w):
        return pl.ds(w * WIN, WIN), pl.ds(w * STACK, STACK)

    def attend(w):
        rows, tall = places(w)
        unit_x, rate_x = layer_norm(xw[rows, :].astype(F32))
        unit[rows, :] = unit_x
        rate[rows, :] = rate_x
        norm = unit_x.astype(BF16)
        normed[rows, :] = norm
        q = dot(norm, w3[0]).astype(BF16)
        k = dot(norm, w3[1]).astype(BF16)
        v = dot(norm, w3[2]).astype(BF16)
        query[rows, :] = q
        key[rows, :] = k
        value[rows, :] = v
        s = dot_nt(stacked(q), k) * (SCALE * LOG2E) + scores[tall, :]
        e = jnp.exp2(s - jnp.max(s, axis=-1, keepdims=True))
        p = e * (1.0 / jnp.sum(e, axis=-1, keepdims=True))
        scores[tall, :] = p
        blended[rows, :] = unstacked(dot(p.astype(BF16), v)).astype(BF16)

    def feed(w):
        rows = pl.ds(w * 2 * WIN, 2 * WIN)
        middle = xw[rows, :].astype(F32) + dot(blended[rows, :], w_proj[...])
        middle = middle.astype(BF16).astype(F32)
        unit_m, rate_m = layer_norm(middle)
        norm_m = unit_m.astype(BF16)
        normed_two[rows, :] = norm_m
        first = dot(norm_m, w_fc1[...])
        phi = 0.5 + 0.5 * lax.erf(first * math.sqrt(0.5))
        hid = (first * phi).astype(BF16)
        hidden[rows, :] = hid
        bell = jnp.exp2(first * first * (-0.5 * LOG2E)) * (1.0 / math.sqrt(2.0 * math.pi))
        slope[rows, :] = phi + first * bell
        unit_two[rows, :] = unit_m
        rate_two[rows, :] = rate_m
        ow[rows, :] = (middle + dot_nt(hid, w_fc2[...])).astype(BF16)

    def feed_back(w):
        rows = pl.ds(w * 2 * WIN, 2 * WIN)
        up = uw[rows, :]
        c_first = (dot(up, w_fc2[...]).astype(BF16).astype(F32) * slope[rows, :]).astype(BF16)
        cot_first[rows, :] = c_first
        c_norm = dot_nt(c_first, w_fc1[...]).astype(BF16).astype(F32)
        c_mid = layer_norm_back(c_norm, unit_two[rows, :], rate_two[rows, :]).astype(BF16).astype(F32)
        cot_mid[rows, :] = (up.astype(F32) + c_mid).astype(BF16)

    def backward(w):
        rows, tall = places(w)
        up = cot_mid[rows, :]
        c_blend = stacked(dot_nt(up, w_proj[...]).astype(BF16))
        p = scores[tall, :]
        c_p = dot_nt(c_blend, value[rows, :])
        c_s = p * (c_p - jnp.sum(p * c_p, axis=-1, keepdims=True))
        scores[tall, :] = c_s
        c_v = dot_tn(p.astype(BF16), c_blend).astype(BF16)
        narrow = c_s.astype(BF16)
        c_q = (unstacked(dot(narrow, key[rows, :])) * SCALE).astype(BF16)
        c_k = (dot_tn(narrow, stacked(query[rows, :])) * SCALE).astype(BF16)
        cot_q[rows, :] = c_q
        cot_k[rows, :] = c_k
        cot_v[rows, :] = c_v

    def inputs_back(w):
        rows = pl.ds(w * 2 * WIN, 2 * WIN)
        c_norm = dot_nt(cot_q[rows, :], w3[0]) + dot_nt(cot_k[rows, :], w3[1])
        c_norm = (c_norm + dot_nt(cot_v[rows, :], w3[2])).astype(BF16).astype(F32)
        c_x = layer_norm_back(c_norm, unit[rows, :], rate[rows, :]).astype(BF16)
        gw[rows, :] = (cot_mid[rows, :].astype(F32) + c_x.astype(F32)).astype(BF16)

    for part in range(2):
        end(inward[part])
        xw[part * PAIR : (part + 1) * PAIR, :] = gather(0, part)
        if not part:
            begin(cot_inward)
        attend(2 * part)
        attend(2 * part + 1)
    end(loads[3:6])
    feed(0)
    feed(1)
    end(cot_inward)
    for part in range(2):
        uw[part * PAIR : (part + 1) * PAIR, :] = gather(1, part)
        feed_back(part)
    early.put(dot_tn(normed_two[...], cot_first[...]), 0)
    early.put(dot_tn(uw[...], hidden[...]), 72)
    early.start()
    backward(0)
    backward(1)
    early.step(0)
    backward(2)
    backward(3)
    norm = normed[...]
    late.put(jnp.concatenate([dot_tn(norm, cot_q[...]), dot_tn(norm, cot_k[...])], axis=1), 0)
    late.start(0)
    c_proj = dot_tn(blended[...], cot_mid[...])
    late.put(jnp.concatenate([dot_tn(norm, cot_v[...]), c_proj], axis=1), 36)
    late.start(1, 2)
    early.step(1)
    collapse_bias(0, WH, scores, strips)
    strip_sum.put(join_strips(strips, columns, index_rows))
    strip_sum.start()
    late.step(0)
    inputs_back(0)
    inputs_back(1)
    early.step(2)
    scatter(1, gw)
    late.step(1)
    strip_sum.step(0)
    scatter(0, ow)
    early.step(3)
    late.step(2)
    strip_sum.step(1)
    end(outward[1])
    for index in range(4):
        merge(grad_field, index, [unpack(out[1, index, part]) for part in range(2)])
    early.step(4)
    strip_sum.step(2)
    finish_bias(strip_sum.get(), lanes, tall_table, bias)
    end(outward[0])
    for index in range(4):
        merge(out_field, index, [unpack(out[0, index, part]) for part in range(2)])
    late.step(3)
    qkv[:, 0:384] = joined(tiles_of(l_out)[:36], 3)
    right = joined(tiles_of(l_out)[36:], 3)
    qkv[:, 384:576] = right[:, 0:C]
    proj[...] = right[:, C:]
    early.step(5)
    fc1[...] = joined(early.get()[:72], 6)
    fc2[...] = joined(early.get()[72:], 6)


def joined(tiles, columns):
    rows = len(tiles) // columns
    cols = [jnp.concatenate(tiles[c * rows : (c + 1) * rows], axis=0) for c in range(columns)]
    return jnp.concatenate(cols, axis=1).astype(F32)


def tiles_of(ref):
    n1 = ref.shape[3]
    return [ref[i // (8 * n1), i // (2 * n1) % RING, i // n1 % 2, i % n1] for i in range(24 * n1)]


def finish_bias(strip, lanes, tall_table, bias):
    runs = dot_nt(strip.astype(BF16), lanes[...])
    for site in range(SITE):
        lev, a = site // WLAT, site % WLAT
        for other in range(WLEV):
            start = ((lev * WLEV + other) * WLAT + a) * RUN
            tall_table[:, start : start + RUN] = runs[
                site * WH : (site + 1) * WH, other * RUN : (other + 1) * RUN
            ]
    for head in range(HEADS):
        bias[head] = tall_table[head * LWIN : (head + 1) * LWIN, :]


def finish_kernel(*refs):
    count = len(refs) // 2
    copies = [pltpu.make_async_copy(refs[i], refs[count + i], refs[-1].at[i]) for i in range(count)]
    copies.sort(key=lambda copy: -math.prod(copy.src_ref.shape))
    begin(copies)
    end(copies)


def per_device(n_lon, n_lat, field, w_qkv, w_proj, w_fc1, w_fc2, bias_table, cotangent):
    vmem, hbm = pl.BlockSpec(memory_space=pltpu.VMEM), pl.BlockSpec(memory_space=pltpu.HBM)
    shape = jax.ShapeDtypeStruct
    dma = pltpu.SemaphoreType.DMA
    rows = row_places()
    columns = columns_of(token_places(), rows, row_codes(), lane_places())
    index_rows = columns_of(token_places(), rows, lane_codes()).T.copy()
    inputs = (
        field, cotangent, w_qkv, w_proj, w_fc1, w_fc2.T, bias_table[0].transpose(1, 0, 2), columns, index_rows
    )
    inputs = [pltpu.with_memory_space_constraint(jnp.asarray(a), pltpu.HBM) for a in inputs]
    tile = shape((WLON, WLAT, LEV, C), BF16)
    outputs = (
        tile,
        tile,
        shape((C, 3 * C), F32),
        shape((C, C), F32),
        shape((C, HIDDEN), F32),
        shape((C, HIDDEN), F32),
        shape((HEADS, LWIN, POS), F32),
    )
    wide = lambda dtype, n=1: [pltpu.VMEM((TOK, C), dtype)] * n
    results = pl.pallas_call(
        functools.partial(block_kernel, n_lon, n_lat),
        out_shape=outputs,
        in_specs=[hbm] * len(inputs),
        out_specs=[vmem] * len(outputs),
        scratch_shapes=[
            *[pltpu.VMEM(a.shape, a.dtype) for a in inputs],
            dma((len(inputs),)),
            pltpu.VMEM((2, 4, 2, PACKED, 128), BF16),
            room(2, 3, RING, E_TILES // 24),
            room(3, RING, 2, L_TILES // 24),
            room(RING, 2, B_TILES // 8),
            pltpu.VMEM((2, 3, PACKED, 128), BF16),
            pltpu.VMEM((2, 4, PACKED, 128), BF16),
            pltpu.VMEM((3, 2, PACKED, 128), BF16),
            pltpu.VMEM((4, 2, PACKED, 128), BF16),
            pltpu.VMEM((2, 4, 2, PACKED, 128), BF16),
            dma((5, 3)),
            dma((5, 3)),
            *wide(BF16, 2),
            pltpu.VMEM((LWIN * STACK, WIN), F32),
            *wide(BF16, 4),
            *wide(F32),
            pltpu.VMEM((TOK, 1), F32),
            *wide(BF16, 2),
            pltpu.VMEM((TOK, HIDDEN), BF16),
            pltpu.VMEM((TOK, HIDDEN), BF16),
            *wide(BF16, 6),
            pltpu.VMEM((WH, POS), F32),
            pltpu.VMEM((SITE * WH, STRIP), F32),
            pltpu.VMEM((WH * 2 * SITE, LANES), F32),
            pltpu.VMEM((3, C, C), BF16),
            pltpu.VMEM((PAIR, PAIR), BF16),
            pltpu.VMEM((PAIR, PAIR), BF16),
            pltpu.VMEM((STRIP, LANES), BF16),
            pltpu.VMEM((TOK, HIDDEN), F32),
            *wide(F32),
            pltpu.VMEM((TOK, 1), F32),
            *PairSum.scratch(E_TILES),
            *WeightSum.scratch(L_TILES),
            *BiasSum.scratch(),
        ],
        compiler_params=pltpu.CompilerParams(
            vmem_limit_bytes=VMEM_LIMIT, collective_id=0, has_side_effects=True
        ),
        name="block",
    )(*inputs)
    *results, fc2, bias = pl.pallas_call(
        finish_kernel,
        out_shape=outputs,
        in_specs=[vmem] * len(outputs),
        out_specs=[hbm] * len(outputs),
        scratch_shapes=[dma((len(outputs),))],
        compiler_params=pltpu.CompilerParams(vmem_limit_bytes=VMEM_LIMIT),
        name="finish",
    )(*results)
    return (*results, fc2.T, bias.transpose(1, 0, 2)[None])


def solution(mesh):
    whole, tiles, banded = P(), P("lon", "lat", None, None), P("lat", None, None, None)
    return jax.shard_map(
        functools.partial(per_device, mesh.shape["lon"], mesh.shape["lat"]),
        mesh=mesh,
        in_specs=(tiles, whole, whole, whole, whole, banded, tiles),
        out_specs=(tiles, tiles, whole, whole, whole, whole, banded),
        check_vma=False,
    )
```

```python
import functools
import math

import jax
import jax.numpy as jnp
import numpy as np
from jax import lax
from jax.experimental import pallas as pl
from jax.experimental.pallas import tpu as pltpu
from jax.sharding import PartitionSpec as P

C = 192
HEADS = 6
HIDDEN = 768
LEV = 8
WLON = 12
WLAT = 6
WLEV = 2
LWIN = LEV // WLEV
WH = LWIN * HEADS
WIN = WLEV * WLAT * WLON
TOK = LWIN * WIN
QUAD = TOK // 4
SITE = WLEV * WLAT
SHIFTS = 2 * WLON - 1
STRIP = SHIFTS * SITE
POS = WLEV * WLEV * WLAT * WLAT * SHIFTS
RUN = WLAT * SHIFTS
LANES = 384
STACK = HEADS * WIN
EPSILON = 1e-05
MASKED = -1000000000.0
LOG2E = math.log2(math.e)
SCALE = 1.0 / math.sqrt(C // HEADS)
RING = 4
FAR_FIRST = (2, 1, 3)
E_TILES = 144
L_TILES = 72
B_TILES = 40
B_LEFT = STRIP - 256
B_ROWS = 48
CHUNK = QUAD // 2
PAIR = 4 * CHUNK
PACKED = 112
TILE = (16, 128)
BF16 = jnp.bfloat16
F32 = jnp.float32
MESH = pl.DeviceIdType.MESH
VMEM_LIMIT = 30 * 1024 * 1024


def token_places():
    w, o, lev, a = np.meshgrid(
        np.arange(2), np.arange(WLON), np.arange(WLEV), np.arange(WLAT), indexing="ij"
    )
    site = (o % 6) * 3 + a % 3
    row = (site % 9) * 8 + (site // 9) * 4 + 2 * w + lev
    return (((o // 6) * 2 + a // 3) * CHUNK + row).reshape(PAIR).astype(np.int32)


def lane_places():
    lev, a, d = np.meshgrid(np.arange(WLEV), np.arange(WLAT), np.arange(SHIFTS), indexing="ij")
    return ((SHIFTS - 1 - d) * SITE + lev * WLAT + a).reshape(STRIP).astype(np.int32)


def row_places():
    wh, _, site = np.meshgrid(np.arange(WH), np.arange(2), np.arange(SITE), indexing="ij")
    return (site * WH + wh).reshape(WH * 2 * SITE).astype(np.int32)


def row_codes():
    _, w, p, lev, a = np.meshgrid(
        np.arange(HEADS), np.arange(LWIN), np.arange(2), np.arange(WLEV), np.arange(WLAT), indexing="ij"
    )
    code = lev + 2 * (a >= WLAT // 2) + 4 * (w == LWIN - 1) + 8 * (p == 0)
    return code.reshape(WH * 2 * SITE).astype(np.int32)


def lane_codes():
    site = np.arange(LANES) % SITE
    return (site // WLAT + 2 * (site % WLAT >= WLAT // 2)).astype(np.int32)


def columns_of(*arrays):
    made = np.zeros((TOK, 8), np.int32)
    for i, array in enumerate(arrays):
        made[: len(array), i] = array
    return made


def dot(a, b):
    return jnp.dot(a, b, preferred_element_type=F32)


def dot_nt(a, b):
    return lax.dot_general(a, b, (((1,), (1,)), ((), ())), preferred_element_type=F32)


def dot_tn(a, b):
    return lax.dot_general(a, b, (((0,), (0,)), ((), ())), preferred_element_type=F32)


def one_hot(places, rows, cols):
    along = 1 if places.shape[1] == 1 else 0
    index = lax.broadcasted_iota(jnp.int32, (rows, cols), along)
    return jnp.where(index == places, 1.0, 0.0).astype(BF16)


def pieces(value, count):
    found = []
    for _ in range(count):
        part = value.astype(BF16)
        found.append(part)
        value = value - part.astype(F32)
    return found


def split(ref, index):
    part = ref[pl.ds((index // 2) * 6, 6), pl.ds((index % 2) * 3, 3)]
    part = pltpu.roll(part.astype(F32).reshape(18, LEV, C), LEV - 1, 1)
    low, high = part[:9], part[9:]
    upper = lax.broadcasted_iota(jnp.int32, low.shape, 1) < LEV // 2
    first = jnp.where(upper, low, pltpu.roll(high, LEV // 2, 1))
    second = jnp.where(upper, pltpu.roll(low, LEV // 2, 1), high)
    return first.reshape(CHUNK, C), second.reshape(CHUNK, C)


def merge(ref, index, chunks):
    first, second = (chunk.reshape(9, LEV, C) for chunk in chunks)
    upper = lax.broadcasted_iota(jnp.int32, first.shape, 1) < LEV // 2
    low = jnp.where(upper, first, pltpu.roll(second, LEV // 2, 1))
    high = jnp.where(upper, pltpu.roll(first, LEV // 2, 1), second)
    part = pltpu.roll(jnp.concatenate([low, high], axis=0), 1, 1)
    ref[pl.ds((index // 2) * 6, 6), pl.ds((index % 2) * 3, 3)] = part.reshape(6, 3, LEV, C).astype(BF16)


def pack(value):
    rest = jnp.concatenate([value[:40, 128:], value[32:, 128:]], axis=1)
    return jnp.concatenate([value[:, :128], rest], axis=0).astype(BF16)


def unpack(value):
    wide = value.astype(F32)
    rest = wide[CHUNK:]
    right = jnp.concatenate([rest[:, :64], rest[8:, 64:]], axis=0)
    return jnp.concatenate([wide[:CHUNK], right], axis=1)


def place_of(lon, lat):
    x = lax.rem(lat, 2) * 2 + lax.div(lon, 8)
    return (x, lax.rem(lax.div(lon, 2), RING), lax.div(lat, 2)), lax.rem(lon, 2)


def device_at(chip, core):
    x, y, z = chip
    return ((lax.rem(x, 2) * RING + y) * 2 + core, z * 2 + lax.div(x, 2))


def moved(chip, axis, step):
    return tuple(lax.rem(c + step, RING) if i == axis else c for i, c in enumerate(chip))


def remote(src, dst, send, recv, device):
    return pltpu.make_async_remote_copy(
        src_ref=src, dst_ref=dst, send_sem=send, recv_sem=recv, device_id=device, device_id_type=MESH
    )


class Here:
    def __init__(self, n_lon, n_lat):
        self.lon, self.lat = lax.axis_index("lon"), lax.axis_index("lat")
        self.chip, self.core = place_of(self.lon, self.lat)
        self.sibling = (self.lon + 1 - 2 * self.core, self.lat)
        self.slot = [[lax.rem(c + k, RING) for k in range(RING)] for c in self.chip]
        chips = [[moved(self.chip, axis, k) for k in range(RING)] for axis in range(3)]
        self.along = [[device_at(chip, self.core) for chip in ring] for ring in chips]
        other = 1 - self.core
        self.eight = []
        for axis in range(3):
            found = []
            for k in FAR_FIRST + (0,):
                if k:
                    found.append((self.along[axis][k], self.slot[axis][k], self.core))
                found.append((device_at(chips[axis][k], other), self.slot[axis][k], other))
            self.eight.append(found)
        self.facing = (lax.rem(self.lon + 8, 16), self.lat)
        self.across = {}
        for step in (-1, 1):
            to_lon = lax.rem(self.lon + n_lon + step, n_lon)
            to_lat = lax.rem(self.lat + n_lat + step, n_lat)
            self.across[step] = ((to_lon, to_lat), (to_lon, self.lat), (self.lon, to_lat))

    def greet(self):
        others = [*self.across[-1], *self.across[1], self.sibling]
        for axis in range(3):
            others += [device for device, _, _ in self.eight[axis][:-1]]
        barrier = pltpu.get_barrier_semaphore()
        for device in others:
            pl.semaphore_signal(barrier, inc=1, device_id=device, device_id_type=MESH)
        return lambda: pl.semaphore_wait(barrier, len(others))


def halo(here, source, target, send, recv, step):
    copies = []
    for index in (0, 2, 1):
        src = index if step < 0 else 3 - index
        device = here.across[step][index]
        copies.append(remote(source.at[src], target.at[3 - src], send.at[index], recv.at[index], device))
    return copies


def begin(copies):
    for copy in copies:
        copy.start()


def end(copies):
    for copy in copies:
        copy.wait()


def wait_bytes(like, sem):
    pltpu.make_async_copy(like, like, sem).wait()


def room(*dims):
    return pltpu.VMEM((*dims, *TILE), BF16)


def tiles_in(block):
    narrow = block.astype(BF16)
    for c in range(block.shape[1] // 128):
        for r in range(block.shape[0] // 16):
            yield narrow[r * 16 : (r + 1) * 16, c * 128 : (c + 1) * 128]


def added(terms):
    total = terms[0].astype(F32)
    for term in terms[1:]:
        total = total + term.astype(F32)
    return total.astype(BF16)


class WeightSum:
    def __init__(self, here, out, refs):
        self.here, self.out = here, out
        self.src, self.r1, self.x2, self.x3, self.send, self.recv = refs

    @staticmethod
    def scratch(tiles):
        n1 = tiles // 24
        dma = pltpu.SemaphoreType.DMA
        return [room(3, RING, 2, n1), room(7, 3, n1), room(3, RING, n1), room(3, RING, n1), dma((4,)), dma((4,))]

    def put(self, block, first):
        n1 = self.src.shape[3]
        for at, tile in enumerate(tiles_in(block), first):
            self.src[at // (8 * n1), at // (2 * n1) % RING, at // n1 % 2, at % n1] = tile

    def phase(self, at, thirds=(0, 1, 2)):
        here, made = self.here, []
        sems = self.send.at[at], self.recv.at[at]
        if at in (0, 3):
            for k in range(7):
                for t in thirds:
                    device, slot, core = here.eight[t][k]
                    mine = self.out.at[t, here.slot[t][0], here.core]
                    if at == 0:
                        made.append(remote(self.src.at[t, slot, core], self.r1.at[k, t], *sems, device))
                    else:
                        made.append(remote(mine, mine, *sems, device))
        else:
            for k in FAR_FIRST:
                for t in range(3):
                    axis = (t + at) % 3
                    mine = (self.x2 if at == 1 else self.x3).at[t, here.slot[axis][0]]
                    made.append(remote(mine, mine, *sems, here.along[axis][k]))
        return made

    def start(self, *thirds):
        begin(self.phase(0, thirds))

    def step(self, at):
        like = self.r1 if at in (0, 3) else self.r1.at[pl.ds(0, 3)]
        wait_bytes(like, self.recv.at[at])
        wait_bytes(like, self.send.at[at])
        core = self.here.core
        for t in range(3):
            one, two, three = (self.here.slot[(t + i) % 3][0] for i in range(3))
            if at == 0:
                self.x2[t, two] = added([self.src[t, one, core]] + [self.r1[k, t] for k in range(7)])
            if at == 1:
                self.x3[t, three] = added([self.x2[t, k] for k in range(RING)])
            if at == 2:
                self.out[t, one, core] = added([self.x3[t, k] for k in range(RING)])
        if at < 3:
            begin(self.phase(at + 1))


class PairSum:
    def __init__(self, here, out, refs):
        self.here, self.out = here, out
        self.src, self.other, self.a1, self.r1, self.x2, self.x3, self.send, self.recv = refs

    @staticmethod
    def scratch(tiles):
        n1 = tiles // 24
        dma = pltpu.SemaphoreType.DMA
        return [
            room(2, tiles // 2), room(tiles // 2),
            room(3, RING, n1), room(3, RING - 1, n1), room(3, RING, n1), room(3, RING, n1),
            dma((6,)), dma((6,)),
        ]

    def put(self, block, first):
        each = self.src.shape[1]
        for at, tile in enumerate(tiles_in(block), first):
            self.src[at // each, at % each] = tile

    def get(self):
        n1 = self.a1.shape[2]
        return [self.out[i // (12 * n1), i // (4 * n1) % 3, i // n1 % 4, i % n1] for i in range(24 * n1)]

    def copies(self, at, axis_of, source, target):
        made = []
        for k in FAR_FIRST:
            for t in range(3):
                axis = (t + axis_of) % 3
                slot = self.here.slot[axis]
                made.append(
                    remote(
                        source(t, slot[k], slot[0]), target(t, k - 1, slot[0]),
                        self.send.at[at], self.recv.at[at], self.here.along[axis][k],
                    )
                )
        return made

    def phase(self, at):
        core = self.here.core
        if at == 0:
            return [remote(self.src.at[1 - core], self.other, self.send.at[0], self.recv.at[0], self.here.sibling)]
        if at == 1:
            return self.copies(1, 0, lambda t, to, me: self.a1.at[t, to], lambda t, k, me: self.r1.at[t, k])
        if at == 2:
            return self.copies(2, 1, lambda t, to, me: self.x2.at[t, me], lambda t, k, me: self.x2.at[t, me])
        if at == 3:
            return self.copies(3, 2, lambda t, to, me: self.x3.at[t, me], lambda t, k, me: self.x3.at[t, me])
        if at == 4:
            out = self.out.at[core]
            return self.copies(4, 0, lambda t, to, me: out.at[t, me], lambda t, k, me: out.at[t, me])
        return [remote(self.out.at[core], self.out.at[core], self.send.at[5], self.recv.at[5], self.here.sibling)]

    def start(self):
        begin(self.phase(0))

    def step(self, at):
        like = self.other if at in (0, 5) else self.r1
        wait_bytes(like, self.recv.at[at])
        wait_bytes(like, self.send.at[at])
        core = self.here.core
        if at == 0:
            total = self.src[core].astype(F32) + self.other[...].astype(F32)
            self.a1[...] = total.astype(BF16).reshape(self.a1.shape)
        for t in range(3):
            one, two, three = (self.here.slot[(t + i) % 3][0] for i in range(3))
            if at == 1:
                total = self.a1[t, one].astype(F32)
                for k in range(RING - 1):
                    total = total + self.r1[t, k].astype(F32)
                self.x2[t, two] = total.astype(BF16)
            if at in (2, 3):
                came = self.x2 if at == 2 else self.x3
                total = came[t, 0].astype(F32)
                for k in range(1, RING):
                    total = total + came[t, k].astype(F32)
                if at == 2:
                    self.x3[t, three] = total.astype(BF16)
                else:
                    self.out[core, t, one] = total.astype(BF16)
        if at < 5:
            begin(self.phase(at + 1))


class BiasSum:
    def __init__(self, here, out, refs):
        self.here, self.out = here, out
        self.src, self.r1, self.x2, self.send, self.recv = refs

    @staticmethod
    def scratch():
        each = B_TILES // 8
        dma = pltpu.SemaphoreType.DMA
        return [room(RING, 2, each), room(7, each), room(2, each), dma((3,)), dma((3,))]

    def put(self, block):
        each = B_TILES // 8
        last = block[:, 256:]
        shared = last[0:B_ROWS]
        for g in range(1, 288 // B_ROWS):
            shared = shared + pltpu.roll(last[g * B_ROWS : (g + 1) * B_ROWS], g * B_LEFT, 1)
        tiles = [*tiles_in(block[:, :256]), *tiles_in(shared), jnp.zeros(TILE, BF16)]
        for at, tile in enumerate(tiles):
            self.src[at // (2 * each), at // each % 2, at % each] = tile

    def get(self):
        each = B_TILES // 8
        tiles = [self.out[at // (2 * each), at // each % 2, at % each] for at in range(B_TILES)]
        first = joined(tiles[:36], 2)
        shared = joined(tiles[36:39], 1)
        last = [shared]
        for g in range(1, 288 // B_ROWS):
            last.append(pltpu.roll(shared, 128 - g * B_LEFT, 1))
        return jnp.concatenate([first, jnp.concatenate(last, axis=0)], axis=1)

    def phase(self, at):
        here, made = self.here, []
        sems = self.send.at[at], self.recv.at[at]
        if at == 1:
            return [remote(self.x2.at[0], self.x2.at[1], *sems, here.facing)]
        mine = self.out.at[here.slot[1][0], here.core]
        for k, (device, slot, core) in enumerate(here.eight[1]):
            if at == 0:
                made.append(remote(self.src.at[slot, core], self.r1.at[k], *sems, device))
            else:
                made.append(remote(mine, mine, *sems, device))
        return made

    def start(self):
        begin(self.phase(0))

    def step(self, at):
        like = self.x2.at[1] if at == 1 else self.r1
        wait_bytes(like, self.recv.at[at])
        wait_bytes(like, self.send.at[at])
        slot, core = self.here.slot[1][0], self.here.core
        if at == 0:
            self.x2[0] = added([self.src[slot, core]] + [self.r1[k] for k in range(7)])
        if at == 1:
            self.out[slot, core] = added([self.x2[0], self.x2[1]])
        if at < 2:
            begin(self.phase(at + 1))


def layer_norm(x):
    centered = x - jnp.mean(x, axis=-1, keepdims=True)
    spread = jnp.mean(centered * centered, axis=-1, keepdims=True)
    rate = lax.rsqrt(spread + EPSILON)
    return centered * rate, rate


def layer_norm_back(cot, unit, rate):
    first = jnp.mean(cot, axis=-1, keepdims=True)
    second = jnp.mean(cot * unit, axis=-1, keepdims=True)
    return rate * (cot - first - unit * second)


def head_mask(head):
    lane = lax.broadcasted_iota(jnp.int32, (1, C), 1)
    return (lane >= head * 32) & (lane < head * 32 + 32)


def stacked(value):
    wide = value.astype(F32)
    parts = [jnp.where(head_mask(h), wide, 0.0).astype(BF16) for h in range(HEADS)]
    return jnp.concatenate(parts, axis=0)


def unstacked(value):
    total = jnp.where(head_mask(0), value[0:WIN], 0.0)
    for h in range(1, HEADS):
        total = total + jnp.where(head_mask(h), value[h * WIN : (h + 1) * WIN], 0.0)
    return total


def expand_bias(last_lat, table, columns, index_rows, lanes, tall_table, gathered, strips, scores):
    for head in range(HEADS):
        tall_table[head * LWIN : (head + 1) * LWIN, :] = table[head]
    for site in range(SITE):
        lev, a = site // WLAT, site % WLAT
        for other in range(WLEV):
            start = ((lev * WLEV + other) * WLAT + a) * RUN
            gathered[site * WH : (site + 1) * WH, other * RUN : (other + 1) * RUN] = tall_table[
                :, start : start + RUN
            ]
    moved = sum(dot(part, lanes[...]) for part in pieces(gathered[...], 3))
    rows = one_hot(columns[:, 1:2], WH * 2 * SITE, SITE * WH)
    moved = sum(dot(rows, part) for part in pieces(moved, 3))
    code = columns[:, 2:3]
    moved = jnp.where((code & 8) != 0, pltpu.roll(moved, LANES - SITE, 1), moved) * LOG2E
    seen = jnp.where((code & 4) != 0, 1, 0) + jnp.where(last_lat, 2, 0)
    apart = (code ^ index_rows[2:3, 0:LANES]) & seen
    strips[...] = jnp.where(apart != 0, MASKED, moved)

    def one(wh, carry):
        strip = strips[pl.ds(pl.multiple_of(wh * 2 * SITE, 8), 2 * SITE), :]
        start = lax.rem(wh, LWIN) * STACK + lax.div(wh, LWIN) * WIN
        for pair in range(WLON // 2):
            offset = (WLON - 2 - 2 * pair) * SITE
            scores[pl.ds(pl.multiple_of(start + pair * 24, 8), 24), :] = strip[
                :, offset : offset + WIN
            ]
        return carry

    lax.fori_loop(0, WH, one, 0)


def collapse_bias(first, last, scores, strips):
    def one(wh, carry):
        start = lax.rem(wh, LWIN) * STACK + lax.div(wh, LWIN) * WIN
        total = jnp.zeros((2 * SITE, LANES), F32)
        for pair in range(WLON // 2):
            offset = (WLON - 2 - 2 * pair) * SITE
            part = scores[pl.ds(pl.multiple_of(start + pair * 24, 8), 24), :]
            part = jnp.concatenate([part, jnp.zeros((2 * SITE, LANES - WIN), F32)], axis=1)
            total = total + (pltpu.roll(part, offset, 1) if offset else part)
        strips[pl.ds(pl.multiple_of(wh * 2 * SITE, 8), 2 * SITE), :] = total
        return carry

    lax.fori_loop(first, last, one, 0)


def join_strips(strips, columns, index_rows):
    total = strips[...]
    total = jnp.where((columns[:, 2:3] & 8) != 0, pltpu.roll(total, SITE, 1), total)
    rows = one_hot(index_rows[1:2, :], SITE * WH, WH * 2 * SITE)
    return sum(dot(rows, part) for part in pieces(total, 2))


def block_kernel(n_lon, n_lat, *refs):
    loaded = refs[:9]
    out_field, grad_field, qkv, proj, fc1, fc2, bias = refs[9:16]
    field, cot, w_qkv, w_proj, w_fc1, w_fc2, table, columns, index_rows, load_sem = refs[16:26]
    (
        out, e_out, l_out, b_out, sent, came, cot_sent, cot_came, back, halo_send, halo_recv,
        xw, uw, scores, normed, query, key, value, unit, rate, blended, normed_two, hidden,
        cot_first, cot_mid, cot_q, cot_k, cot_v, ow, gw, tall_table, gathered, strips, w3,
        places_in, places_out, lanes, slope, unit_two, rate_two,
    ) = refs[26:66]
    here = Here(n_lon, n_lat)
    early = PairSum(here, e_out, refs[66:74])
    late = WeightSum(here, l_out, refs[74:80])
    strip_sum = BiasSum(here, b_out, refs[80:85])

    loads = [
        pltpu.make_async_copy(src, dst, load_sem.at[i]) for i, (src, dst) in enumerate(zip(loaded, refs[16:25]))
    ]
    loads[0].start()
    greeted = here.greet()
    begin(loads[6:9])
    loads[0].wait()
    chunks = [split(field, index) for index in range(3)]
    for index in range(3):
        sent[0, index] = pack(chunks[index][0])
    greeted()
    inward = [
        halo(here, sent.at[i], came.at[i], halo_send.at[i], halo_recv.at[i], -1) for i in range(2)
    ]
    cot_inward = halo(here, cot_sent, cot_came, halo_send.at[2], halo_recv.at[2], -1)
    outward = [
        halo(here, back.at[i], out.at[i], halo_send.at[3 + i], halo_recv.at[3 + i], 1) for i in range(2)
    ]
    begin(inward[0])
    for index in range(3):
        sent[1, index] = pack(chunks[index][1])
    begin(inward[1])
    begin(loads[1:6])
    end(loads[6:9])
    lanes[...] = one_hot(columns[0:STRIP, 3:4], STRIP, LANES)
    last_lat = here.lat == n_lat - 1
    expand_bias(last_lat, table, columns, index_rows, lanes, tall_table, gathered, strips, scores)
    places_in[...] = one_hot(columns[0:PAIR, 0:1], PAIR, PAIR)
    places_out[...] = one_hot(index_rows[0:1, 0:PAIR], PAIR, PAIR)
    loads[1].wait()
    for index in range(3):
        for part, chunk in enumerate(split(cot, index)):
            cot_sent[index, part] = pack(chunk)
    own = [split(ref, 3) for ref in (field, cot)]
    loads[2].wait()
    for third in range(3):
        w3[third] = w_qkv[:, third * C : (third + 1) * C]

    def gather(kind, part):
        if kind:
            arrived = [cot_came[i, part] for i in range(1, 4)]
        else:
            arrived = [came[part, i] for i in range(1, 4)]
        parts = [own[kind][part]] + [unpack(value) for value in arrived]
        return dot(places_in[...], jnp.concatenate(parts, axis=0).astype(BF16)).astype(BF16)

    def scatter(kind, ref):
        for part in range(2):
            whole = dot(places_out[...], ref[part * PAIR : (part + 1) * PAIR, :])
            out[kind, 3, part] = pack(whole[:CHUNK])
            for i in range(1, 4):
                back[kind, i, part] = pack(whole[i * CHUNK : (i + 1) * CHUNK])
        begin(outward[kind])

    def places(w):
        return pl.ds(w * WIN, WIN), pl.ds(w * STACK, STACK)

    def attend(w):
        rows, tall = places(w)
        unit_x, rate_x = layer_norm(xw[rows, :].astype(F32))
        unit[rows, :] = unit_x
        rate[rows, :] = rate_x
        norm = unit_x.astype(BF16)
        normed[rows, :] = norm
        q = dot(norm, w3[0]).astype(BF16)
        k = dot(norm, w3[1]).astype(BF16)
        v = dot(norm, w3[2]).astype(BF16)
        query[rows, :] = q
        key[rows, :] = k
        value[rows, :] = v
        s = dot_nt(stacked(q), k) * (SCALE * LOG2E) + scores[tall, :]
        e = jnp.exp2(s - jnp.max(s, axis=-1, keepdims=True))
        p = e * (1.0 / jnp.sum(e, axis=-1, keepdims=True))
        scores[tall, :] = p
        blended[rows, :] = unstacked(dot(p.astype(BF16), v)).astype(BF16)

    def feed(w):
        rows = pl.ds(w * 2 * WIN, 2 * WIN)
        middle = xw[rows, :].astype(F32) + dot(blended[rows, :], w_proj[...])
        middle = middle.astype(BF16).astype(F32)
        unit_m, rate_m = layer_norm(middle)
        norm_m = unit_m.astype(BF16)
        normed_two[rows, :] = norm_m
        first = dot(norm_m, w_fc1[...])
        phi = 0.5 + 0.5 * lax.erf(first * math.sqrt(0.5))
        hid = (first * phi).astype(BF16)
        hidden[rows, :] = hid
        bell = jnp.exp2(first * first * (-0.5 * LOG2E)) * (1.0 / math.sqrt(2.0 * math.pi))
        slope[rows, :] = phi + first * bell
        unit_two[rows, :] = unit_m
        rate_two[rows, :] = rate_m
        ow[rows, :] = (middle + dot_nt(hid, w_fc2[...])).astype(BF16)

    def feed_back(w):
        rows = pl.ds(w * 2 * WIN, 2 * WIN)
        up = uw[rows, :]
        c_first = (dot(up, w_fc2[...]).astype(BF16).astype(F32) * slope[rows, :]).astype(BF16)
        cot_first[rows, :] = c_first
        c_norm = dot_nt(c_first, w_fc1[...]).astype(BF16).astype(F32)
        c_mid = layer_norm_back(c_norm, unit_two[rows, :], rate_two[rows, :]).astype(BF16).astype(F32)
        cot_mid[rows, :] = (up.astype(F32) + c_mid).astype(BF16)

    def backward(w):
        rows, tall = places(w)
        up = cot_mid[rows, :]
        c_blend = stacked(dot_nt(up, w_proj[...]).astype(BF16))
        p = scores[tall, :]
        c_p = dot_nt(c_blend, value[rows, :])
        c_s = p * (c_p - jnp.sum(p * c_p, axis=-1, keepdims=True))
        scores[tall, :] = c_s
        c_v = dot_tn(p.astype(BF16), c_blend).astype(BF16)
        narrow = c_s.astype(BF16)
        c_q = (unstacked(dot(narrow, key[rows, :])) * SCALE).astype(BF16)
        c_k = (dot_tn(narrow, stacked(query[rows, :])) * SCALE).astype(BF16)
        cot_q[rows, :] = c_q
        cot_k[rows, :] = c_k
        cot_v[rows, :] = c_v

    def inputs_back(w):
        rows = pl.ds(w * 2 * WIN, 2 * WIN)
        c_norm = dot_nt(cot_q[rows, :], w3[0]) + dot_nt(cot_k[rows, :], w3[1])
        c_norm = (c_norm + dot_nt(cot_v[rows, :], w3[2])).astype(BF16).astype(F32)
        c_x = layer_norm_back(c_norm, unit[rows, :], rate[rows, :]).astype(BF16)
        gw[rows, :] = (cot_mid[rows, :].astype(F32) + c_x.astype(F32)).astype(BF16)

    for part in range(2):
        end(inward[part])
        xw[part * PAIR : (part + 1) * PAIR, :] = gather(0, part)
        if not part:
            begin(cot_inward)
        attend(2 * part)
        attend(2 * part + 1)
    end(loads[3:6])
    feed(0)
    feed(1)
    scatter(0, ow)
    end(cot_inward)
    for part in range(2):
        uw[part * PAIR : (part + 1) * PAIR, :] = gather(1, part)
        feed_back(part)
    early.put(dot_tn(normed_two[...], cot_first[...]), 0)
    early.put(dot_tn(uw[...], hidden[...]), 72)
    early.start()
    backward(0)
    backward(1)
    early.step(0)
    backward(2)
    backward(3)
    norm = normed[...]
    late.put(jnp.concatenate([dot_tn(norm, cot_q[...]), dot_tn(norm, cot_k[...])], axis=1), 0)
    late.start(0)
    c_proj = dot_tn(blended[...], cot_mid[...])
    late.put(jnp.concatenate([dot_tn(norm, cot_v[...]), c_proj], axis=1), 36)
    late.start(1, 2)
    early.step(1)
    collapse_bias(0, WH, scores, strips)
    strip_sum.put(join_strips(strips, columns, index_rows))
    strip_sum.start()
    late.step(0)
    inputs_back(0)
    inputs_back(1)
    early.step(2)
    scatter(1, gw)
    late.step(1)
    strip_sum.step(0)
    early.step(3)
    late.step(2)
    strip_sum.step(1)
    end(outward[1])
    for index in range(4):
        merge(grad_field, index, [unpack(out[1, index, part]) for part in range(2)])
    early.step(4)
    strip_sum.step(2)
    finish_bias(strip_sum.get(), lanes, tall_table, bias)
    end(outward[0])
    for index in range(4):
        merge(out_field, index, [unpack(out[0, index, part]) for part in range(2)])
    late.step(3)
    qkv[:, 0:384] = joined(tiles_of(l_out)[:36], 3)
    right = joined(tiles_of(l_out)[36:], 3)
    qkv[:, 384:576] = right[:, 0:C]
    proj[...] = right[:, C:]
    early.step(5)
    fc1[...] = joined(early.get()[:72], 6)
    fc2[...] = joined(early.get()[72:], 6)


def joined(tiles, columns):
    rows = len(tiles) // columns
    cols = [jnp.concatenate(tiles[c * rows : (c + 1) * rows], axis=0) for c in range(columns)]
    return jnp.concatenate(cols, axis=1).astype(F32)


def tiles_of(ref):
    n1 = ref.shape[3]
    return [ref[i // (8 * n1), i // (2 * n1) % RING, i // n1 % 2, i % n1] for i in range(24 * n1)]


def finish_bias(strip, lanes, tall_table, bias):
    runs = dot_nt(strip.astype(BF16), lanes[...])
    for site in range(SITE):
        lev, a = site // WLAT, site % WLAT
        for other in range(WLEV):
            start = ((lev * WLEV + other) * WLAT + a) * RUN
            tall_table[:, start : start + RUN] = runs[
                site * WH : (site + 1) * WH, other * RUN : (other + 1) * RUN
            ]
    for head in range(HEADS):
        bias[head] = tall_table[head * LWIN : (head + 1) * LWIN, :]


def finish_kernel(*refs):
    count = len(refs) // 2
    copies = [pltpu.make_async_copy(refs[i], refs[count + i], refs[-1].at[i]) for i in range(count)]
    copies.sort(key=lambda copy: -math.prod(copy.src_ref.shape))
    begin(copies)
    end(copies)


def per_device(n_lon, n_lat, field, w_qkv, w_proj, w_fc1, w_fc2, bias_table, cotangent):
    vmem, hbm = pl.BlockSpec(memory_space=pltpu.VMEM), pl.BlockSpec(memory_space=pltpu.HBM)
    shape = jax.ShapeDtypeStruct
    dma = pltpu.SemaphoreType.DMA
    rows = row_places()
    columns = columns_of(token_places(), rows, row_codes(), lane_places())
    index_rows = columns_of(token_places(), rows, lane_codes()).T.copy()
    inputs = (
        field, cotangent, w_qkv, w_proj, w_fc1, w_fc2.T, bias_table[0].transpose(1, 0, 2), columns, index_rows
    )
    inputs = [pltpu.with_memory_space_constraint(jnp.asarray(a), pltpu.HBM) for a in inputs]
    tile = shape((WLON, WLAT, LEV, C), BF16)
    outputs = (
        tile,
        tile,
        shape((C, 3 * C), F32),
        shape((C, C), F32),
        shape((C, HIDDEN), F32),
        shape((C, HIDDEN), F32),
        shape((HEADS, LWIN, POS), F32),
    )
    wide = lambda dtype, n=1: [pltpu.VMEM((TOK, C), dtype)] * n
    results = pl.pallas_call(
        functools.partial(block_kernel, n_lon, n_lat),
        out_shape=outputs,
        in_specs=[hbm] * len(inputs),
        out_specs=[vmem] * len(outputs),
        scratch_shapes=[
            *[pltpu.VMEM(a.shape, a.dtype) for a in inputs],
            dma((len(inputs),)),
            pltpu.VMEM((2, 4, 2, PACKED, 128), BF16),
            room(2, 3, RING, E_TILES // 24),
            room(3, RING, 2, L_TILES // 24),
            room(RING, 2, B_TILES // 8),
            pltpu.VMEM((2, 3, PACKED, 128), BF16),
            pltpu.VMEM((2, 4, PACKED, 128), BF16),
            pltpu.VMEM((3, 2, PACKED, 128), BF16),
            pltpu.VMEM((4, 2, PACKED, 128), BF16),
            pltpu.VMEM((2, 4, 2, PACKED, 128), BF16),
            dma((5, 3)),
            dma((5, 3)),
            *wide(BF16, 2),
            pltpu.VMEM((LWIN * STACK, WIN), F32),
            *wide(BF16, 4),
            *wide(F32),
            pltpu.VMEM((TOK, 1), F32),
            *wide(BF16, 2),
            pltpu.VMEM((TOK, HIDDEN), BF16),
            pltpu.VMEM((TOK, HIDDEN), BF16),
            *wide(BF16, 6),
            pltpu.VMEM((WH, POS), F32),
            pltpu.VMEM((SITE * WH, STRIP), F32),
            pltpu.VMEM((WH * 2 * SITE, LANES), F32),
            pltpu.VMEM((3, C, C), BF16),
            pltpu.VMEM((PAIR, PAIR), BF16),
            pltpu.VMEM((PAIR, PAIR), BF16),
            pltpu.VMEM((STRIP, LANES), BF16),
            pltpu.VMEM((TOK, HIDDEN), F32),
            *wide(F32),
            pltpu.VMEM((TOK, 1), F32),
            *PairSum.scratch(E_TILES),
            *WeightSum.scratch(L_TILES),
            *BiasSum.scratch(),
        ],
        compiler_params=pltpu.CompilerParams(
            vmem_limit_bytes=VMEM_LIMIT, collective_id=0, has_side_effects=True
        ),
        name="block",
    )(*inputs)
    *results, fc2, bias = pl.pallas_call(
        finish_kernel,
        out_shape=outputs,
        in_specs=[vmem] * len(outputs),
        out_specs=[hbm] * len(outputs),
        scratch_shapes=[dma((len(outputs),))],
        compiler_params=pltpu.CompilerParams(vmem_limit_bytes=VMEM_LIMIT),
        name="finish",
    )(*results)
    return (*results, fc2.T, bias.transpose(1, 0, 2)[None])


def solution(mesh):
    whole, tiles, banded = P(), P("lon", "lat", None, None), P("lat", None, None, None)
    return jax.shard_map(
        functools.partial(per_device, mesh.shape["lon"], mesh.shape["lat"]),
        mesh=mesh,
        in_specs=(tiles, whole, whole, whole, whole, banded, tiles),
        out_specs=(tiles, tiles, whole, whole, whole, whole, banded),
        check_vma=False,
    )
```

```python
import functools
import math

import jax
import jax.numpy as jnp
import numpy as np
from jax import lax
from jax.experimental import pallas as pl
from jax.experimental.pallas import tpu as pltpu
from jax.sharding import PartitionSpec as P

C = 192
HEADS = 6
HIDDEN = 768
LEV = 8
WLON = 12
WLAT = 6
WLEV = 2
LWIN = LEV // WLEV
WH = LWIN * HEADS
WIN = WLEV * WLAT * WLON
TOK = LWIN * WIN
QUAD = TOK // 4
SITE = WLEV * WLAT
SHIFTS = 2 * WLON - 1
STRIP = SHIFTS * SITE
POS = WLEV * WLEV * WLAT * WLAT * SHIFTS
RUN = WLAT * SHIFTS
LANES = 384
STACK = HEADS * WIN
EPSILON = 1e-05
MASKED = -1000000000.0
LOG2E = math.log2(math.e)
SCALE = 1.0 / math.sqrt(C // HEADS)
RING = 4
FAR_FIRST = (2, 1, 3)
E_TILES = 144
L_TILES = 72
B_TILES = 40
B_LEFT = STRIP - 256
B_ROWS = 48
CHUNK = QUAD // 2
PAIR = 4 * CHUNK
PACKED = 112
TILE = (16, 128)
BF16 = jnp.bfloat16
F32 = jnp.float32
MESH = pl.DeviceIdType.MESH
VMEM_LIMIT = 30 * 1024 * 1024


def token_places():
    w, o, lev, a = np.meshgrid(
        np.arange(2), np.arange(WLON), np.arange(WLEV), np.arange(WLAT), indexing="ij"
    )
    site = (o % 6) * 3 + a % 3
    row = (site % 9) * 8 + (site // 9) * 4 + 2 * w + lev
    return (((o // 6) * 2 + a // 3) * CHUNK + row).reshape(PAIR).astype(np.int32)


def lane_places():
    lev, a, d = np.meshgrid(np.arange(WLEV), np.arange(WLAT), np.arange(SHIFTS), indexing="ij")
    return ((SHIFTS - 1 - d) * SITE + lev * WLAT + a).reshape(STRIP).astype(np.int32)


def row_codes():
    lev, a, _, w = np.meshgrid(
        np.arange(WLEV), np.arange(WLAT), np.arange(HEADS), np.arange(LWIN), indexing="ij"
    )
    code = lev + 2 * (a >= WLAT // 2) + 4 * (w == LWIN - 1)
    return code.reshape(SITE * WH).astype(np.int32)


def lane_codes():
    site = np.arange(LANES) % SITE
    return (site // WLAT + 2 * (site % WLAT >= WLAT // 2)).astype(np.int32)


def columns_of(*arrays):
    made = np.zeros((TOK, 8), np.int32)
    for i, array in enumerate(arrays):
        made[: len(array), i] = array
    return made


def dot(a, b):
    return jnp.dot(a, b, preferred_element_type=F32)


def dot_nt(a, b):
    return lax.dot_general(a, b, (((1,), (1,)), ((), ())), preferred_element_type=F32)


def dot_tn(a, b):
    return lax.dot_general(a, b, (((0,), (0,)), ((), ())), preferred_element_type=F32)


def one_hot(places, rows, cols):
    along = 1 if places.shape[1] == 1 else 0
    index = lax.broadcasted_iota(jnp.int32, (rows, cols), along)
    return jnp.where(index == places, 1.0, 0.0).astype(BF16)


def pieces(value, count):
    found = []
    for _ in range(count):
        part = value.astype(BF16)
        found.append(part)
        value = value - part.astype(F32)
    return found


def split(ref, index):
    part = ref[pl.ds((index // 2) * 6, 6), pl.ds((index % 2) * 3, 3)]
    part = pltpu.roll(part.astype(F32).reshape(18, LEV, C), LEV - 1, 1)
    low, high = part[:9], part[9:]
    upper = lax.broadcasted_iota(jnp.int32, low.shape, 1) < LEV // 2
    first = jnp.where(upper, low, pltpu.roll(high, LEV // 2, 1))
    second = jnp.where(upper, pltpu.roll(low, LEV // 2, 1), high)
    return first.reshape(CHUNK, C), second.reshape(CHUNK, C)


def merge(ref, index, chunks):
    first, second = (chunk.reshape(9, LEV, C) for chunk in chunks)
    upper = lax.broadcasted_iota(jnp.int32, first.shape, 1) < LEV // 2
    low = jnp.where(upper, first, pltpu.roll(second, LEV // 2, 1))
    high = jnp.where(upper, pltpu.roll(first, LEV // 2, 1), second)
    part = pltpu.roll(jnp.concatenate([low, high], axis=0), 1, 1)
    ref[pl.ds((index // 2) * 6, 6), pl.ds((index % 2) * 3, 3)] = part.reshape(6, 3, LEV, C).astype(BF16)


def pack(value):
    rest = jnp.concatenate([value[:40, 128:], value[32:, 128:]], axis=1)
    return jnp.concatenate([value[:, :128], rest], axis=0).astype(BF16)


def unpack(value):
    wide = value.astype(F32)
    rest = wide[CHUNK:]
    right = jnp.concatenate([rest[:, :64], rest[8:, 64:]], axis=0)
    return jnp.concatenate([wide[:CHUNK], right], axis=1)


def place_of(lon, lat):
    x = lax.rem(lat, 2) * 2 + lax.div(lon, 8)
    return (x, lax.rem(lax.div(lon, 2), RING), lax.div(lat, 2)), lax.rem(lon, 2)


def device_at(chip, core):
    x, y, z = chip
    return ((lax.rem(x, 2) * RING + y) * 2 + core, z * 2 + lax.div(x, 2))


def moved(chip, axis, step):
    return tuple(lax.rem(c + step, RING) if i == axis else c for i, c in enumerate(chip))


def remote(src, dst, send, recv, device):
    return pltpu.make_async_remote_copy(
        src_ref=src, dst_ref=dst, send_sem=send, recv_sem=recv, device_id=device, device_id_type=MESH
    )


class Here:
    def __init__(self, n_lon, n_lat):
        self.lon, self.lat = lax.axis_index("lon"), lax.axis_index("lat")
        self.chip, self.core = place_of(self.lon, self.lat)
        self.sibling = (self.lon + 1 - 2 * self.core, self.lat)
        self.slot = [[lax.rem(c + k, RING) for k in range(RING)] for c in self.chip]
        chips = [[moved(self.chip, axis, k) for k in range(RING)] for axis in range(3)]
        self.along = [[device_at(chip, self.core) for chip in ring] for ring in chips]
        other = 1 - self.core
        self.eight = []
        for axis in range(3):
            found = []
            for k in FAR_FIRST + (0,):
                if k:
                    found.append((self.along[axis][k], self.slot[axis][k], self.core))
                found.append((device_at(chips[axis][k], other), self.slot[axis][k], other))
            self.eight.append(found)
        self.facing = (lax.rem(self.lon + 8, 16), self.lat)
        self.across = {}
        for step in (-1, 1):
            to_lon = lax.rem(self.lon + n_lon + step, n_lon)
            to_lat = lax.rem(self.lat + n_lat + step, n_lat)
            self.across[step] = ((to_lon, to_lat), (to_lon, self.lat), (self.lon, to_lat))

    def greet(self):
        others = [*self.across[-1], *self.across[1], self.sibling]
        for axis in range(3):
            others += [device for device, _, _ in self.eight[axis][:-1]]
        barrier = pltpu.get_barrier_semaphore()
        for device in others:
            pl.semaphore_signal(barrier, inc=1, device_id=device, device_id_type=MESH)
        return lambda: pl.semaphore_wait(barrier, len(others))


def halo(here, source, target, send, recv, step):
    copies = []
    for index in (0, 2, 1):
        src = index if step < 0 else 3 - index
        device = here.across[step][index]
        copies.append(remote(source.at[src], target.at[3 - src], send.at[index], recv.at[index], device))
    return copies


def begin(copies):
    for copy in copies:
        copy.start()


def end(copies):
    for copy in copies:
        copy.wait()


def wait_bytes(like, sem):
    pltpu.make_async_copy(like, like, sem).wait()


def room(*dims):
    return pltpu.VMEM((*dims, *TILE), BF16)


def tiles_in(block):
    narrow = block.astype(BF16)
    for c in range(block.shape[1] // 128):
        for r in range(block.shape[0] // 16):
            yield narrow[r * 16 : (r + 1) * 16, c * 128 : (c + 1) * 128]


def added(terms):
    total = terms[0].astype(F32)
    for term in terms[1:]:
        total = total + term.astype(F32)
    return total.astype(BF16)


class WeightSum:
    def __init__(self, here, out, refs):
        self.here, self.out = here, out
        self.src, self.r1, self.x2, self.x3, self.send, self.recv = refs

    @staticmethod
    def scratch(tiles):
        n1 = tiles // 24
        dma = pltpu.SemaphoreType.DMA
        return [room(3, RING, 2, n1), room(7, 3, n1), room(3, RING, n1), room(3, RING, n1), dma((4,)), dma((4,))]

    def put(self, block, first):
        n1 = self.src.shape[3]
        for at, tile in enumerate(tiles_in(block), first):
            self.src[at // (8 * n1), at // (2 * n1) % RING, at // n1 % 2, at % n1] = tile

    def phase(self, at, thirds=(0, 1, 2)):
        here, made = self.here, []
        sems = self.send.at[at], self.recv.at[at]
        if at in (0, 3):
            for k in range(7):
                for t in thirds:
                    device, slot, core = here.eight[t][k]
                    mine = self.out.at[t, here.slot[t][0], here.core]
                    if at == 0:
                        made.append(remote(self.src.at[t, slot, core], self.r1.at[k, t], *sems, device))
                    else:
                        made.append(remote(mine, mine, *sems, device))
        else:
            for k in FAR_FIRST:
                for t in range(3):
                    axis = (t + at) % 3
                    mine = (self.x2 if at == 1 else self.x3).at[t, here.slot[axis][0]]
                    made.append(remote(mine, mine, *sems, here.along[axis][k]))
        return made

    def start(self, *thirds):
        begin(self.phase(0, thirds))

    def step(self, at):
        like = self.r1 if at in (0, 3) else self.r1.at[pl.ds(0, 3)]
        wait_bytes(like, self.recv.at[at])
        wait_bytes(like, self.send.at[at])
        core = self.here.core
        for t in range(3):
            one, two, three = (self.here.slot[(t + i) % 3][0] for i in range(3))
            if at == 0:
                self.x2[t, two] = added([self.src[t, one, core]] + [self.r1[k, t] for k in range(7)])
            if at == 1:
                self.x3[t, three] = added([self.x2[t, k] for k in range(RING)])
            if at == 2:
                self.out[t, one, core] = added([self.x3[t, k] for k in range(RING)])
        if at < 3:
            begin(self.phase(at + 1))


class PairSum:
    def __init__(self, here, out, refs):
        self.here, self.out = here, out
        self.src, self.other, self.a1, self.r1, self.x2, self.x3, self.send, self.recv = refs

    @staticmethod
    def scratch(tiles):
        n1 = tiles // 24
        dma = pltpu.SemaphoreType.DMA
        return [
            room(2, tiles // 2), room(tiles // 2),
            room(3, RING, n1), room(3, RING - 1, n1), room(3, RING, n1), room(3, RING, n1),
            dma((6,)), dma((6,)),
        ]

    def put(self, block, first):
        each = self.src.shape[1]
        for at, tile in enumerate(tiles_in(block), first):
            self.src[at // each, at % each] = tile

    def get(self):
        n1 = self.a1.shape[2]
        return [self.out[i // (12 * n1), i // (4 * n1) % 3, i // n1 % 4, i % n1] for i in range(24 * n1)]

    def copies(self, at, axis_of, source, target):
        made = []
        for k in FAR_FIRST:
            for t in range(3):
                axis = (t + axis_of) % 3
                slot = self.here.slot[axis]
                made.append(
                    remote(
                        source(t, slot[k], slot[0]), target(t, k - 1, slot[0]),
                        self.send.at[at], self.recv.at[at], self.here.along[axis][k],
                    )
                )
        return made

    def phase(self, at):
        core = self.here.core
        if at == 0:
            return [remote(self.src.at[1 - core], self.other, self.send.at[0], self.recv.at[0], self.here.sibling)]
        if at == 1:
            return self.copies(1, 0, lambda t, to, me: self.a1.at[t, to], lambda t, k, me: self.r1.at[t, k])
        if at == 2:
            return self.copies(2, 1, lambda t, to, me: self.x2.at[t, me], lambda t, k, me: self.x2.at[t, me])
        if at == 3:
            return self.copies(3, 2, lambda t, to, me: self.x3.at[t, me], lambda t, k, me: self.x3.at[t, me])
        if at == 4:
            out = self.out.at[core]
            return self.copies(4, 0, lambda t, to, me: out.at[t, me], lambda t, k, me: out.at[t, me])
        return [remote(self.out.at[core], self.out.at[core], self.send.at[5], self.recv.at[5], self.here.sibling)]

    def start(self):
        begin(self.phase(0))

    def step(self, at):
        like = self.other if at in (0, 5) else self.r1
        wait_bytes(like, self.recv.at[at])
        wait_bytes(like, self.send.at[at])
        core = self.here.core
        if at == 0:
            total = self.src[core].astype(F32) + self.other[...].astype(F32)
            self.a1[...] = total.astype(BF16).reshape(self.a1.shape)
        for t in range(3):
            one, two, three = (self.here.slot[(t + i) % 3][0] for i in range(3))
            if at == 1:
                total = self.a1[t, one].astype(F32)
                for k in range(RING - 1):
                    total = total + self.r1[t, k].astype(F32)
                self.x2[t, two] = total.astype(BF16)
            if at in (2, 3):
                came = self.x2 if at == 2 else self.x3
                total = came[t, 0].astype(F32)
                for k in range(1, RING):
                    total = total + came[t, k].astype(F32)
                if at == 2:
                    self.x3[t, three] = total.astype(BF16)
                else:
                    self.out[core, t, one] = total.astype(BF16)
        if at < 5:
            begin(self.phase(at + 1))


class BiasSum:
    def __init__(self, here, out, refs):
        self.here, self.out = here, out
        self.src, self.r1, self.x2, self.send, self.recv = refs

    @staticmethod
    def scratch():
        each = B_TILES // 8
        dma = pltpu.SemaphoreType.DMA
        return [room(RING, 2, each), room(7, each), room(2, each), dma((3,)), dma((3,))]

    def put(self, block):
        each = B_TILES // 8
        last = block[:, 256:]
        shared = last[0:B_ROWS]
        for g in range(1, 288 // B_ROWS):
            shared = shared + pltpu.roll(last[g * B_ROWS : (g + 1) * B_ROWS], g * B_LEFT, 1)
        tiles = [*tiles_in(block[:, :256]), *tiles_in(shared), jnp.zeros(TILE, BF16)]
        for at, tile in enumerate(tiles):
            self.src[at // (2 * each), at // each % 2, at % each] = tile

    def get(self):
        each = B_TILES // 8
        tiles = [self.out[at // (2 * each), at // each % 2, at % each] for at in range(B_TILES)]
        first = joined(tiles[:36], 2)
        shared = joined(tiles[36:39], 1)
        last = [shared]
        for g in range(1, 288 // B_ROWS):
            last.append(pltpu.roll(shared, 128 - g * B_LEFT, 1))
        return jnp.concatenate([first, jnp.concatenate(last, axis=0)], axis=1)

    def phase(self, at):
        here, made = self.here, []
        sems = self.send.at[at], self.recv.at[at]
        if at == 1:
            return [remote(self.x2.at[0], self.x2.at[1], *sems, here.facing)]
        mine = self.out.at[here.slot[1][0], here.core]
        for k, (device, slot, core) in enumerate(here.eight[1]):
            if at == 0:
                made.append(remote(self.src.at[slot, core], self.r1.at[k], *sems, device))
            else:
                made.append(remote(mine, mine, *sems, device))
        return made

    def start(self):
        begin(self.phase(0))

    def step(self, at):
        like = self.x2.at[1] if at == 1 else self.r1
        wait_bytes(like, self.recv.at[at])
        wait_bytes(like, self.send.at[at])
        slot, core = self.here.slot[1][0], self.here.core
        if at == 0:
            self.x2[0] = added([self.src[slot, core]] + [self.r1[k] for k in range(7)])
        if at == 1:
            self.out[slot, core] = added([self.x2[0], self.x2[1]])
        if at < 2:
            begin(self.phase(at + 1))


def layer_norm(x):
    centered = x - jnp.mean(x, axis=-1, keepdims=True)
    spread = jnp.mean(centered * centered, axis=-1, keepdims=True)
    rate = lax.rsqrt(spread + EPSILON)
    return centered * rate, rate


def layer_norm_back(cot, unit, rate):
    first = jnp.mean(cot, axis=-1, keepdims=True)
    second = jnp.mean(cot * unit, axis=-1, keepdims=True)
    return rate * (cot - first - unit * second)


def head_mask(head):
    lane = lax.broadcasted_iota(jnp.int32, (1, C), 1)
    return (lane >= head * 32) & (lane < head * 32 + 32)


def stacked(value):
    wide = value.astype(F32)
    parts = [jnp.where(head_mask(h), wide, 0.0).astype(BF16) for h in range(HEADS)]
    return jnp.concatenate(parts, axis=0)


def unstacked(value):
    total = jnp.where(head_mask(0), value[0:WIN], 0.0)
    for h in range(1, HEADS):
        total = total + jnp.where(head_mask(h), value[h * WIN : (h + 1) * WIN], 0.0)
    return total


def expand_bias(last_lat, table, columns, index_rows, lanes, tall_table, gathered, strips, scores):
    for head in range(HEADS):
        tall_table[head * LWIN : (head + 1) * LWIN, :] = table[head]
    for site in range(SITE):
        lev, a = site // WLAT, site % WLAT
        for other in range(WLEV):
            start = ((lev * WLEV + other) * WLAT + a) * RUN
            gathered[site * WH : (site + 1) * WH, other * RUN : (other + 1) * RUN] = tall_table[
                :, start : start + RUN
            ]
    strip = sum(dot(part, lanes[...]) for part in pieces(gathered[...], 3)) * LOG2E
    code = columns[0 : SITE * WH, 2:3]
    seen = jnp.where((code & 4) != 0, 1, 0) + jnp.where(last_lat, 2, 0)
    apart = (code ^ index_rows[2:3, 0:LANES]) & seen
    strip = jnp.where(apart != 0, MASKED, strip)
    for c in range(LANES // 128):
        strips[c] = strip[:, c * 128 : (c + 1) * 128]

    def one(wh, carry):
        odd = jnp.concatenate([strips[c, pl.ds(wh, SITE, WH), :] for c in range(LANES // 128)], axis=1)
        both = jnp.concatenate([pltpu.roll(odd, LANES - SITE, 1), odd], axis=0)
        start = lax.rem(wh, LWIN) * STACK + lax.div(wh, LWIN) * WIN
        for pair in range(WLON // 2):
            offset = (WLON - 2 - 2 * pair) * SITE
            scores[pl.ds(pl.multiple_of(start + pair * 24, 8), 24), :] = both[:, offset : offset + WIN]
        return carry

    lax.fori_loop(0, WH, one, 0)


def collapse_bias(scores, strips):
    def one(wh, carry):
        start = lax.rem(wh, LWIN) * STACK + lax.div(wh, LWIN) * WIN
        total = jnp.zeros((2 * SITE, LANES), F32)
        for pair in range(WLON // 2):
            offset = (WLON - 2 - 2 * pair) * SITE
            part = scores[pl.ds(pl.multiple_of(start + pair * 24, 8), 24), :]
            part = jnp.concatenate([part, jnp.zeros((2 * SITE, LANES - WIN), F32)], axis=1)
            total = total + (pltpu.roll(part, offset, 1) if offset else part)
        total = pltpu.roll(total[:SITE], SITE, 1) + total[SITE:]
        for c in range(LANES // 128):
            strips[c, pl.ds(wh, SITE, WH), :] = total[:, c * 128 : (c + 1) * 128]
        return carry

    lax.fori_loop(0, WH, one, 0)


def block_kernel(n_lon, n_lat, *refs):
    loaded = refs[:9]
    out_field, grad_field, qkv, proj, fc1, fc2, bias = refs[9:16]
    field, cot, w_qkv, w_proj, w_fc1, w_fc2, table, columns, index_rows, load_sem = refs[16:26]
    (
        out, e_out, l_out, b_out, sent, came, cot_sent, cot_came, back, halo_send, halo_recv,
        xw, uw, scores, normed, query, key, value, unit, rate, blended, normed_two, hidden,
        cot_first, cot_mid, cot_q, cot_k, cot_v, ow, gw, tall_table, gathered, strips, w3,
        places_in, places_out, lanes, slope, unit_two, rate_two,
    ) = refs[26:66]
    here = Here(n_lon, n_lat)
    early = PairSum(here, e_out, refs[66:74])
    late = WeightSum(here, l_out, refs[74:80])
    strip_sum = BiasSum(here, b_out, refs[80:85])

    loads = [
        pltpu.make_async_copy(src, dst, load_sem.at[i]) for i, (src, dst) in enumerate(zip(loaded, refs[16:25]))
    ]
    loads[0].start()
    greeted = here.greet()
    begin(loads[6:9])
    loads[0].wait()
    for index in range(3):
        for part, chunk in enumerate(split(field, index)):
            sent[part, index] = pack(chunk)
    greeted()
    inward = [
        halo(here, sent.at[i], came.at[i], halo_send.at[i], halo_recv.at[i], -1) for i in range(2)
    ]
    cot_inward = halo(here, cot_sent, cot_came, halo_send.at[2], halo_recv.at[2], -1)
    outward = [
        halo(here, back.at[i], out.at[i], halo_send.at[3 + i], halo_recv.at[3 + i], 1) for i in range(2)
    ]
    begin(inward[0])
    begin(inward[1])
    begin(loads[1:6])
    end(loads[6:9])
    lanes[...] = one_hot(columns[0:STRIP, 3:4], STRIP, LANES)
    last_lat = here.lat == n_lat - 1
    expand_bias(last_lat, table, columns, index_rows, lanes, tall_table, gathered, strips, scores)
    places_in[...] = one_hot(columns[0:PAIR, 0:1], PAIR, PAIR)
    places_out[...] = one_hot(index_rows[0:1, 0:PAIR], PAIR, PAIR)
    loads[1].wait()
    for index in range(3):
        for part, chunk in enumerate(split(cot, index)):
            cot_sent[index, part] = pack(chunk)
    own = [split(ref, 3) for ref in (field, cot)]
    loads[2].wait()
    for third in range(3):
        w3[third] = w_qkv[:, third * C : (third + 1) * C]

    def gather(kind, part):
        if kind:
            arrived = [cot_came[i, part] for i in range(1, 4)]
        else:
            arrived = [came[part, i] for i in range(1, 4)]
        parts = [own[kind][part]] + [unpack(value) for value in arrived]
        return dot(places_in[...], jnp.concatenate(parts, axis=0).astype(BF16)).astype(BF16)

    def scatter(kind, ref):
        for part in range(2):
            whole = dot(places_out[...], ref[part * PAIR : (part + 1) * PAIR, :])
            out[kind, 3, part] = pack(whole[:CHUNK])
            for i in range(1, 4):
                back[kind, i, part] = pack(whole[i * CHUNK : (i + 1) * CHUNK])
        begin(outward[kind])

    def places(w):
        return pl.ds(w * WIN, WIN), pl.ds(w * STACK, STACK)

    def attend(w):
        rows, tall = places(w)
        unit_x, rate_x = layer_norm(xw[rows, :].astype(F32))
        unit[rows, :] = unit_x
        rate[rows, :] = rate_x
        norm = unit_x.astype(BF16)
        normed[rows, :] = norm
        q = dot(norm, w3[0]).astype(BF16)
        k = dot(norm, w3[1]).astype(BF16)
        v = dot(norm, w3[2]).astype(BF16)
        query[rows, :] = q
        key[rows, :] = k
        value[rows, :] = v
        s = dot_nt(stacked(q), k) * (SCALE * LOG2E) + scores[tall, :]
        e = jnp.exp2(s - jnp.max(s, axis=-1, keepdims=True))
        p = e * (1.0 / jnp.sum(e, axis=-1, keepdims=True))
        scores[tall, :] = p
        blended[rows, :] = unstacked(dot(p.astype(BF16), v)).astype(BF16)

    def feed(w):
        rows = pl.ds(w * 2 * WIN, 2 * WIN)
        middle = xw[rows, :].astype(F32) + dot(blended[rows, :], w_proj[...])
        middle = middle.astype(BF16).astype(F32)
        unit_m, rate_m = layer_norm(middle)
        norm_m = unit_m.astype(BF16)
        normed_two[rows, :] = norm_m
        first = dot(norm_m, w_fc1[...])
        phi = 0.5 + 0.5 * lax.erf(first * math.sqrt(0.5))
        hid = (first * phi).astype(BF16)
        hidden[rows, :] = hid
        bell = jnp.exp2(first * first * (-0.5 * LOG2E)) * (1.0 / math.sqrt(2.0 * math.pi))
        slope[rows, :] = phi + first * bell
        unit_two[rows, :] = unit_m
        rate_two[rows, :] = rate_m
        ow[rows, :] = (middle + dot_nt(hid, w_fc2[...])).astype(BF16)

    def feed_back(w):
        rows = pl.ds(w * 2 * WIN, 2 * WIN)
        up = uw[rows, :]
        c_first = (dot(up, w_fc2[...]).astype(BF16).astype(F32) * slope[rows, :]).astype(BF16)
        cot_first[rows, :] = c_first
        c_norm = dot_nt(c_first, w_fc1[...]).astype(BF16).astype(F32)
        c_mid = layer_norm_back(c_norm, unit_two[rows, :], rate_two[rows, :]).astype(BF16).astype(F32)
        cot_mid[rows, :] = (up.astype(F32) + c_mid).astype(BF16)

    def backward(w):
        rows, tall = places(w)
        up = cot_mid[rows, :]
        c_blend = stacked(dot_nt(up, w_proj[...]).astype(BF16))
        p = scores[tall, :]
        c_p = dot_nt(c_blend, value[rows, :])
        c_s = p * (c_p - jnp.sum(p * c_p, axis=-1, keepdims=True))
        scores[tall, :] = c_s
        c_v = dot_tn(p.astype(BF16), c_blend).astype(BF16)
        narrow = c_s.astype(BF16)
        c_q = (unstacked(dot(narrow, key[rows, :])) * SCALE).astype(BF16)
        c_k = (dot_tn(narrow, stacked(query[rows, :])) * SCALE).astype(BF16)
        cot_q[rows, :] = c_q
        cot_k[rows, :] = c_k
        cot_v[rows, :] = c_v

    def inputs_back(w):
        rows = pl.ds(w * 2 * WIN, 2 * WIN)
        c_norm = dot_nt(cot_q[rows, :], w3[0]) + dot_nt(cot_k[rows, :], w3[1])
        c_norm = (c_norm + dot_nt(cot_v[rows, :], w3[2])).astype(BF16).astype(F32)
        c_x = layer_norm_back(c_norm, unit[rows, :], rate[rows, :]).astype(BF16)
        gw[rows, :] = (cot_mid[rows, :].astype(F32) + c_x.astype(F32)).astype(BF16)

    for part in range(2):
        end(inward[part])
        xw[part * PAIR : (part + 1) * PAIR, :] = gather(0, part)
        if not part:
            begin(cot_inward)
        attend(2 * part)
        attend(2 * part + 1)
    end(loads[3:6])
    feed(0)
    feed(1)
    end(cot_inward)
    for part in range(2):
        uw[part * PAIR : (part + 1) * PAIR, :] = gather(1, part)
        feed_back(part)
    early.put(dot_tn(normed_two[...], cot_first[...]), 0)
    early.put(dot_tn(uw[...], hidden[...]), 72)
    early.start()
    backward(0)
    backward(1)
    early.step(0)
    backward(2)
    backward(3)
    norm = normed[...]
    late.put(jnp.concatenate([dot_tn(norm, cot_q[...]), dot_tn(norm, cot_k[...])], axis=1), 0)
    late.start(0)
    c_proj = dot_tn(blended[...], cot_mid[...])
    late.put(jnp.concatenate([dot_tn(norm, cot_v[...]), c_proj], axis=1), 36)
    late.start(1, 2)
    early.step(1)
    collapse_bias(scores, strips)
    strip_sum.put(jnp.concatenate([strips[c] for c in range(LANES // 128)], axis=1))
    strip_sum.start()
    late.step(0)
    inputs_back(0)
    inputs_back(1)
    early.step(2)
    scatter(1, gw)
    late.step(1)
    strip_sum.step(0)
    scatter(0, ow)
    early.step(3)
    late.step(2)
    strip_sum.step(1)
    end(outward[1])
    for index in range(4):
        merge(grad_field, index, [unpack(out[1, index, part]) for part in range(2)])
    early.step(4)
    strip_sum.step(2)
    finish_bias(strip_sum.get(), lanes, tall_table, bias)
    end(outward[0])
    for index in range(4):
        merge(out_field, index, [unpack(out[0, index, part]) for part in range(2)])
    late.step(3)
    qkv[:, 0:384] = joined(tiles_of(l_out)[:36], 3)
    right = joined(tiles_of(l_out)[36:], 3)
    qkv[:, 384:576] = right[:, 0:C]
    proj[...] = right[:, C:]
    early.step(5)
    fc1[...] = joined(early.get()[:72], 6)
    fc2[...] = joined(early.get()[72:], 6)


def joined(tiles, columns):
    rows = len(tiles) // columns
    cols = [jnp.concatenate(tiles[c * rows : (c + 1) * rows], axis=0) for c in range(columns)]
    return jnp.concatenate(cols, axis=1).astype(F32)


def tiles_of(ref):
    n1 = ref.shape[3]
    return [ref[i // (8 * n1), i // (2 * n1) % RING, i // n1 % 2, i % n1] for i in range(24 * n1)]


def finish_bias(strip, lanes, tall_table, bias):
    runs = dot_nt(strip.astype(BF16), lanes[...])
    for site in range(SITE):
        lev, a = site // WLAT, site % WLAT
        for other in range(WLEV):
            start = ((lev * WLEV + other) * WLAT + a) * RUN
            tall_table[:, start : start + RUN] = runs[
                site * WH : (site + 1) * WH, other * RUN : (other + 1) * RUN
            ]
    for head in range(HEADS):
        bias[head] = tall_table[head * LWIN : (head + 1) * LWIN, :]


def finish_kernel(*refs):
    count = len(refs) // 2
    copies = [pltpu.make_async_copy(refs[i], refs[count + i], refs[-1].at[i]) for i in range(count)]
    copies.sort(key=lambda copy: -math.prod(copy.src_ref.shape))
    begin(copies)
    end(copies)


def per_device(n_lon, n_lat, field, w_qkv, w_proj, w_fc1, w_fc2, bias_table, cotangent):
    vmem, hbm = pl.BlockSpec(memory_space=pltpu.VMEM), pl.BlockSpec(memory_space=pltpu.HBM)
    shape = jax.ShapeDtypeStruct
    dma = pltpu.SemaphoreType.DMA
    columns = columns_of(token_places(), [], row_codes(), lane_places())
    index_rows = columns_of(token_places(), [], lane_codes()).T.copy()
    inputs = (
        field, cotangent, w_qkv, w_proj, w_fc1, w_fc2.T, bias_table[0].transpose(1, 0, 2), columns, index_rows
    )
    inputs = [pltpu.with_memory_space_constraint(jnp.asarray(a), pltpu.HBM) for a in inputs]
    tile = shape((WLON, WLAT, LEV, C), BF16)
    outputs = (
        tile,
        tile,
        shape((C, 3 * C), F32),
        shape((C, C), F32),
        shape((C, HIDDEN), F32),
        shape((C, HIDDEN), F32),
        shape((HEADS, LWIN, POS), F32),
    )
    wide = lambda dtype, n=1: [pltpu.VMEM((TOK, C), dtype)] * n
    results = pl.pallas_call(
        functools.partial(block_kernel, n_lon, n_lat),
        out_shape=outputs,
        in_specs=[hbm] * len(inputs),
        out_specs=[vmem] * len(outputs),
        scratch_shapes=[
            *[pltpu.VMEM(a.shape, a.dtype) for a in inputs],
            dma((len(inputs),)),
            pltpu.VMEM((2, 4, 2, PACKED, 128), BF16),
            room(2, 3, RING, E_TILES // 24),
            room(3, RING, 2, L_TILES // 24),
            room(RING, 2, B_TILES // 8),
            pltpu.VMEM((2, 3, PACKED, 128), BF16),
            pltpu.VMEM((2, 4, PACKED, 128), BF16),
            pltpu.VMEM((3, 2, PACKED, 128), BF16),
            pltpu.VMEM((4, 2, PACKED, 128), BF16),
            pltpu.VMEM((2, 4, 2, PACKED, 128), BF16),
            dma((5, 3)),
            dma((5, 3)),
            *wide(BF16, 2),
            pltpu.VMEM((LWIN * STACK, WIN), F32),
            *wide(BF16, 4),
            *wide(F32),
            pltpu.VMEM((TOK, 1), F32),
            *wide(BF16, 2),
            pltpu.VMEM((TOK, HIDDEN), BF16),
            pltpu.VMEM((TOK, HIDDEN), BF16),
            *wide(BF16, 6),
            pltpu.VMEM((WH, POS), F32),
            pltpu.VMEM((SITE * WH, STRIP), F32),
            pltpu.VMEM((LANES // 128, SITE * WH, 128), F32),
            pltpu.VMEM((3, C, C), BF16),
            pltpu.VMEM((PAIR, PAIR), BF16),
            pltpu.VMEM((PAIR, PAIR), BF16),
            pltpu.VMEM((STRIP, LANES), BF16),
            pltpu.VMEM((TOK, HIDDEN), F32),
            *wide(F32),
            pltpu.VMEM((TOK, 1), F32),
            *PairSum.scratch(E_TILES),
            *WeightSum.scratch(L_TILES),
            *BiasSum.scratch(),
        ],
        compiler_params=pltpu.CompilerParams(
            vmem_limit_bytes=VMEM_LIMIT, collective_id=0, has_side_effects=True
        ),
        name="block",
    )(*inputs)
    *results, fc2, bias = pl.pallas_call(
        finish_kernel,
        out_shape=outputs,
        in_specs=[vmem] * len(outputs),
        out_specs=[hbm] * len(outputs),
        scratch_shapes=[dma((len(outputs),))],
        compiler_params=pltpu.CompilerParams(vmem_limit_bytes=VMEM_LIMIT),
        name="finish",
    )(*results)
    return (*results, fc2.T, bias.transpose(1, 0, 2)[None])


def solution(mesh):
    whole, tiles, banded = P(), P("lon", "lat", None, None), P("lat", None, None, None)
    return jax.shard_map(
        functools.partial(per_device, mesh.shape["lon"], mesh.shape["lat"]),
        mesh=mesh,
        in_specs=(tiles, whole, whole, whole, whole, banded, tiles),
        out_specs=(tiles, tiles, whole, whole, whole, whole, banded),
        check_vma=False,
    )
```
